32 devices in a mesh: rep: 2 (over x), dat: 4 (over y, core), ctx: 4 (over z).
Axes of the slice: x: 2, y: 2, z: 4, core: 2. Of those that a mesh axis runs over, the one named last changes fastest.
Arguments:
- tokens: bfloat16 [8, 2048, 1600], P(('rep', 'dat'), 'ctx'), may hold values from -6 to 6
- segments: int32 [8, 2048], P(('rep', 'dat')), may hold values from 0 to 3, as said below
- cotangent: bfloat16 [8, 2048, 1600], P(('rep', 'dat'), 'ctx'), may hold values from -6 to 6
- ln1_gain: float32 [1600], P('ctx'), may hold values from 0.5 to 1.5
- ln1_bias: float32 [1600], P('ctx'), may hold values from -1.25 to 1.25
- w_qkv: float32 [1600, 4800], P('dat', 'ctx'), may hold values from -0.21875 to 0.21875
- b_qv: float32 [3200], P('ctx'), may hold values from -1.25 to 1.25
- w_out: float32 [1600, 1600], P('dat', 'ctx'), may hold values from -0.625 to 0.625
- b_out: float32 [1600], P('ctx'), may hold values from -1.25 to 1.25
- ln2_gain: float32 [1600], P('ctx'), may hold values from 0.5 to 1.5
- ln2_bias: float32 [1600], P('ctx'), may hold values from -1.25 to 1.25
- w_fc: float32 [1600, 6400], P('dat', 'ctx'), may hold values from -0.15625 to 0.15625
- b_fc: float32 [6400], P('ctx'), may hold values from -1.25 to 1.25
- w_proj: float32 [6400, 1600], P('dat', 'ctx'), may hold values from -0.078125 to 0.078125
- b_proj: float32 [1600], P('ctx'), may hold values from -1.25 to 1.25
Outputs:
- layer_out: bfloat16 [8, 2048, 1600], P(('rep', 'dat'), 'ctx')
- input_grad: bfloat16 [8, 2048, 1600], P(('rep', 'dat'), 'ctx')
- grad_ln1_gain: float32 [1600], P('ctx')
- grad_ln1_bias: float32 [1600], P('ctx')
- grad_w_qkv: float32 [1600, 4800], P('dat', 'ctx')
- grad_b_qv: float32 [3200], P('ctx')
- grad_w_out: float32 [1600, 1600], P('dat', 'ctx')
- grad_b_out: float32 [1600], P('ctx')
- grad_ln2_gain: float32 [1600], P('ctx')
- grad_ln2_bias: float32 [1600], P('ctx')
- grad_w_fc: float32 [1600, 6400], P('dat', 'ctx')
- grad_b_fc: float32 [6400], P('ctx')
- grad_w_proj: float32 [6400, 1600], P('dat', 'ctx')
- grad_b_proj: float32 [1600], P('ctx')
The draws below stay inside these ranges and needn't reach their ends.
Inputs may be any that keep to these rules, and one draw needn't show every extreme that they name: `segments`: along each sequence the document numbers start at 0 and never fall; one sequence, drawn from the seed, is a single document.
All inputs are finite; a program needn't handle non-finite values.
Results may differ from the reference program's by a relative error of at most 0.014.
The reference program's roundings to bfloat16 on the way count: a program that leaves them out, or rounds other values in their place, can miss the bound.
Values may be sent and summed in bfloat16 or wider, within the bound.
No kernel may reach another device: no remote copies, remote signals or barrier semaphores. Data moves between devices by JAX's collectives and lax.ppermute only.
A program may use at most 384 MiB of HBM per device.

```python
import jax
import jax.numpy as jnp
from jax import lax

D = 1600
HEADS = 25
HEAD_DIM = 64
FF = 6400
WINDOW = 1024
SEQLEN = 2048
SEQS = 8


def draw_segments(key, part):
    key = jax.random.fold_in(key, 7)
    cut_key, pick_key = jax.random.split(key)
    cuts = jax.random.randint(cut_key, (SEQS, 3), 1, SEQLEN)
    chosen = jax.random.randint(pick_key, (), 0, SEQS)
    whole = (jnp.arange(SEQS, dtype=jnp.int32) == chosen)[:, None]
    cuts = jnp.where(whole, SEQLEN, cuts)
    positions = jnp.arange(SEQLEN, dtype=jnp.int32)
    passed = (positions[None, :, None] >= cuts[:, None, :]).astype(jnp.int32)
    return jnp.sum(passed, axis=-1).astype(jnp.int32)


def level_of(stream_key, shape, shards, low, top_value):
    def one(axis_at, blocks):
        steps = jax.random.uniform(jax.random.fold_in(jax.random.fold_in(stream_key, 6), axis_at), (blocks,), jnp.float32, low / len(shards), top_value / len(shards))
        return jnp.repeat(jnp.exp(steps), shape[axis_at] // blocks).reshape((-1,) + (1,) * (len(shape) - axis_at - 1))

    factor_of = one(*shards[0])
    for cut in shards[1:]:
        factor_of = factor_of * one(*cut)
    return factor_of


def normal_values(own_key, dims, spread, reach, cuts=(), kind=jnp.bfloat16):
    level = level_of(own_key, dims, cuts, -0.22, 0.18) if cuts else 1.0
    values = jax.random.normal(own_key, dims, jnp.float32) * spread * level
    return jnp.minimum(jnp.maximum(values, -reach), reach).astype(kind)


def setup_inputs(seed: int = 0) -> dict:
    key_list = jax.random.split(jax.random.key(seed), 16)
    tokens = normal_values(key_list[0], (SEQS, SEQLEN, D), 1.0, 6.0, ((0, 8), (1, 4)))
    segments = draw_segments(jax.random.fold_in(key_list[15], 71), 0)
    cotangent = normal_values(key_list[2], (SEQS, SEQLEN, D), 1.0, 6.0, ((0, 8), (1, 4)))
    ln1_gain = jnp.clip(1.0 + 0.1 * jax.random.normal(key_list[3], (D,), jnp.float32), 0.5, 1.5)
    ln1_bias = normal_values(key_list[4], (D,), 0.2, 1.25, ((0, 4),), jnp.float32)
    w_qkv = normal_values(key_list[5], (D, 3 * D), (D // 2) ** -0.5, 0.21875, ((0, 4), (1, 4)), jnp.float32)
    b_qv = normal_values(key_list[6], (2 * D,), 0.2, 1.25, ((0, 4),), jnp.float32)
    w_out = normal_values(key_list[7], (D, D), (D // 16) ** -0.5, 0.625, ((0, 4), (1, 4)), jnp.float32)
    b_out = normal_values(key_list[8], (D,), 0.2, 1.25, ((0, 4),), jnp.float32)
    ln2_gain = jnp.clip(1.0 + 0.1 * jax.random.normal(key_list[9], (D,), jnp.float32), 0.5, 1.5)
    ln2_bias = normal_values(key_list[10], (D,), 0.2, 1.25, ((0, 4),), jnp.float32)
    w_fc = normal_values(key_list[11], (D, FF), D ** -0.5, 0.15625, ((0, 4), (1, 4)), jnp.float32)
    b_fc = normal_values(key_list[12], (FF,), 0.2, 1.25, ((0, 4),), jnp.float32)
    w_proj = normal_values(key_list[13], (FF, D), FF ** -0.5, 0.078125, ((0, 4), (1, 4)), jnp.float32)
    b_proj = normal_values(key_list[14], (D,), 0.2, 1.25, ((0, 4),), jnp.float32)
    return {"tokens": tokens, "segments": segments, "cotangent": cotangent, "ln1_gain": ln1_gain, "ln1_bias": ln1_bias, "w_qkv": w_qkv, "b_qv": b_qv, "w_out": w_out, "b_out": b_out, "ln2_gain": ln2_gain, "ln2_bias": ln2_bias, "w_fc": w_fc, "b_fc": b_fc, "w_proj": w_proj, "b_proj": b_proj}


EPS = 1e-05
MASKED = -1e+30
HIGH = lax.Precision.HIGHEST

@jax.custom_vjp
def low(v):
    return lax.optimization_barrier(v.astype(jnp.bfloat16)).astype(jnp.float32)

@jax.custom_vjp
def low_back(v):
    return v

def low_keep(v):
    return (low(v), None)

def low_pass(kept, grad):
    return (grad,)

def back_keep(v):
    return (v, None)

def back_low(kept, grad):
    return (low(grad),)
low.defvjp(low_keep, low_pass)
low_back.defvjp(back_keep, back_low)

def matmul_high(left, right):
    return jnp.dot(left, right, precision=HIGH, preferred_element_type=jnp.float32)

def layer_norm(values, gain, shift):
    average = lax.optimization_barrier(jnp.mean(values, axis=-1, keepdims=True))
    centred = values - average
    variance = lax.optimization_barrier(jnp.mean(centred * centred, axis=-1, keepdims=True))
    return centred * lax.rsqrt(variance + EPS) * gain + shift

def attend_block(query, keys_padded, values_padded, segment, segment_padded, index):
    block_rows = min(512, query.shape[0])
    start = (index * block_rows).astype(jnp.int32)
    scale = HEAD_DIM ** (-0.5)
    query_part = lax.dynamic_slice_in_dim(query, start, block_rows, 0)
    key_part = lax.dynamic_slice_in_dim(keys_padded, start, WINDOW + block_rows, 0)
    value_part = lax.dynamic_slice_in_dim(values_padded, start, WINDOW + block_rows, 0)
    query_segment = lax.dynamic_slice_in_dim(segment, start, block_rows, 0)
    key_segment = lax.dynamic_slice_in_dim(segment_padded, start, WINDOW + block_rows, 0)
    query_position = start + jnp.arange(block_rows, dtype=jnp.int32)
    key_position = start - WINDOW + jnp.arange(WINDOW + block_rows, dtype=jnp.int32)
    scores = jnp.einsum('qhe,khe->hqk', query_part, key_part, precision=HIGH) * scale
    scores = low_back(scores)
    visible = (query_segment[:, None] == key_segment[None, :]) & (key_position[None, :] <= query_position[:, None]) & (key_position[None, :] > query_position[:, None] - WINDOW)
    scores = jnp.where(visible[None], scores, MASKED)
    row_top = lax.optimization_barrier(jnp.max(scores, axis=-1, keepdims=True))
    weights = jnp.exp(scores - row_top)
    probs = weights / lax.optimization_barrier(jnp.sum(weights, axis=-1, keepdims=True))
    return jnp.einsum('hqk,khe->qhe', low(probs), value_part, precision=HIGH)

def attend(query, keys, values, segment):
    length = query.shape[0]
    block_rows = min(512, length)
    padding = jnp.zeros((WINDOW, HEADS, HEAD_DIM), jnp.float32)
    keys_padded = jnp.concatenate([padding, keys], axis=0)
    values_padded = jnp.concatenate([padding, values], axis=0)
    segment_padded = jnp.concatenate([jnp.full((WINDOW,), -1, jnp.int32), segment.astype(jnp.int32)])
    checked = jax.checkpoint(attend_block)

    def per_block(index):
        return checked(query, keys_padded, values_padded, segment, segment_padded, index)
    blocks = lax.map(per_block, jnp.arange(length // block_rows, dtype=jnp.int32))
    return blocks.reshape(length, HEADS * HEAD_DIM)

def sequence_forward(inputs, params, segment):
    rounded = [low(param) for param in params]
    gain_one, shift_one, weight_qkv, bias_qv, weight_out, bias_out = rounded[:6]
    gain_two, shift_two, weight_fc, bias_fc, weight_proj, bias_proj = rounded[6:]
    length = inputs.shape[0]
    normed_one = layer_norm(inputs, gain_one, shift_one)
    qkv_bias = jnp.concatenate([bias_qv[:D], jnp.zeros((D,), jnp.float32), bias_qv[D:]])
    mixed = low(low_back(matmul_high(low(normed_one), weight_qkv) + qkv_bias))
    query = mixed[:, :D].reshape(length, HEADS, HEAD_DIM)
    keys = mixed[:, D:2 * D].reshape(length, HEADS, HEAD_DIM)
    values = mixed[:, 2 * D:].reshape(length, HEADS, HEAD_DIM)
    attended = low(low_back(attend(query, keys, values, segment)))
    resid = inputs + low_back(matmul_high(attended, weight_out) + bias_out)
    normed_two = layer_norm(resid, gain_two, shift_two)
    hidden = low_back(matmul_high(low(normed_two), weight_fc) + bias_fc)
    active = low(jax.nn.gelu(hidden, approximate=True))
    return resid + low_back(matmul_high(active, weight_proj) + bias_proj)

def reference(tokens, segments, cotangent, ln1_gain, ln1_bias, w_qkv, b_qv, w_out, b_out, ln2_gain, ln2_bias, w_fc, b_fc, w_proj, b_proj):
    params = (ln1_gain, ln1_bias, w_qkv, b_qv, w_out, b_out, ln2_gain, ln2_bias, w_fc, b_fc, w_proj, b_proj)

    def per_sequence(totals, item):
        seq_tokens, seq_segment, seq_cotangent = item

        def forward(inputs, weights):
            return sequence_forward(inputs, weights, seq_segment)
        outputs, pullback = jax.vjp(forward, seq_tokens.astype(jnp.float32), params)
        grad_inputs, grad_params = pullback(seq_cotangent.astype(jnp.float32))
        totals = jax.tree.map(jnp.add, totals, grad_params)
        return (totals, (outputs.astype(jnp.bfloat16), grad_inputs.astype(jnp.bfloat16)))
    zeros = jax.tree.map(jnp.zeros_like, params)
    totals, (layer_out, input_grad) = lax.scan(per_sequence, zeros, (tokens, segments, cotangent))
    return (layer_out, input_grad, totals[0], totals[1], totals[2], totals[3], totals[4], totals[5], totals[6], totals[7], totals[8], totals[9], totals[10], totals[11])
```

```python
import functools

import jax
import jax.numpy as jnp
from jax import lax
from jax.experimental import pallas as pl
from jax.experimental.pallas import tpu as pltpu
from jax.sharding import PartitionSpec as P

D = 1600
HEADS = 25
HEAD_DIM = 64
WINDOW = 1024


EPS = 1e-05
MASKED = -1e30
LANES = 128
PAIRS = -(-HEADS // 2)
WIDE = PAIRS * LANES
SCALE = HEAD_DIM ** (-0.5)
NT = (((1,), (1,)), ((), ()))
TN = (((0,), (0,)), ((), ()))


def permute(value, axes, pairs):
    return lax.ppermute(value, axes, pairs)


def roll_ctx(value, steps):
    count = lax.axis_size("ctx")
    return permute(value, "ctx", [(s, (s + steps) % count) for s in range(count)])


def shift_ctx(value, steps, first, last):
    return permute(value, "ctx", [(s, s + steps) for s in range(first, last)])


def roll_ctx_by_rep(value, steps):
    count = lax.axis_size("ctx")
    pairs = [
        (rep * count + s, rep * count + (s + steps[rep]) % count)
        for rep in range(len(steps))
        for s in range(count)
    ]
    return permute(value, ("rep", "ctx"), pairs)


def roll_y(value, steps):
    count = lax.axis_size("dat")
    return permute(value, "dat", [(s, (s + 2 * steps) % count) for s in range(count)])


def swap_dat(value, bit):
    count = lax.axis_size("dat")
    return permute(value, "dat", [(s, s ^ bit) for s in range(count)])


def swap_rep(value):
    return permute(value, "rep", [(0, 1), (1, 0)])


def norm_forward(values, gain, shift):
    average = jnp.mean(values, axis=-1, keepdims=True)
    centred = values - average
    variance = jnp.mean(centred * centred, axis=-1, keepdims=True)
    inverse = lax.rsqrt(variance + EPS)
    normal = centred * inverse
    return (normal * gain + shift, normal, inverse)


def norm_backward(grad_out, gain, normal, inverse):
    scaled = grad_out * gain
    first = jnp.mean(scaled, axis=-1, keepdims=True)
    second = jnp.mean(scaled * normal, axis=-1, keepdims=True)
    return inverse * (scaled - first - normal * second)


def dot(left, right):
    return jnp.dot(left, right, preferred_element_type=jnp.float32)


def dot_cols(left, right):
    return lax.dot_general(left, right, NT, preferred_element_type=jnp.float32)


def low(value):
    return value.astype(jnp.bfloat16)


def wide(value):
    return value.astype(jnp.float32)


def pick(stacked, index):
    return lax.dynamic_index_in_dim(stacked, index, axis=0, keepdims=False)


def stage(run, ready, sends):
    count = len(ready)
    flat = lax.optimization_barrier((*ready, *[value for value, _ in sends]))
    outs = run(*flat[:count])
    moved = [move(value) for (_, move), value in zip(sends, flat[count:])]
    flat = lax.optimization_barrier((*outs, *moved))
    return (flat[: len(outs)], flat[len(outs) :])


def after(value, *others):
    return lax.optimization_barrier((value, *others))[0]


def head_lanes(half, rows):
    lane = lax.broadcasted_iota(jnp.int32, (rows, LANES), 1)
    return (lane < HEAD_DIM) if half == 0 else (lane >= HEAD_DIM)


def forward_kernel(sub, q_ref, kv_ref, bias_ref, out_ref, out32_ref, log_ref):
    rows = q_ref.shape[0]
    span = WINDOW + sub
    reach = kv_ref.shape[1] - rows
    for n in range(rows // sub):
        r0 = n * sub
        k0 = reach - WINDOW + r0
        keys = kv_ref[0, k0 : k0 + span, :]
        values = kv_ref[1, k0 : k0 + span, :]
        bias = bias_ref[r0 : r0 + sub, k0 : k0 + span]
        parts = []
        for half in range(2):
            query = jnp.where(
                head_lanes(half, sub), q_ref[r0 : r0 + sub, :] * jnp.bfloat16(SCALE), jnp.bfloat16(0)
            )
            scores = lax.dot_general(query, keys, NT, preferred_element_type=jnp.float32) + bias
            top = jnp.max(scores, axis=1, keepdims=True)
            weights = jnp.exp(scores - top)
            total = jnp.sum(weights, axis=1, keepdims=True)
            summed = jnp.dot(
                weights.astype(jnp.bfloat16), values, preferred_element_type=jnp.float32
            )
            parts.append((summed / total, top + jnp.log(total)))
        first = head_lanes(0, sub)
        out = jnp.where(first, parts[0][0], parts[1][0])
        out_ref[r0 : r0 + sub, :] = out.astype(jnp.bfloat16)
        out32_ref[r0 : r0 + sub, :] = out
        log_ref[r0 : r0 + sub, :] = jnp.where(first, parts[0][1], parts[1][1])


def sub_rows(rows):
    return 256 if rows % 256 == 0 else rows


def pair_block(rows):
    return pl.BlockSpec((rows, LANES), lambda h: (0, h))


def kv_block(rows):
    return pl.BlockSpec((2, rows, LANES), lambda h: (0, 0, h))


def attention_forward(query, kv, bias):
    rows, span = (query.shape[0], kv.shape[1])
    sub = sub_rows(rows)
    return pl.pallas_call(
        functools.partial(forward_kernel, sub),
        grid=(PAIRS,),
        in_specs=[
            pair_block(rows),
            kv_block(span),
            pl.BlockSpec((rows, span), lambda h: (0, 0)),
        ],
        out_specs=[pair_block(rows)] * 3,
        out_shape=[
            jax.ShapeDtypeStruct((rows, WIDE), kind)
            for kind in (jnp.bfloat16, jnp.float32, jnp.float32)
        ],
        compiler_params=pltpu.CompilerParams(vmem_limit_bytes=48 << 20),
        cost_estimate=hint(),
    )(query, kv, bias)


def backward_kernel(
    sub,
    q_ref,
    kv_ref,
    da_ref,
    out_ref,
    log_ref,
    bias_ref,
    *refs,
):
    dq_ref, dkv_ref, sum_k_ref, sum_v_ref = refs[-4:]
    rows = q_ref.shape[0]
    span = WINDOW + sub
    reach = kv_ref.shape[1] - rows
    sum_k_ref[...] = jnp.zeros_like(sum_k_ref)
    sum_v_ref[...] = jnp.zeros_like(sum_v_ref)
    for n in range(rows // sub):
        r0 = n * sub
        k0 = reach - WINDOW + r0
        all_da = da_ref[r0 : r0 + sub, :]
        product = jnp.transpose(all_da.astype(jnp.float32) * out_ref[r0 : r0 + sub, :])
        logs = jnp.transpose(log_ref[r0 : r0 + sub, :])
        all_query = q_ref[r0 : r0 + sub, :] * jnp.bfloat16(SCALE)
        keys = kv_ref[0, k0 : k0 + span, :]
        values = kv_ref[1, k0 : k0 + span, :]
        bias = bias_ref[k0 : k0 + span, r0 : r0 + sub]
        d_query = []
        for half in range(2):
            mask = head_lanes(half, sub)
            query = jnp.where(mask, all_query, jnp.bfloat16(0))
            da = jnp.where(mask, all_da, jnp.bfloat16(0))
            h0 = half * HEAD_DIM
            inner = jnp.sum(product[h0 : h0 + HEAD_DIM, :], axis=0, keepdims=True)
            log = logs[h0 : h0 + 1, :]
            scores = lax.dot_general(keys, query, NT, preferred_element_type=jnp.float32) + bias
            probs = jnp.exp(scores - log)
            d_probs = lax.dot_general(values, da, NT, preferred_element_type=jnp.float32)
            d_scores = (probs * (d_probs - inner)).astype(jnp.bfloat16)
            sum_v_ref[k0 : k0 + span, :] += jnp.dot(
                probs.astype(jnp.bfloat16), da, preferred_element_type=jnp.float32
            )
            sum_k_ref[k0 : k0 + span, :] += jnp.dot(
                d_scores, query, preferred_element_type=jnp.float32
            )
            d_query.append(
                lax.dot_general(d_scores, keys, TN, preferred_element_type=jnp.float32)
            )
        merged = jnp.where(head_lanes(0, sub), d_query[0], d_query[1])
        dq_ref[r0 : r0 + sub, :] = (merged * SCALE).astype(jnp.bfloat16)
    dkv_ref[0] = sum_k_ref[...].astype(jnp.bfloat16)
    dkv_ref[1] = sum_v_ref[...].astype(jnp.bfloat16)


def attention_backward(query, kv, d_attended, attended, logs, bias, first, last, earlier=()):
    rows, span = (query.shape[0], kv.shape[1])
    sub = sub_rows(rows)
    pair = pl.BlockSpec((rows, LANES), lambda h: (0, h + first))
    both = pl.BlockSpec((2, span, LANES), lambda h: (0, 0, h + first))
    return pl.pallas_call(
        functools.partial(backward_kernel, sub),
        grid=(last - first,),
        in_specs=[
            pair,
            both,
            pair,
            pair,
            pair,
            pl.BlockSpec((span, rows), lambda h: (0, 0)),
            *[pl.BlockSpec(memory_space=pl.ANY)] * len(earlier),
        ],
        out_specs=[pair, both],
        out_shape=[
            jax.ShapeDtypeStruct((rows, WIDE), jnp.bfloat16),
            jax.ShapeDtypeStruct((2, span, WIDE), jnp.bfloat16),
        ],
        input_output_aliases={6 + n: n for n in range(len(earlier))},
        scratch_shapes=[pltpu.VMEM((span, LANES), jnp.float32)] * 2,
        compiler_params=pltpu.CompilerParams(vmem_limit_bytes=48 << 20),
        cost_estimate=hint(),
    )(query, kv, d_attended, attended, logs, bias, *earlier)


def row_chunks(rows):
    step = 256 if rows % 256 == 0 else rows
    return [slice(n, n + step) for n in range(0, rows, step)]


def lane_block(cols, full):
    return min(full, full_lanes(cols))


def params(megabytes=56):
    return pltpu.CompilerParams(vmem_limit_bytes=megabytes << 20)


def hint():
    return pl.CostEstimate(flops=1 << 20, bytes_accessed=1 << 20, transcendentals=0)


def full_lanes(cols):
    return -(-cols // LANES) * LANES


def store_wide(ref, at, value):
    cols, full = (value.shape[1], ref.shape[-1])
    ref[(*at, slice(0, cols))] = value.astype(ref.dtype)
    if cols < full:
        ref[(*at, slice(cols, full))] = jnp.zeros((value.shape[0], full - cols), ref.dtype)


def assemble_kernel(cols, blocks_ref, qkv_ref, out_ref):
    count, rows, full = blocks_ref.shape
    fill = jnp.zeros((rows, WIDE - D), qkv_ref.dtype)

    def fill_in(write, start, stop, skip, size):
        for j in range(count):
            first, last = (max(start, j * size), min(stop, (j + 1) * size))
            if first < last:
                cut = slice(skip + first - j * size, skip + last - j * size)
                write(slice(first - start, last - start), blocks_ref[j, :, cut])

    for n in range(3):

        def write(cut, value, n=n):
            qkv_ref[n, :, cut] = value

        fill_in(write, n * D, (n + 1) * D, 0, cols)
        qkv_ref[n, :, D:] = fill

    def write_out(cut, value):
        out_ref[:, cut] = value

    fill_in(write_out, 0, D, cols, full - cols)


def assemble(blocks, cols):
    count, rows, full = blocks.shape
    step = 320 if rows % 320 == 0 else rows
    return pl.pallas_call(
        functools.partial(assemble_kernel, cols),
        grid=(rows // step,),
        in_specs=[pl.BlockSpec((count, step, full), lambda n: (0, n, 0))],
        out_specs=[
            pl.BlockSpec((3, step, WIDE), lambda n: (0, n, 0)),
            pl.BlockSpec((step, D), lambda n: (n, 0)),
        ],
        out_shape=[
            jax.ShapeDtypeStruct((3, rows, WIDE), blocks.dtype),
            jax.ShapeDtypeStruct((rows, D), blocks.dtype),
        ],
        compiler_params=params(),
        cost_estimate=hint(),
    )(blocks)


def project_kernel(x_ref, w_ref, bias_ref, q_ref, kv_ref):
    step = pl.program_id(0)
    rows, own = (x_ref.shape[0], q_ref.shape[0])

    @pl.when(step == 0)
    def _():
        for cut in row_chunks(own):
            at = slice(rows - own + cut.start, rows - own + cut.stop)
            total = jnp.dot(x_ref[at, :], w_ref[0], preferred_element_type=jnp.float32)
            q_ref[cut, :] = (total + bias_ref[0]).astype(q_ref.dtype)

    @pl.when(step > 0)
    def _():
        for cut in row_chunks(rows):
            total = jnp.dot(x_ref[cut, :], w_ref[0], preferred_element_type=jnp.float32)
            kv_ref[0, cut, :] = (total + bias_ref[0]).astype(kv_ref.dtype)


def project(x, weights, bias, own):
    rows, depth = x.shape
    full = weights.shape[2]
    return pl.pallas_call(
        project_kernel,
        grid=(3,),
        in_specs=[
            pl.BlockSpec((rows, depth), lambda t: (0, 0)),
            pl.BlockSpec((1, depth, full), lambda t: (t, 0, 0)),
            pl.BlockSpec((1, 1, full), lambda t: (t, 0, 0)),
        ],
        out_specs=[
            pl.BlockSpec((own, full), lambda t: (0, 0)),
            pl.BlockSpec((1, rows, full), lambda t: (jnp.maximum(t - 1, 0), 0, 0)),
        ],
        out_shape=[
            jax.ShapeDtypeStruct((own, full), jnp.bfloat16),
            jax.ShapeDtypeStruct((2, rows, full), jnp.bfloat16),
        ],
        compiler_params=params(),
        cost_estimate=hint(),
    )(x, weights, bias[:, None, :])


def norm_back_kernel(own_ref, got_ref, normal_ref, inverse_ref, gain_ref, dy_ref, *outs):
    wide_ref, low_ref, sums_ref = outs
    cols = own_ref.shape[1]
    grad = own_ref[...] + got_ref[:, :cols].astype(jnp.float32)
    normal = normal_ref[...]
    product = grad * normal
    scaled = grad * gain_ref[...]
    first = jnp.mean(scaled, axis=1, keepdims=True)
    second = jnp.mean(scaled * normal, axis=1, keepdims=True)
    out = dy_ref[:, :cols].astype(jnp.float32) + inverse_ref[...] * (
        scaled - first - normal * second
    )
    rounded = out.astype(jnp.bfloat16)
    wide_ref[...] = out
    store_wide(low_ref, (slice(None),), rounded)
    parts = [product, grad, rounded.astype(jnp.float32)]
    sums = jnp.concatenate([jnp.sum(part, axis=0, keepdims=True) for part in parts], axis=0)

    @pl.when(pl.program_id(0) == 0)
    def _():
        sums_ref[...] = sums

    @pl.when(pl.program_id(0) > 0)
    def _():
        sums_ref[...] += sums


def norm_back(own, got, normal, inverse, gain, dy):
    rows, cols = own.shape
    step = 128 if rows % 128 == 0 else rows
    block = lambda size: pl.BlockSpec((step, size), lambda n: (n, 0))
    return pl.pallas_call(
        norm_back_kernel,
        grid=(rows // step,),
        in_specs=[
            block(cols),
            block(got.shape[1]),
            block(cols),
            block(1),
            pl.BlockSpec((1, cols), lambda n: (0, 0)),
            block(dy.shape[1]),
        ],
        out_specs=[block(cols), block(WIDE), pl.BlockSpec((3, cols), lambda n: (0, 0))],
        out_shape=[
            jax.ShapeDtypeStruct((rows, cols), jnp.float32),
            jax.ShapeDtypeStruct((rows, WIDE), jnp.bfloat16),
            jax.ShapeDtypeStruct((3, cols), jnp.float32),
        ],
        compiler_params=params(),
        cost_estimate=hint(),
    )(own, got, normal, inverse, gain[None], dy)


def unit_of(w_ref, cols):
    parts, _, rows, lanes = w_ref.shape
    return w_ref[:, 0].reshape(parts * rows, lanes)[:, :cols]


def unit_block(weights, cols, lane):
    parts, _, rows, full = weights.shape
    return pl.BlockSpec((parts, 1, rows, lane_block(cols, full)), lambda b: (0, b, 0, lane))


def hidden_kernel(x_ref, w_ref, bias_ref, active_ref, slope_ref):
    cols = slope_ref.shape[2]
    weight = unit_of(w_ref, cols)
    depth = weight.shape[0]
    first, second = (0.7978845608028654, 0.044715)
    for rows in row_chunks(x_ref.shape[0]):
        u = jnp.dot(x_ref[rows, :depth], weight, preferred_element_type=jnp.float32) + bias_ref[0]
        square = u * u
        t = jnp.tanh(first * u * (1.0 + second * square))
        half = 0.5 * (1.0 + t)
        store_wide(active_ref, (0, rows), u * half)
        slope_ref[0, rows, :] = half + (0.5 * first) * u * (1.0 - t * t) * (
            1.0 + (3.0 * second) * square
        )


def ffn_hidden(x, weights, bias, cols, lane):
    count = weights.shape[1]
    rows = x.shape[0]
    return pl.pallas_call(
        hidden_kernel,
        grid=(count,),
        in_specs=[
            pl.BlockSpec(x.shape, lambda b: (0, 0)),
            unit_block(weights, cols, lane),
            pl.BlockSpec((1, 1, cols), lambda b: (b, 0, 0)),
        ],
        out_specs=[
            pl.BlockSpec((1, rows, size), lambda b: (b, 0, 0)) for size in (full_lanes(cols), cols)
        ],
        out_shape=[
            jax.ShapeDtypeStruct((count, rows, full_lanes(cols)), jnp.bfloat16),
            jax.ShapeDtypeStruct((count, rows, cols), jnp.float32),
        ],
        compiler_params=params(),
        cost_estimate=hint(),
    )(x, weights, bias[:, None, :])


def slope_kernel(dy_ref, w_ref, slope_ref, out_ref, sum_ref):
    total = None
    weight = unit_of(w_ref, slope_ref.shape[2])
    depth = weight.shape[0]
    for rows in row_chunks(dy_ref.shape[0]):
        d_active = jnp.dot(dy_ref[rows, :depth], weight, preferred_element_type=jnp.float32)
        part = (d_active * slope_ref[0, rows, :]).astype(jnp.bfloat16)
        store_wide(out_ref, (0, rows), part)
        sums = jnp.sum(part.astype(jnp.float32), axis=0, keepdims=True)
        total = sums if total is None else total + sums
    sum_ref[0] = total


def ffn_d_hidden(dy, weights, slope, lane):
    count, rows, cols = slope.shape
    block = lambda n, m: pl.BlockSpec((1, n, m), lambda b: (b, 0, 0))
    return pl.pallas_call(
        slope_kernel,
        grid=(count,),
        in_specs=[
            pl.BlockSpec(dy.shape, lambda b: (0, 0)),
            unit_block(weights, cols, lane),
            block(rows, cols),
        ],
        out_specs=[block(rows, full_lanes(cols)), block(1, cols)],
        out_shape=[
            jax.ShapeDtypeStruct((count, rows, full_lanes(cols)), jnp.bfloat16),
            jax.ShapeDtypeStruct((count, 1, cols), jnp.float32),
        ],
        compiler_params=params(),
        cost_estimate=hint(),
    )(dy, weights, slope)


def back_kernel(cols, x_ref, w_ref, out_ref, sum_ref):
    step = pl.program_id(0)
    part = lax.dot_general(
        x_ref[0][:, :cols], unit_of(w_ref, cols), NT, preferred_element_type=jnp.float32
    )

    @pl.when(step == 0)
    def _():
        sum_ref[...] = part

    @pl.when(step > 0)
    def _():
        sum_ref[...] += part

    @pl.when(step == pl.num_programs(0) - 1)
    def _():
        store_wide(out_ref, (slice(None),), sum_ref[...])


def ffn_back(x, weights, cols, lane, part, rows, kind):
    count = x.shape[0]
    width = weights.shape[0] * weights.shape[2]
    out_cols = WIDE if kind == jnp.bfloat16 else width
    return pl.pallas_call(
        functools.partial(back_kernel, cols),
        grid=(count,),
        in_specs=[
            pl.BlockSpec((1, rows, x.shape[2]), lambda b: (b, part, 0)),
            unit_block(weights, cols, lane),
        ],
        out_specs=pl.BlockSpec((rows, out_cols), lambda b: (0, 0)),
        out_shape=jax.ShapeDtypeStruct((rows, out_cols), kind),
        scratch_shapes=[pltpu.VMEM((rows, width), jnp.float32)],
        compiler_params=params(),
        cost_estimate=hint(),
    )(x, weights)


def index_list(parts):
    return jnp.stack([jnp.asarray(part, jnp.int32) for part in parts])


def by_left_kernel(at_r, at_q, left_ref, *refs):
    *rights, got_ref, out_ref = refs
    depth = rights[0].shape[1]
    cols = out_ref.shape[3]
    left = left_ref[0]
    for q, right_ref in enumerate(rights):
        total = jnp.dot(left[:, :depth], right_ref[0][:, :cols], preferred_element_type=jnp.float32)
        total += jnp.dot(left[:, depth:], got_ref[q][:, :cols], preferred_element_type=jnp.float32)
        out_ref[0, q] = total.astype(jnp.bfloat16)


def grads_by_left(left, right, got, cols, at_r, at_q):
    count, (_, rows, depth), (_, half, lanes) = (len(at_r), left.shape, right.shape)
    ny = len(at_q)
    own = lambda q: pl.BlockSpec((1, half, lanes), lambda r, a, b: (b[q], 0, 0))
    return pl.pallas_call(
        by_left_kernel,
        grid_spec=pltpu.PrefetchScalarGridSpec(
            num_scalar_prefetch=2,
            grid=(count,),
            in_specs=[
                pl.BlockSpec((1, rows, depth), lambda r, a, b: (a[r], 0, 0)),
                *[own(q) for q in range(ny)],
                pl.BlockSpec((ny, half, lanes), lambda r, a, b: (0, 0, 0)),
            ],
            out_specs=pl.BlockSpec((1, ny, rows, cols), lambda r, a, b: (r, 0, 0, 0)),
        ),
        out_shape=jax.ShapeDtypeStruct((count, ny, rows, cols), jnp.bfloat16),
        compiler_params=params(),
        cost_estimate=hint(),
    )(index_list(at_r), index_list(at_q), left, *[right] * ny, got)


def by_right_kernel(at_r, at_q, right_ref, right_got_ref, *refs):
    *lefts, got_ref, out_ref = refs
    cols = out_ref.shape[3]
    right, right_got = (right_ref[0][:, :cols], right_got_ref[0][:, :cols])
    for q, left_ref in enumerate(lefts):
        total = jnp.dot(left_ref[0], right, preferred_element_type=jnp.float32)
        total += jnp.dot(got_ref[q], right_got, preferred_element_type=jnp.float32)
        out_ref[0, q] = total.astype(jnp.bfloat16)


def grads_by_right(left, left_got, right, right_got, cols, at_r, at_q):
    count, (_, rows, depth) = (len(at_r), left.shape)
    ny = len(at_q)
    own = lambda q: pl.BlockSpec((1, rows, depth), lambda r, a, b: (b[q], 0, 0))
    moving = pl.BlockSpec((1, depth, right.shape[2]), lambda r, a, b: (a[r], 0, 0))
    return pl.pallas_call(
        by_right_kernel,
        grid_spec=pltpu.PrefetchScalarGridSpec(
            num_scalar_prefetch=2,
            grid=(count,),
            in_specs=[
                moving,
                moving,
                *[own(q) for q in range(ny)],
                pl.BlockSpec((ny, rows, depth), lambda r, a, b: (0, 0, 0)),
            ],
            out_specs=pl.BlockSpec((1, ny, rows, cols), lambda r, a, b: (r, 0, 0, 0)),
        ),
        out_shape=jax.ShapeDtypeStruct((count, ny, rows, cols), jnp.bfloat16),
        compiler_params=params(),
        cost_estimate=hint(),
    )(index_list(at_r), index_list(at_q), right, right_got, *[left] * ny, left_got)


def mixed_kernel(cols, own_rows, at_r, at_q, dq_ref, dq_got_ref, dkv_ref, dkv_got_ref, *refs):
    *lefts, got_ref, out_ref = refs
    step = pl.program_id(0)
    nc = out_ref.shape[0]
    for part, at_step in ((2, 0), (1, 1), (0, 2)):

        @pl.when(step == at_step)
        def _(part=part):
            for q, left_ref in enumerate(lefts):
                if part == 0:
                    first, second = (dq_ref[...], dq_got_ref[...])
                    left, got = (left_ref[0][:, -own_rows:], got_ref[q][:, -own_rows:])
                else:
                    first, second = (dkv_ref[0], dkv_got_ref[0])
                    left, got = (left_ref[0], got_ref[q])
                total = jnp.dot(left, first, preferred_element_type=jnp.float32)
                total += jnp.dot(got, second, preferred_element_type=jnp.float32)
                total = total.astype(jnp.bfloat16)
                for j in range(nc):
                    start, stop = (max(part * D, j * cols), min((part + 1) * D, (j + 1) * cols))
                    if start < stop:
                        out_ref[at_r[j], q, :, start - j * cols : stop - j * cols] = total[
                            :, start - part * D : stop - part * D
                        ]


def grads_mixed(left, left_got, d_query, query_got, d_kv, kv_got, cols, at_q):
    nc, _, ctx, _, _ = place()
    ny = len(at_q)
    _, rows, depth = left.shape
    own_rows, wide_cols = d_query.shape
    own = lambda q: pl.BlockSpec((1, rows, depth), lambda t, a, b: (b[q], 0, 0))
    once = pl.Buffered(1)
    query_block = pl.BlockSpec((own_rows, wide_cols), lambda t, a, b: (0, 0), pipeline_mode=once)
    kv_block = pl.BlockSpec(
        (1, depth, wide_cols), lambda t, a, b: (jnp.where(t == 0, 1, 0), 0, 0)
    )
    return pl.pallas_call(
        functools.partial(mixed_kernel, cols, own_rows),
        grid_spec=pltpu.PrefetchScalarGridSpec(
            num_scalar_prefetch=2,
            grid=(3,),
            in_specs=[
                query_block,
                query_block,
                kv_block,
                kv_block,
                *[own(q) for q in range(ny)],
                pl.BlockSpec((ny, rows, depth), lambda t, a, b: (0, 0, 0), pipeline_mode=once),
            ],
            out_specs=pl.BlockSpec((nc, ny, rows, cols), lambda t, a, b: (0, 0, 0, 0)),
        ),
        out_shape=jax.ShapeDtypeStruct((nc, ny, rows, cols), jnp.bfloat16),
        compiler_params=params(60),
        cost_estimate=hint(),
    )(
        index_list([(j - ctx) % nc for j in range(nc)]),
        index_list(at_q),
        d_query,
        query_got,
        d_kv,
        kv_got,
        *[left] * ny,
        left_got,
    )


def out_kernel(cols, at_r, at_q, right_ref, right_got_ref, *refs):
    *lefts, got_ref, out_ref = refs
    full = out_ref.shape[0] * cols
    right, right_got = (right_ref[:, :full], right_got_ref[:, :full])
    for q, left_ref in enumerate(lefts):
        total = jnp.dot(left_ref[0], right, preferred_element_type=jnp.float32)
        total += jnp.dot(got_ref[q], right_got, preferred_element_type=jnp.float32)
        total = total.astype(jnp.bfloat16)
        for j in range(out_ref.shape[0]):
            out_ref[at_r[j], q] = total[:, j * cols : (j + 1) * cols]


def grads_out(left, left_got, right, right_got, cols, at_q):
    nc, _, ctx, _, _ = place()
    ny = len(at_q)
    _, rows, depth = left.shape
    own = lambda q: pl.BlockSpec((1, rows, depth), lambda t, a, b: (b[q], 0, 0))
    right_block = pl.BlockSpec(right.shape, lambda t, a, b: (0, 0))
    return pl.pallas_call(
        functools.partial(out_kernel, cols),
        grid_spec=pltpu.PrefetchScalarGridSpec(
            num_scalar_prefetch=2,
            grid=(1,),
            in_specs=[
                right_block,
                right_block,
                *[own(q) for q in range(ny)],
                pl.BlockSpec((ny, rows, depth), lambda t, a, b: (0, 0, 0)),
            ],
            out_specs=pl.BlockSpec((nc, ny, rows, cols), lambda t, a, b: (0, 0, 0, 0)),
        ),
        out_shape=jax.ShapeDtypeStruct((nc, ny, rows, cols), jnp.bfloat16),
        compiler_params=params(),
        cost_estimate=hint(),
    )(
        index_list([(j - ctx) % nc for j in range(nc)]),
        index_list(at_q),
        right,
        right_got,
        *[left] * ny,
        left_got,
    )


def normed_kernel(dq_ref, dkv_ref, w_ref, out_ref):
    step = pl.program_id(0)
    rows = out_ref.shape[0]
    own = dq_ref.shape[0]

    @pl.when(step == 0)
    def _():
        for cut in row_chunks(rows):
            out_ref[cut, :] = lax.dot_general(
                dkv_ref[0, cut, :], w_ref[0], NT, preferred_element_type=jnp.float32
            )

    @pl.when(step == 1)
    def _():
        for cut in row_chunks(rows):
            out_ref[cut, :] += lax.dot_general(
                dkv_ref[0, cut, :], w_ref[0], NT, preferred_element_type=jnp.float32
            )

    @pl.when(step == 2)
    def _():
        out_ref[rows - own :, :] += lax.dot_general(
            dq_ref[...], w_ref[0], NT, preferred_element_type=jnp.float32
        )


def normed_back(d_query, d_kv, weights):
    own, wide_cols = d_query.shape
    rows = d_kv.shape[1]
    return pl.pallas_call(
        normed_kernel,
        grid=(3,),
        in_specs=[
            pl.BlockSpec((own, wide_cols), lambda t: (0, 0)),
            pl.BlockSpec((1, rows, wide_cols), lambda t: (jnp.where(t == 0, 1, 0), 0, 0)),
            pl.BlockSpec((1, D, wide_cols), lambda t: (2 - t, 0, 0)),
        ],
        out_specs=pl.BlockSpec((rows, D), lambda t: (0, 0)),
        out_shape=jax.ShapeDtypeStruct((rows, D), jnp.float32),
        compiler_params=params(),
        cost_estimate=hint(),
    )(d_query, d_kv, weights)


def place():
    nc, nd = (lax.axis_size("ctx"), lax.axis_size("dat"))
    ctx, dat = (lax.axis_index("ctx"), lax.axis_index("dat"))
    return (nc, nd, ctx, dat // 2, dat % 2)


def dat_of(q, other):
    _, nd, _, y, core = place()
    return 2 * ((y + q) % (nd // 2)) + (1 - core if other else core)


def ctx_of(r):
    nc, _, ctx, _, _ = place()
    return (ctx + r) % nc


def swap_core(value):
    return swap_dat(value, 1)


def ny_of():
    return lax.axis_size("dat") // 2


def y_sends(parts):
    return [(parts[q], functools.partial(roll_y, steps=q)) for q in range(1, ny_of())]


def z_send(part, r):
    return (part, functools.partial(roll_ctx, steps=r))


def sum_of(parts):
    total = wide(parts[0])
    for part in parts[1:]:
        total = total + wide(part)
    return total


def odd_kept(blocks, n, q):
    return jnp.where(lax.axis_index("rep") == 0, blocks[n, q], blocks[n + 2, q])


def odd_given(blocks, n, q):
    return (jnp.where(lax.axis_index("rep") == 0, blocks[n + 2, q], blocks[n, q]), swap_rep)


def odd_z_send(part, n):
    return (part, functools.partial(roll_ctx_by_rep, steps=(n, n + 2)))


def gather_small(vector):
    nc, _, ctx, _, _ = place()
    out = jnp.zeros((nc,) + vector.shape, vector.dtype)
    for r in range(nc):
        part = roll_ctx(vector, r) if r else vector
        out = lax.dynamic_update_index_in_dim(out, part, (ctx - r) % nc, 0)
    return out


def sum_small(parts):
    nc, nd, _, _, _ = place()
    stacked = jnp.concatenate([part.reshape(nc, -1) for part in parts], axis=1)
    total = pick(stacked, ctx_of(0))
    for r in range(1, nc):
        total = total + roll_ctx(pick(stacked, ctx_of(r)), r)
    bit = 1
    while bit < nd:
        total = total + swap_dat(total, bit)
        bit *= 2
    total = total + swap_rep(total)
    outs, at = ([], 0)
    for part in parts:
        size = part.shape[0] // nc
        outs.append(total[at : at + size])
        at += size
    return outs


def pad_cols(value):
    return jnp.pad(value, ((0, 0), (0, WIDE - value.shape[1])))


def regroup(units, count):
    have, rows, cols = units.shape
    if have == count:
        return units
    if have > count:
        per = have // count
        return units.reshape(count, per, rows, cols).swapaxes(1, 2).reshape(count, rows, -1)
    per = count // have
    return units.reshape(have, rows, per, cols // per).swapaxes(1, 2).reshape(count, rows, -1)


def regroup_wide(units, cols, count):
    if units.shape[0] == count:
        return units
    value = regroup(units[:, :, :cols], count)
    return jnp.pad(value, ((0, 0), (0, 0), (0, full_lanes(value.shape[2]) - value.shape[2])))


def local(
    tokens,
    segments,
    cotangent,
    ln1_gain,
    ln1_bias,
    w_qkv,
    b_qv,
    w_out,
    b_out,
    ln2_gain,
    ln2_bias,
    w_fc,
    b_fc,
    w_proj,
    b_proj,
):
    nc, nd, ctx, y, core = place()
    rep = lax.axis_index("rep")
    ff = w_fc.shape[1] * nc
    row_count = tokens.shape[1]
    reach_count = -(-WINDOW // row_count)
    reach_rows = reach_count * row_count

    blocks = max(nc, nd)
    width = ff // blocks // 2
    per_b, per_c = (blocks // nc, blocks // nd)
    qkv_cols, out_cols = (w_qkv.shape[1], w_out.shape[1])
    fc_cols = per_b * width

    small_all = gather_small(
        low(jnp.concatenate([ln1_gain, ln1_bias, b_qv, b_out, ln2_gain, ln2_bias, b_fc, b_proj]))
    )
    smalls, at = ([], 0)
    for part in (ln1_gain, ln1_bias, b_qv, b_out, ln2_gain, ln2_bias, b_fc, b_proj):
        size = part.shape[0]
        smalls.append(wide(small_all[:, at : at + size].reshape(-1)))
        at += size
    gain_one, shift_one, bias_qv, bias_out, gain_two, shift_two, bias_fc, bias_proj = smalls
    bias_half = bias_fc.reshape(blocks, 2, width)
    bias_half = lax.dynamic_index_in_dim(bias_half, rep, axis=1, keepdims=False)

    stretches = [pad_cols(tokens[0])]
    for n in range(reach_count):
        stretches.insert(0, shift_ctx(stretches[0], 1, n, nc - 1))
    all_tokens = jnp.concatenate(stretches, axis=0)[:, :D]
    inputs = wide(tokens[0])
    d_ffn = cotangent[0]
    d_ffn_wide = pad_cols(d_ffn)
    d_ffn_pair = jnp.concatenate([d_ffn_wide, swap_rep(d_ffn_wide)], axis=0)
    d_ffn_quad = jnp.concatenate([d_ffn_pair, swap_core(d_ffn_pair)], axis=0)[:, :D]
    d_ffn_quad = d_ffn_quad.T.reshape(nc, D // nc, -1)
    at_ctx = [ctx_of(r) for r in range(nc)]
    at_own = [dat_of(q, False) for q in range(nd // 2)]
    at_other = [dat_of(q, True) for q in range(nd // 2)]

    def from_other_core(stacked):
        return swap_core(jnp.stack([pick(stacked, at) for at in at_other]))

    shard_a = jnp.concatenate([low(w_qkv), low(w_out)], axis=1)
    full_a = lax.all_gather(shard_a, ("ctx", "dat"), axis=0, tiled=True)
    full_a = full_a.reshape(nc, D, qkv_cols + out_cols)
    fc_half = lax.dynamic_index_in_dim(
        low(w_fc).reshape(-1, per_b, 2, width), rep, axis=2, keepdims=False
    ).reshape(-1, fc_cols)
    proj_half = lax.dynamic_index_in_dim(
        low(w_proj).reshape(per_c, 2, width, -1), rep, axis=1, keepdims=False
    ).reshape(per_c * width, -1)
    proj_half = proj_half.T
    if nc == nd:
        fill = jnp.zeros((fc_half.shape[0], full_lanes(width) - width), jnp.bfloat16)
        shard_b = jnp.concatenate([fc_half, fill, proj_half, fill], axis=1)
        shard_b = after(shard_b, stretches[-2], small_all)
        units_fc = lax.all_gather(shard_b, ("ctx", "dat"), axis=0, tiled=True)
        units_proj = units_fc.reshape(nc, nd, D // nd, -1)
        units_fc = units_fc.reshape(1, nc, D, -1)
        lane_proj = 1
    else:
        units_fc = lax.all_gather(fc_half, ("ctx", "dat"), axis=0, tiled=True)
        units_proj = lax.all_gather(proj_half, ("dat", "ctx"), axis=0, tiled=True)
        units_fc = regroup(units_fc.reshape(nc, D, -1), blocks)[None]
        units_proj = regroup(units_proj.reshape(nd, D, -1), blocks)[None]
        lane_proj = 0

    normed_all, normal_all, inverse_all = norm_forward(wide(all_tokens), gain_one, shift_one)
    normed_all = low(normed_all)
    left_one = normed_all.T.reshape(nd, D // nd, -1)
    left_one_got = from_other_core(left_one)
    d_ffn_quad, left_one, normed_all = lax.optimization_barrier((d_ffn_quad, left_one, normed_all))
    full_a = after(full_a, left_one, d_ffn_quad)
    weights_qkv, weight_out = assemble(full_a, qkv_cols)
    bias_qkv = jnp.stack([bias_qv[:D], jnp.zeros((D,), jnp.float32), bias_qv[D:]])
    query, kv = project(normed_all, weights_qkv, pad_cols(bias_qkv), row_count)

    segment_row = segments[0]
    padded_segment = jnp.concatenate([jnp.full((reach_rows,), -1, jnp.int32), segment_row])
    key_segment = lax.dynamic_slice_in_dim(padded_segment, ctx * row_count, reach_rows + row_count)
    query_segment = lax.dynamic_slice_in_dim(segment_row, ctx * row_count, row_count)
    query_position = reach_rows + jnp.arange(row_count, dtype=jnp.int32)
    key_position = jnp.arange(reach_rows + row_count, dtype=jnp.int32)

    def mask(at_query, at_key):
        visible = (
            (at_query(query_segment) == at_key(key_segment))
            & (at_key(key_position) <= at_query(query_position))
            & (at_key(key_position) > at_query(query_position) - WINDOW)
        )
        return jnp.where(visible, 0.0, MASKED)

    as_column, as_row = (lambda v: v[:, None], lambda v: v[None, :])
    bias_forward, bias_back = (mask(as_column, as_row), mask(as_row, as_column))
    bias_forward = after(bias_forward, bias_back)
    attended, attended_wide, logs = attention_forward(query, kv, bias_forward)
    resid = inputs + dot(attended[:, :D], weight_out) + bias_out
    normed_two, normal_two, inverse_two = norm_forward(resid, gain_two, shift_two)
    normed_two = pad_cols(low(normed_two))
    normed_two_got = swap_rep(normed_two)
    left_out = attended[:, :D].T.reshape(nd, D // nd, -1)
    left_out_got = from_other_core(left_out)
    normed_two_got = after(normed_two_got, left_out)
    normed_two_pair = jnp.concatenate([normed_two, normed_two_got], axis=0)
    left_two = normed_two_pair[:, :D].T.reshape(nd, D // nd, -1)
    left_two_got = from_other_core(left_two)

    active, slope = ffn_hidden(normed_two_pair, units_fc, bias_half, width, 0)
    active_dat = regroup_wide(active, width, nd)
    given = jnp.stack([pick(active_dat, at) for at in at_other])
    (d_hidden, grad_bias_fc), (active_got,) = stage(
        lambda x: ffn_d_hidden(x, units_proj, slope, lane_proj),
        [d_ffn_pair],
        [(given, swap_core)],
    )
    d_hidden_ctx = regroup_wide(d_hidden, width, nc)
    (blocks_proj,), (d_hidden_got,) = stage(
        lambda x: (
            grads_by_left(d_ffn_quad, x, active_got, per_c * width, at_ctx, at_own),
        ),
        [active_dat],
        [(d_hidden_ctx, swap_core)],
    )
    ny = ny_of()
    split = row_count // 2
    order = [*range(1, nc, 2), *range(2, nc, 2), 0]
    proj_y, proj_z, fc_y, fc_z = ({}, {}, {}, {})

    def y_of(blocks, steps):
        return [send for r in steps for send in y_sends([blocks[r, q] for q in range(ny)])]

    def take_y(blocks, moved, steps, into):
        for r in steps:
            parts, moved = (moved[: ny - 1], moved[ny - 1 :])
            into[r] = low(sum_of([blocks[r, 0], *parts]))
        return moved

    odd, even = (order[: nc // 2], order[nc // 2 : -1])
    first, second = (odd[: len(odd) // 2], odd[len(odd) // 2 :])
    (d_theirs,), moved = stage(
        lambda x: (ffn_back(x, units_fc, width, 0, 1, row_count, jnp.bfloat16),),
        [d_hidden],
        y_of(blocks_proj, first),
    )
    take_y(blocks_proj, moved, first, proj_y)
    (blocks_fc,), (got_top, *moved) = stage(
        lambda x: (
            grads_by_right(left_two, left_two_got, x, d_hidden_got, fc_cols, at_ctx, at_own),
        ),
        [d_hidden_ctx],
        [
            (d_theirs[:split], swap_rep),
            *y_of(blocks_proj, second),
            *[z_send(proj_y[r], r) for r in first],
        ],
    )
    moved = take_y(blocks_proj, moved, second, proj_y)
    proj_z.update(zip(first, moved))
    (d_normed_two,), (got_rest, *moved) = stage(
        lambda x: (ffn_back(x, units_fc, width, 0, 0, row_count, jnp.float32),),
        [after(d_hidden, blocks_fc)],
        [
            (d_theirs[split:], swap_rep),
            *y_of(blocks_proj, even),
            *[z_send(proj_y[r], r) for r in second],
        ],
    )
    moved = take_y(blocks_proj, moved, even, proj_y)
    proj_z.update(zip(second, moved))
    d_normed_got = jnp.concatenate([got_top, got_rest], axis=0)

    def to_branch(x):
        d_resid, d_branch, sums = norm_back(
            x, d_normed_got, normal_two, inverse_two, gain_two, d_ffn_wide
        )
        d_branch_got = swap_core(d_branch)
        d_attended = pad_cols(low(dot_cols(d_branch[:, :D], weight_out)))
        blocks_out = grads_out(
            left_out, left_out_got, after(d_branch, d_attended), d_branch_got, out_cols, at_own
        )
        return (d_resid, sums, d_attended, blocks_out)

    (d_resid, sums_two, d_attended, blocks_out), moved = stage(
        to_branch,
        [d_normed_two],
        [*y_of(blocks_proj, [0]), *[z_send(proj_y[r], r) for r in even]],
    )
    moved = take_y(blocks_proj, moved, [0], proj_y)
    proj_z.update(zip(even, moved))
    proj_total = low(sum_of([proj_y[0], *proj_z.values()]))

    pairs_at = [(n, q) for n in range(1, nc, 4) for q in reversed(range(ny))]
    middle = PAIRS // 2
    earlier, moved = stage(
        lambda x: attention_backward(
            query, kv, x, attended_wide, logs, bias_back, 0, middle
        ),
        [d_attended],
        [
            *y_of(blocks_fc, odd),
            *[odd_given(blocks_out, n, q) for n, q in pairs_at],
            (proj_total, swap_rep),
        ],
    )
    moved = take_y(blocks_fc, moved, odd, fc_y)
    out_kept = {
        at: low(wide(odd_kept(blocks_out, *at)) + wide(got)) for at, got in zip(pairs_at, moved)
    }
    proj_got = moved[-1]
    (d_query, d_kv), moved = stage(
        lambda x, *done: attention_backward(
            query, kv, x, attended_wide, logs, bias_back, middle, PAIRS, done
        ),
        [d_attended, *earlier],
        [
            *y_of(blocks_fc, [*even, 0]),
            *[z_send(fc_y[r], r) for r in odd],
        ],
    )
    moved = take_y(blocks_fc, moved, [*even, 0], fc_y)
    fc_z.update(zip(odd, moved))

    def odd_y_sends(kept):
        return [
            send
            for n in range(1, nc, 4)
            for send in y_sends([kept[n, q] for q in range(ny)])
        ]

    def take_odd_y(kept, moved):
        sums = {}
        for n in range(1, nc, 4):
            parts, moved = (moved[: ny - 1], moved[ny - 1 :])
            sums[n] = low(sum_of([kept[n, 0], *parts]))
        return (sums, moved)

    (d_normed_all,), (d_query_got, d_kv_got, *moved) = stage(
        lambda x: (normed_back(x, d_kv, weights_qkv),),
        [d_query],
        [
            (d_query, swap_core),
            (d_kv, swap_core),
            *[z_send(fc_y[r], r) for r in even],
            *odd_y_sends(out_kept),
            *y_of(blocks_out, [*even, 0]),
        ],
    )
    fc_z.update(zip(even, moved))
    out_odd, moved = take_odd_y(out_kept, moved[len(even) :])
    out_y = {}
    take_y(blocks_out, moved, [*even, 0], out_y)
    fc_total = low(sum_of([fc_y[0], *fc_z.values()]))
    d_normed_halo, d_normed_own = (d_normed_all[:reach_rows], d_normed_all[reach_rows:])
    returned = pad_cols(low(d_normed_halo[:row_count]))
    for n in range(1, reach_count - 1):
        returned = shift_ctx(returned, -1, reach_count + 1 - n, nc)
        part = d_normed_halo[n * row_count : (n + 1) * row_count]
        returned = pad_cols(low(wide(returned[:, :D]) + part))
    back_one = functools.partial(shift_ctx, steps=-1, first=min(2, reach_count), last=nc)
    (blocks_qkv,), (returned, fc_got, *moved) = stage(
        lambda x: (
            grads_mixed(
                left_one, left_one_got, x, d_query_got, d_kv, d_kv_got, qkv_cols, at_own
            ),
        ),
        [d_query],
        [
            (returned, back_one),
            (fc_total, swap_rep),
            *[z_send(out_y[r], r) for r in even],
            *[odd_z_send(out_odd[n], n) for n in out_odd],
        ],
    )
    out_total = low(sum_of([out_y[0], *moved]))
    if reach_count > 1:
        part = d_normed_halo[reach_rows - row_count :]
        returned = pad_cols(low(wide(returned[:, :D]) + part))
        back_two = functools.partial(shift_ctx, steps=-1, first=1, last=nc)
    else:
        back_two = lambda value: value

    last_q, rest_q = (pairs_at[: len(pairs_at) // 2], pairs_at[len(pairs_at) // 2 :])
    qkv_y, qkv_z, qkv_kept = ({}, [], {})
    (ffn_theirs,), (out_got, *moved) = stage(
        lambda x: (ffn_back(x, units_proj, width, lane_proj, 1, row_count, jnp.bfloat16),),
        [active],
        [
            (out_total, swap_rep),
            *y_of(blocks_qkv, even),
            *[odd_given(blocks_qkv, *at) for at in last_q],
        ],
    )
    grad_out_weight = wide(out_total) + wide(out_got)
    moved = take_y(blocks_qkv, moved, even, qkv_y)
    for at, got in zip(last_q, moved):
        qkv_kept[at] = low(wide(odd_kept(blocks_qkv, *at)) + wide(got))
    (ffn_own,), moved = stage(
        lambda x: (ffn_back(x, units_proj, width, lane_proj, 0, row_count, jnp.float32),),
        [after(active, ffn_theirs)],
        [
            *y_of(blocks_qkv, [0]),
            *[z_send(qkv_y[r], r) for r in even],
            *[odd_given(blocks_qkv, *at) for at in rest_q],
        ],
    )
    moved = take_y(blocks_qkv, moved, [0], qkv_y)
    qkv_z += moved[: len(even)]
    for at, got in zip(rest_q, moved[len(even) :]):
        qkv_kept[at] = low(wide(odd_kept(blocks_qkv, *at)) + wide(got))
    returned = back_two(returned)
    ffn_got = swap_rep(ffn_theirs)
    moved = [move(value) for value, move in odd_y_sends(qkv_kept)]
    qkv_odd, _ = take_odd_y(qkv_kept, moved)
    qkv_z += [move(value) for value, move in [odd_z_send(qkv_odd[n], n) for n in qkv_odd]]
    qkv_total = low(sum_of([qkv_y[0], *qkv_z]))
    grad_qkv = wide(qkv_total) + wide(swap_rep(qkv_total))
    layer_out = low(resid + ffn_own + wide(ffn_got[:, :D]) + bias_proj)
    grad_gain_two, grad_shift_two, grad_bias_out = after(sums_two, blocks_qkv)
    grad_bias_proj = jnp.sum(wide(d_ffn), axis=0)
    grad_bias_fc = after(grad_bias_fc, blocks_qkv)

    grad_bias_query = jnp.sum(wide(d_query[:, :D]), axis=0)
    grad_bias_values = jnp.sum(wide(d_kv[1, :, :D]), axis=0)
    grad_gain_one = jnp.sum(d_normed_halo * normal_all[:reach_rows], axis=0) + jnp.sum(
        d_normed_own * normal_all[reach_rows:], axis=0
    )
    grad_shift_one = jnp.sum(d_normed_halo, axis=0) + jnp.sum(d_normed_own, axis=0)
    d_normed_one = d_normed_own + wide(returned[:, :D])
    input_grad = low(
        d_resid
        + norm_backward(d_normed_one, gain_one, normal_all[reach_rows:], inverse_all[reach_rows:])
    )

    def widen(half, got):
        first = jnp.where(rep == 0, half, got)
        second = jnp.where(rep == 0, got, half)
        return wide(jnp.stack([first, second], axis=1)).reshape(-1, half.shape[2])

    def units_first(half, units):
        return half.T.reshape(units, width, -1)

    fc_half_low, fc_half_got = (fc_total, fc_got)
    proj_half_low, proj_half_got = (proj_total, proj_got)
    rows_fc = fc_half_low.shape[0]
    first = jnp.where(rep == 0, fc_half_low, fc_half_got).reshape(rows_fc, per_b, 1, width)
    second = jnp.where(rep == 0, fc_half_got, fc_half_low).reshape(rows_fc, per_b, 1, width)
    grad_fc = wide(jnp.concatenate([first, second], axis=2).reshape(rows_fc, -1))
    grad_proj = widen(units_first(proj_half_low, per_c), units_first(proj_half_got, per_c))

    grad_bias_fc = grad_bias_fc.reshape(blocks, width)
    zero = jnp.zeros_like(grad_bias_fc)
    grad_bias_fc = jnp.stack(
        [jnp.where(rep == 0, grad_bias_fc, zero), jnp.where(rep == 0, zero, grad_bias_fc)], axis=1
    ).reshape(-1)
    small_out = sum_small(
        [grad_bias_out, grad_gain_two, grad_shift_two, grad_bias_fc, grad_bias_proj]
    )
    grad_bias_out, grad_gain_two, grad_shift_two, grad_bias_fc, grad_bias_proj = small_out
    grad_bias_qv = jnp.concatenate([grad_bias_query, grad_bias_values])
    grad_gain_one, grad_shift_one, grad_bias_qv = sum_small(
        [grad_gain_one, grad_shift_one, grad_bias_qv]
    )

    return (
        layer_out[None],
        input_grad[None],
        grad_gain_one,
        grad_shift_one,
        grad_qkv,
        grad_bias_qv,
        grad_out_weight,
        grad_bias_out,
        grad_gain_two,
        grad_shift_two,
        grad_fc,
        grad_bias_fc,
        grad_proj,
        grad_bias_proj,
    )


def solution(mesh):
    in_specs = (
        P(("rep", "dat"), "ctx", None),
        P(("rep", "dat"), None),
        P(("rep", "dat"), "ctx", None),
        P("ctx"),
        P("ctx"),
        P("dat", "ctx"),
        P("ctx"),
        P("dat", "ctx"),
        P("ctx"),
        P("ctx"),
        P("ctx"),
        P("dat", "ctx"),
        P("ctx"),
        P("dat", "ctx"),
        P("ctx"),
    )
    out_specs = (
        P(("rep", "dat"), "ctx", None),
        P(("rep", "dat"), "ctx", None),
        P("ctx"),
        P("ctx"),
        P("dat", "ctx"),
        P("ctx"),
        P("dat", "ctx"),
        P("ctx"),
        P("ctx"),
        P("ctx"),
        P("dat", "ctx"),
        P("ctx"),
        P("dat", "ctx"),
        P("ctx"),
    )
    return jax.shard_map(local, mesh=mesh, in_specs=in_specs, out_specs=out_specs, check_vma=False)
```

```python
import functools

import jax
import jax.numpy as jnp
from jax import lax
from jax.experimental import pallas as pl
from jax.experimental.pallas import tpu as pltpu
from jax.sharding import PartitionSpec as P

D = 1600
HEADS = 25
HEAD_DIM = 64
WINDOW = 1024


EPS = 1e-05
MASKED = -1e30
LANES = 128
PAIRS = -(-HEADS // 2)
WIDE = PAIRS * LANES
SCALE = HEAD_DIM ** (-0.5)
NT = (((1,), (1,)), ((), ()))
TN = (((0,), (0,)), ((), ()))


def permute(value, axes, pairs):
    return lax.ppermute(value, axes, pairs)


def roll_ctx(value, steps):
    count = lax.axis_size("ctx")
    return permute(value, "ctx", [(s, (s + steps) % count) for s in range(count)])


def shift_ctx(value, steps, first, last):
    return permute(value, "ctx", [(s, s + steps) for s in range(first, last)])


def roll_ctx_by_rep(value, steps):
    count = lax.axis_size("ctx")
    pairs = [
        (rep * count + s, rep * count + (s + steps[rep]) % count)
        for rep in range(len(steps))
        for s in range(count)
    ]
    return permute(value, ("rep", "ctx"), pairs)


def roll_y(value, steps):
    count = lax.axis_size("dat")
    return permute(value, "dat", [(s, (s + 2 * steps) % count) for s in range(count)])


def swap_dat(value, bit):
    count = lax.axis_size("dat")
    return permute(value, "dat", [(s, s ^ bit) for s in range(count)])


def swap_rep(value):
    return permute(value, "rep", [(0, 1), (1, 0)])


def norm_forward(values, gain, shift):
    average = jnp.mean(values, axis=-1, keepdims=True)
    centred = values - average
    variance = jnp.mean(centred * centred, axis=-1, keepdims=True)
    inverse = lax.rsqrt(variance + EPS)
    normal = centred * inverse
    return (normal * gain + shift, normal, inverse)


def norm_backward(grad_out, gain, normal, inverse):
    scaled = grad_out * gain
    first = jnp.mean(scaled, axis=-1, keepdims=True)
    second = jnp.mean(scaled * normal, axis=-1, keepdims=True)
    return inverse * (scaled - first - normal * second)


def dot(left, right):
    return jnp.dot(left, right, preferred_element_type=jnp.float32)


def dot_cols(left, right):
    return lax.dot_general(left, right, NT, preferred_element_type=jnp.float32)


def low(value):
    return value.astype(jnp.bfloat16)


def wide(value):
    return value.astype(jnp.float32)


def pick(stacked, index):
    return lax.dynamic_index_in_dim(stacked, index, axis=0, keepdims=False)


def stage(run, ready, sends):
    count = len(ready)
    flat = lax.optimization_barrier((*ready, *[value for value, _ in sends]))
    outs = run(*flat[:count])
    moved = [move(value) for (_, move), value in zip(sends, flat[count:])]
    flat = lax.optimization_barrier((*outs, *moved))
    return (list(flat[: len(outs)]), list(flat[len(outs) :]))


def after(value, *others):
    return lax.optimization_barrier((value, *others))[0]


def head_lanes(half, rows):
    lane = lax.broadcasted_iota(jnp.int32, (rows, LANES), 1)
    return (lane < HEAD_DIM) if half == 0 else (lane >= HEAD_DIM)


def forward_kernel(sub, q_ref, kv_ref, bias_ref, out_ref, out32_ref, log_ref):
    rows = q_ref.shape[0]
    span = WINDOW + sub
    reach = kv_ref.shape[1] - rows
    for n in range(rows // sub):
        r0 = n * sub
        k0 = reach - WINDOW + r0
        keys = kv_ref[0, k0 : k0 + span, :]
        values = kv_ref[1, k0 : k0 + span, :]
        bias = bias_ref[r0 : r0 + sub, k0 : k0 + span]
        parts = []
        for half in range(2):
            query = jnp.where(
                head_lanes(half, sub), q_ref[r0 : r0 + sub, :] * jnp.bfloat16(SCALE), jnp.bfloat16(0)
            )
            scores = lax.dot_general(query, keys, NT, preferred_element_type=jnp.float32) + bias
            top = jnp.max(scores, axis=1, keepdims=True)
            weights = jnp.exp(scores - top)
            total = jnp.sum(weights, axis=1, keepdims=True)
            summed = jnp.dot(
                weights.astype(jnp.bfloat16), values, preferred_element_type=jnp.float32
            )
            parts.append((summed / total, top + jnp.log(total)))
        first = head_lanes(0, sub)
        out = jnp.where(first, parts[0][0], parts[1][0])
        out_ref[r0 : r0 + sub, :] = out.astype(jnp.bfloat16)
        out32_ref[r0 : r0 + sub, :] = out
        log_ref[r0 : r0 + sub, :] = jnp.where(first, parts[0][1], parts[1][1])


def sub_rows(rows):
    return 256 if rows % 256 == 0 else rows


def pair_block(rows):
    return pl.BlockSpec((rows, LANES), lambda h: (0, h))


def kv_block(rows):
    return pl.BlockSpec((2, rows, LANES), lambda h: (0, 0, h))


def attention_forward(query, kv, bias):
    rows, span = (query.shape[0], kv.shape[1])
    sub = sub_rows(rows)
    return pl.pallas_call(
        functools.partial(forward_kernel, sub),
        grid=(PAIRS,),
        in_specs=[
            pair_block(rows),
            kv_block(span),
            pl.BlockSpec((rows, span), lambda h: (0, 0)),
        ],
        out_specs=[pair_block(rows)] * 3,
        out_shape=[
            jax.ShapeDtypeStruct((rows, WIDE), kind)
            for kind in (jnp.bfloat16, jnp.float32, jnp.float32)
        ],
        compiler_params=pltpu.CompilerParams(vmem_limit_bytes=48 << 20),
        cost_estimate=hint(),
    )(query, kv, bias)


def backward_kernel(
    sub,
    q_ref,
    kv_ref,
    da_ref,
    attended_ref,
    log_ref,
    bias_ref,
    *refs,
):
    out_ref, sum_k_ref, sum_v_ref = refs[-3:]
    rows = q_ref.shape[0]
    span = WINDOW + sub
    reach = kv_ref.shape[1] - rows
    sum_k_ref[...] = jnp.zeros_like(sum_k_ref)
    sum_v_ref[...] = jnp.zeros_like(sum_v_ref)
    for n in range(rows // sub):
        r0 = n * sub
        k0 = reach - WINDOW + r0
        all_da = da_ref[r0 : r0 + sub, :]
        product = jnp.transpose(all_da.astype(jnp.float32) * attended_ref[r0 : r0 + sub, :])
        logs = jnp.transpose(log_ref[r0 : r0 + sub, :])
        all_query = q_ref[r0 : r0 + sub, :] * jnp.bfloat16(SCALE)
        keys = kv_ref[0, k0 : k0 + span, :]
        values = kv_ref[1, k0 : k0 + span, :]
        bias = bias_ref[k0 : k0 + span, r0 : r0 + sub]
        d_query = []
        for half in range(2):
            mask = head_lanes(half, sub)
            query = jnp.where(mask, all_query, jnp.bfloat16(0))
            da = jnp.where(mask, all_da, jnp.bfloat16(0))
            h0 = half * HEAD_DIM
            inner = jnp.sum(product[h0 : h0 + HEAD_DIM, :], axis=0, keepdims=True)
            log = logs[h0 : h0 + 1, :]
            scores = lax.dot_general(keys, query, NT, preferred_element_type=jnp.float32) + bias
            probs = jnp.exp(scores - log)
            d_probs = lax.dot_general(values, da, NT, preferred_element_type=jnp.float32)
            d_scores = (probs * (d_probs - inner)).astype(jnp.bfloat16)
            sum_v_ref[k0 : k0 + span, :] += jnp.dot(
                probs.astype(jnp.bfloat16), da, preferred_element_type=jnp.float32
            )
            sum_k_ref[k0 : k0 + span, :] += jnp.dot(
                d_scores, query, preferred_element_type=jnp.float32
            )
            d_query.append(
                lax.dot_general(d_scores, keys, TN, preferred_element_type=jnp.float32)
            )
        merged = jnp.where(head_lanes(0, sub), d_query[0], d_query[1])
        out_ref[out_ref.shape[0] - 1, r0 : r0 + sub, :] = (merged * SCALE).astype(jnp.bfloat16)
    count = out_ref.shape[0] // 2
    out_ref[:count] = sum_k_ref[...].astype(jnp.bfloat16).reshape(count, rows, LANES)
    out_ref[count : 2 * count] = sum_v_ref[...].astype(jnp.bfloat16).reshape(count, rows, LANES)


def attention_backward(query, kv, d_attended, attended, logs, bias, first, last, earlier=()):
    rows, span = (query.shape[0], kv.shape[1])
    count = 2 * (span // rows) + 1
    sub = sub_rows(rows)
    pair = pl.BlockSpec((rows, LANES), lambda h: (0, h + first))
    both = pl.BlockSpec((2, span, LANES), lambda h: (0, 0, h + first))
    return pl.pallas_call(
        functools.partial(backward_kernel, sub),
        grid=(last - first,),
        in_specs=[
            pair,
            both,
            pair,
            pair,
            pair,
            pl.BlockSpec((span, rows), lambda h: (0, 0)),
            *[pl.BlockSpec(memory_space=pl.ANY)] * len(earlier),
        ],
        out_specs=pl.BlockSpec((count, rows, LANES), lambda h: (0, 0, h + first)),
        out_shape=jax.ShapeDtypeStruct((count, rows, WIDE), jnp.bfloat16),
        input_output_aliases={6 + n: n for n in range(len(earlier))},
        scratch_shapes=[pltpu.VMEM((span, LANES), jnp.float32)] * 2,
        compiler_params=pltpu.CompilerParams(vmem_limit_bytes=48 << 20),
        cost_estimate=hint(),
    )(query, kv, d_attended, attended, logs, bias, *earlier)


def row_chunks(rows):
    step = 256 if rows % 256 == 0 else rows
    return [slice(n, n + step) for n in range(0, rows, step)]


def lane_block(cols, full):
    return min(full, full_lanes(cols))


def params(megabytes=56):
    return pltpu.CompilerParams(vmem_limit_bytes=megabytes << 20)


def hint():
    return pl.CostEstimate(flops=1 << 20, bytes_accessed=1 << 20, transcendentals=0)


def full_lanes(cols):
    return -(-cols // LANES) * LANES


def store_wide(ref, at, value):
    cols, full = (value.shape[1], ref.shape[-1])
    ref[(*at, slice(0, cols))] = value.astype(ref.dtype)
    if cols < full:
        ref[(*at, slice(cols, full))] = jnp.zeros((value.shape[0], full - cols), ref.dtype)


def assemble_kernel(cols, blocks_ref, qkv_ref, out_ref):
    count, rows, full = blocks_ref.shape
    fill = jnp.zeros((rows, WIDE - D), qkv_ref.dtype)

    def fill_in(write, start, stop, skip, size):
        for j in range(count):
            first, last = (max(start, j * size), min(stop, (j + 1) * size))
            if first < last:
                cut = slice(skip + first - j * size, skip + last - j * size)
                write(slice(first - start, last - start), blocks_ref[j, :, cut])

    for n in range(3):

        def write(cut, value, n=n):
            qkv_ref[n, :, cut] = value

        fill_in(write, n * D, (n + 1) * D, 0, cols)
        qkv_ref[n, :, D:] = fill

    def write_out(cut, value):
        out_ref[:, cut] = value

    fill_in(write_out, 0, D, cols, full - cols)


def assemble(blocks, cols):
    count, rows, full = blocks.shape
    step = 320 if rows % 320 == 0 else rows
    return pl.pallas_call(
        functools.partial(assemble_kernel, cols),
        grid=(rows // step,),
        in_specs=[pl.BlockSpec((count, step, full), lambda n: (0, n, 0))],
        out_specs=[
            pl.BlockSpec((3, step, WIDE), lambda n: (0, n, 0)),
            pl.BlockSpec((step, D), lambda n: (n, 0)),
        ],
        out_shape=[
            jax.ShapeDtypeStruct((3, rows, WIDE), blocks.dtype),
            jax.ShapeDtypeStruct((rows, D), blocks.dtype),
        ],
        compiler_params=params(),
        cost_estimate=hint(),
    )(blocks)


def project_kernel(x_ref, w_ref, bias_ref, *refs):
    out_ref = refs[-1]
    total = jnp.dot(x_ref[...], w_ref[0], preferred_element_type=jnp.float32)
    out_ref[0] = (total + bias_ref[0]).astype(out_ref.dtype)


def project_own_kernel(x_ref, w_ref, bias_ref, q_ref, kv_ref):
    total = jnp.dot(x_ref[...], w_ref[0], preferred_element_type=jnp.float32)
    total = (total + bias_ref[0]).astype(q_ref.dtype)

    @pl.when(pl.program_id(0) == 0)
    def _():
        q_ref[...] = total

    @pl.when(pl.program_id(0) > 0)
    def _():
        kv_ref[0] = total


def project_own(x, weights, bias, reach):
    rows, depth = x.shape
    full = weights.shape[2]
    return pl.pallas_call(
        project_own_kernel,
        grid=(3,),
        in_specs=[
            pl.BlockSpec((rows, depth), lambda t: (0, 0)),
            pl.BlockSpec((1, depth, full), lambda t: (t, 0, 0)),
            pl.BlockSpec((1, 1, full), lambda t: (t, 0, 0)),
        ],
        out_specs=[
            pl.BlockSpec((rows, full), lambda t: (0, 0)),
            pl.BlockSpec((1, rows, full), lambda t: (jnp.maximum(t - 1, 0), reach, 0)),
        ],
        out_shape=[
            jax.ShapeDtypeStruct((rows, full), jnp.bfloat16),
            jax.ShapeDtypeStruct((2, (reach + 1) * rows, full), jnp.bfloat16),
        ],
        compiler_params=params(),
        cost_estimate=hint(),
    )(x, weights, bias[:, None, :])


def project_earlier(x, weights, bias, kv, at):
    rows, depth = x.shape
    full = weights.shape[2]
    return pl.pallas_call(
        project_kernel,
        grid=(2,),
        in_specs=[
            pl.BlockSpec((rows, depth), lambda p: (0, 0)),
            pl.BlockSpec((1, depth, full), lambda p: (p + 1, 0, 0)),
            pl.BlockSpec((1, 1, full), lambda p: (p + 1, 0, 0)),
            pl.BlockSpec(memory_space=pl.ANY),
        ],
        out_specs=pl.BlockSpec((1, rows, full), lambda p: (p, at, 0)),
        out_shape=jax.ShapeDtypeStruct(kv.shape, kv.dtype),
        input_output_aliases={3: 0},
        compiler_params=params(),
        cost_estimate=hint(),
    )(x, weights, bias[:, None, :], kv)


def norm_back_kernel(own_ref, got_ref, normal_ref, inverse_ref, gain_ref, dy_ref, *outs):
    wide_ref, low_ref, sums_ref = outs
    cols = own_ref.shape[1]
    grad = own_ref[...] + got_ref[:, :cols].astype(jnp.float32)
    normal = normal_ref[...]
    product = grad * normal
    scaled = grad * gain_ref[...]
    first = jnp.mean(scaled, axis=1, keepdims=True)
    second = jnp.mean(scaled * normal, axis=1, keepdims=True)
    out = dy_ref[:, :cols].astype(jnp.float32) + inverse_ref[...] * (
        scaled - first - normal * second
    )
    rounded = out.astype(jnp.bfloat16)
    wide_ref[...] = out
    store_wide(low_ref, (slice(None),), rounded)
    parts = [product, grad, rounded.astype(jnp.float32)]
    sums = jnp.concatenate([jnp.sum(part, axis=0, keepdims=True) for part in parts], axis=0)

    @pl.when(pl.program_id(0) == 0)
    def _():
        sums_ref[...] = sums

    @pl.when(pl.program_id(0) > 0)
    def _():
        sums_ref[...] += sums


def norm_back(own, got, normal, inverse, gain, dy):
    rows, cols = own.shape
    step = 128 if rows % 128 == 0 else rows
    block = lambda size: pl.BlockSpec((step, size), lambda n: (n, 0))
    return pl.pallas_call(
        norm_back_kernel,
        grid=(rows // step,),
        in_specs=[
            block(cols),
            block(got.shape[1]),
            block(cols),
            block(1),
            pl.BlockSpec((1, cols), lambda n: (0, 0)),
            block(dy.shape[1]),
        ],
        out_specs=[block(cols), block(WIDE), pl.BlockSpec((3, cols), lambda n: (0, 0))],
        out_shape=[
            jax.ShapeDtypeStruct((rows, cols), jnp.float32),
            jax.ShapeDtypeStruct((rows, WIDE), jnp.bfloat16),
            jax.ShapeDtypeStruct((3, cols), jnp.float32),
        ],
        compiler_params=params(),
        cost_estimate=hint(),
    )(own, got, normal, inverse, gain[None], dy)


def unit_of(w_ref, cols):
    parts, _, rows, lanes = w_ref.shape
    return w_ref[:, 0].reshape(parts * rows, lanes)[:, :cols]


def unit_block(weights, cols, lane):
    parts, _, rows, full = weights.shape
    return pl.BlockSpec((parts, 1, rows, lane_block(cols, full)), lambda b: (0, b, 0, lane))


def ffn_kernel(x_ref, dy_ref, fc_ref, proj_ref, bias_ref, *refs):
    active_ref, d_hidden_ref, sum_ref, out_ref, total_ref = refs[-5:]
    step = pl.program_id(0)
    cols = bias_ref.shape[2]
    first, second = (0.7978845608028654, 0.044715)
    weight = unit_of(fc_ref, cols)
    depth = weight.shape[0]
    u = jnp.dot(x_ref[:, :depth], weight, preferred_element_type=jnp.float32) + bias_ref[0]
    square = u * u
    t = jnp.tanh(first * u * (1.0 + second * square))
    half = 0.5 * (1.0 + t)
    store_wide(active_ref, (0, slice(None)), u * half)
    slope = half + (0.5 * first) * u * (1.0 - t * t) * (1.0 + (3.0 * second) * square)
    d_active = jnp.dot(
        dy_ref[:, :depth], unit_of(proj_ref, cols), preferred_element_type=jnp.float32
    )
    d_hidden = (d_active * slope).astype(jnp.bfloat16)
    store_wide(d_hidden_ref, (0, slice(None)), d_hidden)
    sum_ref[0] = jnp.sum(d_hidden.astype(jnp.float32), axis=0, keepdims=True)
    part = lax.dot_general(d_hidden, weight, NT, preferred_element_type=jnp.float32)

    @pl.when(step == 0)
    def _():
        total_ref[...] = part

    @pl.when(step > 0)
    def _():
        total_ref[...] += part

    @pl.when(step == pl.num_programs(0) - 1)
    def _():
        store_wide(out_ref, (slice(None),), total_ref[...])


def feed_forward(x, dy, fc, proj, lane, bias, part, kind, earlier=()):
    count, cols = bias.shape
    rows = x.shape[0]
    lanes = full_lanes(cols)
    out_cols = WIDE if kind == jnp.bfloat16 else D
    mine = pl.BlockSpec((1, rows, lanes), lambda b: (b, part, 0))
    units = jax.ShapeDtypeStruct((count, 2 * rows, lanes), jnp.bfloat16)
    return pl.pallas_call(
        ffn_kernel,
        grid=(count,),
        in_specs=[
            pl.BlockSpec(x.shape, lambda b: (0, 0)),
            pl.BlockSpec(dy.shape, lambda b: (0, 0)),
            unit_block(fc, cols, 0),
            unit_block(proj, cols, lane),
            pl.BlockSpec((1, 1, cols), lambda b: (b, 0, 0)),
            *[pl.BlockSpec(memory_space=pl.ANY)] * len(earlier),
        ],
        out_specs=[
            mine,
            mine,
            pl.BlockSpec((1, 1, cols), lambda b: (b, 0, 0)),
            pl.BlockSpec((rows, out_cols), lambda b: (0, 0)),
        ],
        out_shape=[
            units,
            units,
            jax.ShapeDtypeStruct((count, 1, cols), jnp.float32),
            jax.ShapeDtypeStruct((rows, out_cols), kind),
        ],
        input_output_aliases={5 + n: n for n in range(len(earlier))},
        scratch_shapes=[pltpu.VMEM((rows, D), jnp.float32)],
        compiler_params=params(),
        cost_estimate=hint(),
    )(x, dy, fc, proj, bias[:, None, :], *earlier)


def back_kernel(cols, x_ref, w_ref, out_ref, sum_ref):
    step = pl.program_id(0)
    part = lax.dot_general(
        x_ref[0][:, :cols], unit_of(w_ref, cols), NT, preferred_element_type=jnp.float32
    )

    @pl.when(step == 0)
    def _():
        sum_ref[...] = part

    @pl.when(step > 0)
    def _():
        sum_ref[...] += part

    @pl.when(step == pl.num_programs(0) - 1)
    def _():
        store_wide(out_ref, (slice(None),), sum_ref[...])


def ffn_back(x, weights, cols, lane, part, rows, kind):
    count = x.shape[0]
    width = weights.shape[0] * weights.shape[2]
    out_cols = WIDE if kind == jnp.bfloat16 else width
    return pl.pallas_call(
        functools.partial(back_kernel, cols),
        grid=(count,),
        in_specs=[
            pl.BlockSpec((1, rows, x.shape[2]), lambda b: (b, part, 0)),
            unit_block(weights, cols, lane),
        ],
        out_specs=pl.BlockSpec((rows, out_cols), lambda b: (0, 0)),
        out_shape=jax.ShapeDtypeStruct((rows, out_cols), kind),
        scratch_shapes=[pltpu.VMEM((rows, width), jnp.float32)],
        compiler_params=params(),
        cost_estimate=hint(),
    )(x, weights)


def index_list(parts):
    return jnp.stack([jnp.asarray(part, jnp.int32) for part in parts])


def split_specs(count, ny, rows, cols):
    half = count // 2
    block = (1, rows, cols)
    specs = [pl.BlockSpec(block, lambda g, a, b: (g, 0, 0))]
    shapes = [jax.ShapeDtypeStruct((count, rows, cols), jnp.bfloat16)]
    for _ in range(1, ny):
        specs.append(pl.BlockSpec(block, lambda g, a, b: (jnp.minimum(g, half - 1), 0, 0)))
        specs.append(pl.BlockSpec(block, lambda g, a, b: (jnp.maximum(g - half, 0), 0, 0)))
        for size in (half, count - half):
            shapes.append(jax.ShapeDtypeStruct((size, rows, cols), jnp.bfloat16))
    return (specs, shapes)


def store_split(outs, q, value):
    value = value.astype(jnp.bfloat16)
    if q == 0:
        outs[0][0] = value
        return
    step = pl.program_id(0)
    half = pl.num_programs(0) // 2

    @pl.when(step < half)
    def _():
        outs[2 * q - 1][0] = value

    @pl.when(step >= half)
    def _():
        outs[2 * q][0] = value


def by_left_kernel(ny, at_r, at_q, left_ref, *refs):
    rights, got_ref, outs = (refs[:ny], refs[ny], refs[ny + 1 :])
    depth = rights[0].shape[1]
    cols = outs[0].shape[2]
    left = left_ref[0]
    for q in range(ny):
        total = jnp.dot(
            left[:, :depth], rights[q][0][:, :cols], preferred_element_type=jnp.float32
        )
        total += jnp.dot(left[:, depth:], got_ref[q][:, :cols], preferred_element_type=jnp.float32)
        store_split(outs, q, total)


def grads_by_left(left, right, got, cols, at_r, at_q):
    count, (_, rows, depth), (_, half, lanes) = (at_r.size, left.shape, right.shape)
    ny = at_q.size
    own = lambda q: pl.BlockSpec((1, half, lanes), lambda r, a, b: (b[q], 0, 0))
    out_specs, out_shape = split_specs(count, ny, rows, cols)
    return pl.pallas_call(
        functools.partial(by_left_kernel, ny),
        grid_spec=pltpu.PrefetchScalarGridSpec(
            num_scalar_prefetch=2,
            grid=(count,),
            in_specs=[
                pl.BlockSpec((1, rows, depth), lambda r, a, b: (a[r], 0, 0)),
                *[own(q) for q in range(ny)],
                pl.BlockSpec((ny, half, lanes), lambda r, a, b: (0, 0, 0)),
            ],
            out_specs=out_specs,
        ),
        out_shape=out_shape,
        compiler_params=params(),
        cost_estimate=hint(),
    )(at_r, at_q, left, *[right] * ny, got)


def by_right_kernel(ny, at_r, at_q, right_ref, right_got_ref, *refs):
    lefts, got_ref, outs = (refs[:ny], refs[ny], refs[ny + 1 :])
    cols = outs[0].shape[2]
    right, right_got = (right_ref[0][:, :cols], right_got_ref[0][:, :cols])
    for q in range(ny):
        total = jnp.dot(lefts[q][0], right, preferred_element_type=jnp.float32)
        total += jnp.dot(got_ref[q], right_got, preferred_element_type=jnp.float32)
        store_split(outs, q, total)


def grads_by_right(left, left_got, right, right_got, cols, at_r, at_q):
    count, (_, rows, depth) = (at_r.size, left.shape)
    ny = at_q.size
    own = lambda q: pl.BlockSpec((1, rows, depth), lambda r, a, b: (b[q], 0, 0))
    moving = pl.BlockSpec((1, depth, right.shape[2]), lambda r, a, b: (a[r], 0, 0))
    out_specs, out_shape = split_specs(count, ny, rows, cols)
    return pl.pallas_call(
        functools.partial(by_right_kernel, ny),
        grid_spec=pltpu.PrefetchScalarGridSpec(
            num_scalar_prefetch=2,
            grid=(count,),
            in_specs=[
                moving,
                moving,
                *[own(q) for q in range(ny)],
                pl.BlockSpec((ny, rows, depth), lambda r, a, b: (0, 0, 0)),
            ],
            out_specs=out_specs,
        ),
        out_shape=out_shape,
        compiler_params=params(),
        cost_estimate=hint(),
    )(at_r, at_q, right, right_got, *[left] * ny, left_got)


def mixed_kernel(cols, count, at_r, at_q, q_ref, q_got_ref, kv_ref, kv_got_ref, *refs):
    lefts, gots, out_ref = (refs[:count], refs[count:-1], refs[-1])
    step = pl.program_id(0)
    nc = out_ref.shape[0]
    _, own, full = q_ref.shape
    for part, at_step in ((2, 0), (1, 1), (0, 2)):

        @pl.when(step == at_step)
        def _(part=part):
            for q, left_ref in enumerate(lefts):
                if part == 0:
                    first, second = (q_ref[0], q_got_ref[0])
                    left, got = (left_ref[0][:, -own:], gots[q][0][:, -own:])
                else:
                    first, second = (kv_ref[...].reshape(-1, full), kv_got_ref[...].reshape(-1, full))
                    left, got = (left_ref[0], gots[q][0])
                total = jnp.dot(left, first, preferred_element_type=jnp.float32)
                total += jnp.dot(got, second, preferred_element_type=jnp.float32)
                total = total.astype(jnp.bfloat16)
                for j in range(nc):
                    start, stop = (max(part * D, j * cols), min((part + 1) * D, (j + 1) * cols))
                    if start < stop:
                        out_ref[at_r[j], q, :, start - j * cols : stop - j * cols] = total[
                            :, start - part * D : stop - part * D
                        ]


def grads_mixed(left, left_got, grads, grads_got, cols, places, at_q, qs):
    nc = places.size
    _, rows, depth = left.shape
    count, own_rows, wide_cols = grads.shape
    reach = count // 2
    own = lambda q: pl.BlockSpec((1, rows, depth), lambda t, a, b: (b[q], 0, 0))
    once = pl.Buffered(1)
    got = lambda q: pl.BlockSpec((1, rows, depth), lambda t, a, b: (q, 0, 0), pipeline_mode=once)
    query_block = pl.BlockSpec(
        (1, own_rows, wide_cols), lambda t, a, b: (count - 1, 0, 0), pipeline_mode=once
    )
    kv_block = pl.BlockSpec(
        (reach, own_rows, wide_cols), lambda t, a, b: (jnp.where(t == 0, 1, 0), 0, 0)
    )
    return pl.pallas_call(
        functools.partial(mixed_kernel, cols, len(qs)),
        grid_spec=pltpu.PrefetchScalarGridSpec(
            num_scalar_prefetch=2,
            grid=(3,),
            in_specs=[
                query_block,
                query_block,
                kv_block,
                kv_block,
                *[own(q) for q in qs],
                *[got(q) for q in qs],
            ],
            out_specs=pl.BlockSpec((nc, len(qs), rows, cols), lambda t, a, b: (0, 0, 0, 0)),
        ),
        out_shape=jax.ShapeDtypeStruct((nc, len(qs), rows, cols), jnp.bfloat16),
        compiler_params=params(60),
        cost_estimate=hint(),
    )(
        places,
        at_q,
        grads,
        grads_got,
        grads,
        grads_got,
        *[left] * len(qs),
        *[left_got] * len(qs),
    )


def sums_kernel(count, halo_refs, own_ref, normal_refs, q_ref, v_ref, out_ref):
    own = own_ref[...]
    parts = [ref[...].astype(jnp.float32) for ref in halo_refs] + [own]
    down = lambda value: jnp.sum(value, axis=0, keepdims=True)
    gain = sum(down(part * ref[...]) for part, ref in zip(parts, normal_refs))
    shift = sum(down(part) for part in parts)
    query = down(q_ref[0].astype(jnp.float32))
    values = sum(down(v_ref[n].astype(jnp.float32)) for n in range(count))
    fill = jnp.zeros((4, own.shape[1]), jnp.float32)
    out_ref[...] = jnp.concatenate([gain, shift, query, values, fill], axis=0)


def column_sums(halo, own, normals, grads):
    rows = own.shape[0]
    reach = len(normals) - 1
    count = reach + 1
    block = lambda n: pl.BlockSpec((rows, LANES), lambda c: (n, c))

    def kernel(*refs):
        halos, refs = (refs[:reach], refs[reach:])
        sums_kernel(count, halos, refs[0], refs[1 : count + 1], *refs[count + 1 :])

    return pl.pallas_call(
        kernel,
        grid=(PAIRS,),
        in_specs=[
            *[block(n) for n in range(reach)],
            block(0),
            *[block(0)] * count,
            pl.BlockSpec((1, rows, LANES), lambda c: (2 * count, 0, c)),
            pl.BlockSpec((count, rows, LANES), lambda c: (1, 0, c)),
        ],
        out_specs=pl.BlockSpec((8, LANES), lambda c: (0, c)),
        out_shape=jax.ShapeDtypeStruct((8, WIDE), jnp.float32),
        compiler_params=params(),
        cost_estimate=hint(),
    )(*[halo] * reach, own, *normals, grads, grads)


def out_kernel(cols, at_r, at_q, right_ref, right_got_ref, *refs):
    *lefts, got_ref, out_ref = refs
    full = out_ref.shape[0] * cols
    right, right_got = (right_ref[:, :full], right_got_ref[:, :full])
    for q, left_ref in enumerate(lefts):
        total = jnp.dot(left_ref[0], right, preferred_element_type=jnp.float32)
        total += jnp.dot(got_ref[q], right_got, preferred_element_type=jnp.float32)
        total = total.astype(jnp.bfloat16)
        for j in range(out_ref.shape[0]):
            out_ref[at_r[j], q] = total[:, j * cols : (j + 1) * cols]


def grads_out(left, left_got, right, right_got, cols, places, at_q):
    nc = places.size
    ny = at_q.size
    _, rows, depth = left.shape
    own = lambda q: pl.BlockSpec((1, rows, depth), lambda t, a, b: (b[q], 0, 0))
    right_block = pl.BlockSpec(right.shape, lambda t, a, b: (0, 0))
    return pl.pallas_call(
        functools.partial(out_kernel, cols),
        grid_spec=pltpu.PrefetchScalarGridSpec(
            num_scalar_prefetch=2,
            grid=(1,),
            in_specs=[
                right_block,
                right_block,
                *[own(q) for q in range(ny)],
                pl.BlockSpec((ny, rows, depth), lambda t, a, b: (0, 0, 0)),
            ],
            out_specs=pl.BlockSpec((nc, ny, rows, cols), lambda t, a, b: (0, 0, 0, 0)),
        ),
        out_shape=jax.ShapeDtypeStruct((nc, ny, rows, cols), jnp.bfloat16),
        compiler_params=params(),
        cost_estimate=hint(),
    )(
        places,
        at_q,
        right,
        right_got,
        *[left] * ny,
        left_got,
    )


def normed_kernel(q_ref, kv_ref, w_ref, own_ref, halo_ref, sum_ref):
    step = pl.program_id(0)
    count, own, _ = kv_ref.shape

    @pl.when(step == 0)
    def _():
        for n in range(count):
            sum_ref[n * own : (n + 1) * own, :] = lax.dot_general(
                kv_ref[n], w_ref[0], NT, preferred_element_type=jnp.float32
            )

    @pl.when(step == 1)
    def _():
        for n in range(count):
            rows = slice(n * own, (n + 1) * own)
            total = sum_ref[rows, :] + lax.dot_general(
                kv_ref[n], w_ref[0], NT, preferred_element_type=jnp.float32
            )
            if n < count - 1:
                store_wide(halo_ref, (rows,), total)
            else:
                sum_ref[rows, :] = total

    @pl.when(step == 2)
    def _():
        own_ref[...] = sum_ref[(count - 1) * own :, :] + lax.dot_general(
            q_ref[0], w_ref[0], NT, preferred_element_type=jnp.float32
        )


def normed_back(grads, weights):
    count, own, wide_cols = grads.shape
    reach = count // 2
    rows = (reach - 1) * own
    return pl.pallas_call(
        normed_kernel,
        grid=(3,),
        in_specs=[
            pl.BlockSpec((1, own, wide_cols), lambda t: (count - 1, 0, 0)),
            pl.BlockSpec((reach, own, wide_cols), lambda t: (jnp.where(t == 0, 1, 0), 0, 0)),
            pl.BlockSpec((1, D, wide_cols), lambda t: (2 - t, 0, 0)),
        ],
        out_specs=[
            pl.BlockSpec((own, D), lambda t: (0, 0)),
            pl.BlockSpec((rows, WIDE), lambda t: (0, 0)),
        ],
        out_shape=[
            jax.ShapeDtypeStruct((own, D), jnp.float32),
            jax.ShapeDtypeStruct((rows, WIDE), jnp.bfloat16),
        ],
        scratch_shapes=[pltpu.VMEM((reach * own, D), jnp.float32)],
        compiler_params=params(),
        cost_estimate=hint(),
    )(grads, grads, weights)


def place():
    nc, nd = (lax.axis_size("ctx"), lax.axis_size("dat"))
    ctx, dat = (lax.axis_index("ctx"), lax.axis_index("dat"))
    return (nc, nd, ctx, dat // 2, dat % 2)


def dat_of(q, other):
    _, nd, _, y, core = place()
    return 2 * ((y + q) % (nd // 2)) + (1 - core if other else core)


def ctx_of(r):
    nc, _, ctx, _, _ = place()
    return (ctx + r) % nc


def swap_core(value):
    return swap_dat(value, 1)


def ny_of():
    return lax.axis_size("dat") // 2


def sum_of(parts):
    total = wide(parts[0])
    for part in parts[1:]:
        total = total + wide(part)
    return total


def steps_of(nc):
    half = nc // 2
    out = [half]
    for n in range(1, half):
        out += [half + n, half - n]
    return [*out, 0]


class WholeSum:
    def __init__(self, blocks, nc):
        self.own, self.others = (blocks[0], blocks[1:])
        self.order = steps_of(nc)
        self.nc = nc
        self.sums = {}

    def y_sends(self, second):
        return [
            (part, functools.partial(roll_y, steps=q + 1))
            for q, part in enumerate(self.others[second::2])
        ]

    def take_y(self, moved, second):
        half = self.nc // 2
        for n, r in enumerate(self.order[half:] if second else self.order[:half]):
            parts = [part[n] for part in moved]
            self.sums[r] = low(sum_of([self.own[half * second + n], *parts]))

    def z_sends(self):
        half = self.nc // 2
        sends = [(self.sums[half], functools.partial(roll_ctx, steps=1))]
        if half + 1 < self.nc:
            sends.append((self.sums[half + 1], functools.partial(roll_ctx, steps=-1)))
        return sends

    def z_next(self, moved):
        half = self.nc // 2
        ahead = moved[0]
        for r in range(half - 1, 0, -1):
            ahead = low(sum_of([self.sums[r], ahead]))
            if r > 1:
                ahead = roll_ctx(ahead, 1)
        back = moved[1] if len(moved) > 1 else None
        for r in range(half + 2, self.nc):
            back = roll_ctx(low(sum_of([self.sums[r], back])), -1)
        self.back = back
        return [(ahead, functools.partial(roll_ctx, steps=1))]

    def total(self, moved):
        parts = [self.sums[0], moved[0]]
        if self.back is not None:
            parts.append(self.back)
        return low(sum_of(parts))


def mixed_places():
    nc, _, ctx, _, _ = place()
    rep = lax.axis_index("rep")
    quarter = nc // 4
    places = []
    for r in range(nc):
        if r == 0:
            places.append(nc - 1)
        elif r % 2 == 0:
            places.append(2 * quarter + r // 2 - 1)
        else:
            places.append(r // 4 + quarter * jnp.where(rep == r % 4 // 2, 1, 0))
    places = index_list(places)
    return index_list([places[(j - ctx) % nc] for j in range(nc)])


class MixedSum:
    def __init__(self, blocks):
        self.blocks = blocks
        self.nc, self.ny = (blocks[0].shape[0], len(blocks))
        self.quarter = self.nc // 4
        self.rep = lax.axis_index("rep")
        self.kept = {}
        self.sums = {}

    def even(self, r):
        return self.nc - 1 if r == 0 else 2 * self.quarter + r // 2 - 1

    def x_sends(self, qs):
        if len(qs) == self.ny:
            return [(jnp.stack([self.blocks[q][: self.quarter] for q in qs], axis=1), swap_rep)]
        return [(self.blocks[q][: self.quarter], swap_rep) for q in qs]

    def take_x(self, moved, qs):
        for n, q in enumerate(qs):
            got = moved[0][:, q] if len(qs) == self.ny else moved[n]
            self.kept[q] = low(sum_of([self.blocks[q][self.quarter : 2 * self.quarter], got]))

    def y_sends(self, steps):
        return [
            (self.blocks[q][self.even(r)], functools.partial(roll_y, steps=q))
            for r in steps
            for q in range(1, self.ny)
        ]

    def take_y(self, moved, steps):
        for n, r in enumerate(steps):
            parts = moved[n * (self.ny - 1) : (n + 1) * (self.ny - 1)]
            self.sums[r] = low(sum_of([self.blocks[0][self.even(r)], *parts]))

    def odd_y_sends(self):
        return [
            (self.kept[q], functools.partial(roll_y, steps=q)) for q in range(1, self.ny)
        ]

    def take_odd_y(self, moved):
        total = low(sum_of([self.kept[0], *moved]))
        for m in range(self.quarter):
            self.sums[4 * m + 1] = total[m]

    def all_y_sends(self):
        return [
            (
                jnp.concatenate([self.blocks[q][2 * self.quarter :], self.kept[q]], axis=0),
                functools.partial(roll_y, steps=q),
            )
            for q in range(1, self.ny)
        ]

    def take_all_y(self, moved):
        evens = self.nc // 2
        own = jnp.concatenate([self.blocks[0][2 * self.quarter :], self.kept[0]], axis=0)
        total = low(sum_of([own, *moved]))
        for n in range(evens):
            self.sums[2 * n + 2 if n < evens - 1 else 0] = total[n]
        for m in range(self.quarter):
            self.sums[4 * m + 1] = total[evens + m]

    def at(self, distance):
        if distance % 2 == 0:
            if 2 * distance == self.nc:
                return self.sums[distance]
            return jnp.where(self.rep == 0, self.sums[distance], self.sums[self.nc - distance])
        if distance % 4 == 1:
            return self.sums[distance]
        return None

    def move(self, value):
        return roll_ctx_by_rep(value, (1, -1))

    def z_sends(self):
        return [(self.at(self.nc - 2), self.move)]

    def z_next(self, moved):
        carried = moved[0]
        for distance in range(self.nc - 3, 0, -1):
            part = self.at(distance)
            carried = carried if part is None else low(sum_of([part, carried]))
            if distance > 1:
                carried = self.move(carried)
        return [(carried, self.move)]

    def total(self, moved):
        return low(sum_of([self.sums[0], moved[0]]))


class SmallSum:
    @staticmethod
    def prepare(parts):
        nc = lax.axis_size("ctx")
        return (jnp.concatenate([part.reshape(nc, -1) for part in parts], axis=1),)

    def __init__(self, value, sizes):
        nc, nd, ctx, _, _ = place()
        self.sizes = [size // nc for size in sizes]
        self.value = value
        self.ctx = ctx
        self.left = []
        bit = nc // 2
        while bit:
            self.left.append(("ctx", bit))
            bit //= 2
        bit = 1
        while bit < nd:
            self.left.append(("dat", bit))
            bit *= 2
        self.left.append(("rep", 1))

    def sends(self):
        axis, bit = self.left[0]
        count = lax.axis_size(axis)
        pairs = [(s, s ^ bit) for s in range(count)]
        if axis != "ctx":
            return [(self.value, lambda value: permute(value, axis, pairs))]
        halves = self.value.reshape(2, bit, -1)
        mine = (self.ctx // bit) % 2
        self.value = pick(halves, mine)
        return [(pick(halves, 1 - mine), lambda value: permute(value, axis, pairs))]

    def take(self, moved):
        self.left.pop(0)
        self.value = self.value + moved[0].reshape(self.value.shape)

    def finish(self):
        while self.left:
            self.take([move(value) for value, move in self.sends()])
        value = self.value.reshape(-1)
        outs, at = ([], 0)
        for size in self.sizes:
            outs.append(value[at : at + size])
            at += size
        return outs


def gather_small(vector):
    nc, _, ctx, _, _ = place()
    out = jnp.zeros((nc,) + vector.shape, vector.dtype)
    for r in range(nc):
        part = roll_ctx(vector, r) if r else vector
        out = lax.dynamic_update_index_in_dim(out, part, (ctx - r) % nc, 0)
    return out


def pad_cols(value):
    return jnp.pad(value, ((0, 0), (0, WIDE - value.shape[1])))


def regroup(units, count):
    have, rows, cols = units.shape
    if have == count:
        return units
    if have > count:
        per = have // count
        return units.reshape(count, per, rows, cols).swapaxes(1, 2).reshape(count, rows, -1)
    per = count // have
    return units.reshape(have, rows, per, cols // per).swapaxes(1, 2).reshape(count, rows, -1)


def regroup_wide(units, cols, count):
    if units.shape[0] == count:
        return units
    value = regroup(units[:, :, :cols], count)
    return jnp.pad(value, ((0, 0), (0, 0), (0, full_lanes(value.shape[2]) - value.shape[2])))


def local(
    tokens,
    segments,
    cotangent,
    ln1_gain,
    ln1_bias,
    w_qkv,
    b_qv,
    w_out,
    b_out,
    ln2_gain,
    ln2_bias,
    w_fc,
    b_fc,
    w_proj,
    b_proj,
):
    nc, nd, ctx, y, core = place()
    rep = lax.axis_index("rep")
    ff = w_fc.shape[1] * nc
    row_count = tokens.shape[1]
    reach_count = -(-WINDOW // row_count)
    reach_rows = reach_count * row_count

    blocks = max(nc, nd)
    width = ff // blocks // 2
    per_b, per_c = (blocks // nc, blocks // nd)
    qkv_cols, out_cols = (w_qkv.shape[1], w_out.shape[1])
    fc_cols = per_b * width

    small_all = gather_small(
        low(jnp.concatenate([ln1_gain, ln1_bias, b_qv, b_out, ln2_gain, ln2_bias, b_fc, b_proj]))
    )
    smalls, at = ([], 0)
    for part in (ln1_gain, ln1_bias, b_qv, b_out, ln2_gain, ln2_bias, b_fc, b_proj):
        size = part.shape[0]
        smalls.append(wide(small_all[:, at : at + size].reshape(-1)))
        at += size
    gain_one, shift_one, bias_qv, bias_out, gain_two, shift_two, bias_fc, bias_proj = smalls
    bias_half = bias_fc.reshape(blocks, 2, width)
    bias_half = lax.dynamic_index_in_dim(bias_half, rep, axis=1, keepdims=False)

    inputs = wide(tokens[0])
    d_ffn = cotangent[0]
    d_ffn_wide = pad_cols(d_ffn)
    d_ffn_got = swap_rep(d_ffn_wide)
    d_ffn_pair = jnp.concatenate([d_ffn_wide, d_ffn_got], axis=0)
    d_ffn_quad = jnp.concatenate([d_ffn_pair, swap_core(d_ffn_pair)], axis=0)[:, :D]
    d_ffn_quad = d_ffn_quad.T.reshape(nc, D // nc, -1)
    order = steps_of(nc)
    at_ctx = index_list([ctx_of(r) for r in order])
    at_own = index_list([dat_of(q, False) for q in range(nd // 2)])
    at_other = [dat_of(q, True) for q in range(nd // 2)]
    places = mixed_places()
    at_ctx, at_own, places, d_ffn_quad = lax.optimization_barrier(
        (at_ctx, at_own, places, d_ffn_quad)
    )

    def from_other_core(stacked):
        return swap_core(jnp.stack([pick(stacked, at) for at in at_other]))

    shard_a = jnp.concatenate([low(w_qkv), low(w_out)], axis=1)
    full_a = lax.all_gather(shard_a, ("ctx", "dat"), axis=0, tiled=True)
    full_a = full_a.reshape(nc, D, qkv_cols + out_cols)
    normed_own, normal_own, inverse_own = norm_forward(inputs, gain_one, shift_one)
    normed_own = low(normed_own)
    full_a = after(full_a, normed_own, d_ffn_quad)

    segment_row = segments[0]
    padded_segment = jnp.concatenate([jnp.full((reach_rows,), -1, jnp.int32), segment_row])
    key_segment = lax.dynamic_slice_in_dim(padded_segment, ctx * row_count, reach_rows + row_count)
    query_segment = lax.dynamic_slice_in_dim(segment_row, ctx * row_count, row_count)
    query_position = reach_rows + jnp.arange(row_count, dtype=jnp.int32)
    key_position = jnp.arange(reach_rows + row_count, dtype=jnp.int32)

    def mask(at_query, at_key):
        visible = (
            (at_query(query_segment) == at_key(key_segment))
            & (at_key(key_position) <= at_query(query_position))
            & (at_key(key_position) > at_query(query_position) - WINDOW)
        )
        return jnp.where(visible, 0.0, MASKED)

    as_column, as_row = (lambda v: v[:, None], lambda v: v[None, :])
    bias_forward, bias_back = (mask(as_column, as_row), mask(as_row, as_column))
    left_own = normed_own.T

    fc_half = lax.dynamic_index_in_dim(
        low(w_fc).reshape(-1, per_b, 2, width), rep, axis=2, keepdims=False
    ).reshape(-1, fc_cols)
    proj_half = lax.dynamic_index_in_dim(
        low(w_proj).reshape(per_c, 2, width, -1), rep, axis=1, keepdims=False
    ).reshape(per_c * width, -1)
    proj_half = proj_half.T
    shard_b = None
    if nc == nd:
        fill = jnp.zeros((fc_half.shape[0], full_lanes(width) - width), jnp.bfloat16)
        shard_b = jnp.concatenate([fc_half, fill, proj_half, fill], axis=1)
        full_a = after(full_a, shard_b)
    tokens_wide, normed_own, full_a, bias_forward, bias_back, left_own = lax.optimization_barrier(
        (pad_cols(tokens[0]), normed_own, full_a, bias_forward, bias_back, left_own)
    )
    bias_qkv = pad_cols(jnp.stack([bias_qv[:D], jnp.zeros((D,), jnp.float32), bias_qv[D:]]))

    def first_weights(weights, x):
        weights_qkv, weight_out = assemble(weights, qkv_cols)
        return (weights_qkv, weight_out, *project_own(x, weights_qkv, bias_qkv, reach_count))

    (weights_qkv, weight_out, query, kv), (halo,) = stage(
        first_weights,
        [full_a, normed_own],
        [(tokens_wide, functools.partial(shift_ctx, steps=1, first=0, last=nc - 1))],
    )
    normed_halo, normal_halo = ([], [])
    for n in range(reach_count):

        def next_block(tokens_of, kv, n=n):
            normed, normal, _ = norm_forward(wide(tokens_of[:, :D]), gain_one, shift_one)
            normed = low(normed)
            at = reach_count - 1 - n
            return (normed, normal, project_earlier(normed, weights_qkv, bias_qkv, kv, at))

        more = n + 1 < reach_count
        (normed, normal, kv), moved = stage(
            next_block,
            [halo, kv],
            [(halo, functools.partial(shift_ctx, steps=1, first=n + 1, last=nc - 1))] * more,
        )
        normed_halo.insert(0, normed)
        normal_halo.insert(0, normal)
        halo = moved[0] if more else halo
    normed_earlier = jnp.concatenate(normed_halo, axis=0)

    if nc == nd:
        shard_b = after(shard_b, small_all, halo)
        gathered = [lax.all_gather(shard_b, ("ctx", "dat"), axis=0, tiled=True)]
    else:
        gathered = [
            lax.all_gather(fc_half, ("ctx", "dat"), axis=0, tiled=True),
            lax.all_gather(proj_half, ("dat", "ctx"), axis=0, tiled=True),
        ]

    attended, attended_wide, logs = attention_forward(query, kv, bias_forward)
    resid = inputs + dot(attended[:, :D], weight_out) + bias_out
    normed_two, normal_two, inverse_two = norm_forward(resid, gain_two, shift_two)
    normed_two = pad_cols(low(normed_two))

    left_one = jnp.concatenate([normed_earlier.T, left_own], axis=1).reshape(nd, D // nd, -1)
    left_out = attended[:, :D].T.reshape(nd, D // nd, -1)
    left_one_got = from_other_core(left_one)
    left_out_got = from_other_core(left_out)
    gathered = [after(part, normed_two, left_one_got, left_out_got) for part in gathered]
    if nc == nd:
        units_proj = gathered[0].reshape(nc, nd, D // nd, -1)
        units_fc = gathered[0].reshape(1, nc, D, -1)
        lane_proj = 1
    else:
        units_fc = regroup(gathered[0].reshape(nc, D, -1), blocks)[None]
        units_proj = regroup(gathered[1].reshape(nd, D, -1), blocks)[None]
        lane_proj = 0

    (active, d_hidden, sums_own, d_normed_own), (normed_two_got,) = stage(
        lambda x: feed_forward(
            x, d_ffn_wide, units_fc, units_proj, lane_proj, bias_half, 0, jnp.float32
        ),
        [normed_two],
        [(normed_two, swap_rep)],
    )
    active, d_hidden, sums_theirs, d_theirs = feed_forward(
        normed_two_got,
        d_ffn_got,
        units_fc,
        units_proj,
        lane_proj,
        bias_half,
        1,
        jnp.bfloat16,
        (active, d_hidden),
    )
    grad_bias_fc = sums_own + sums_theirs
    active_dat = regroup_wide(active, width, nd)
    d_hidden_ctx = regroup_wide(d_hidden, width, nc)
    ny = ny_of()

    def other(stacked):
        return jnp.stack([pick(stacked, at) for at in at_other])

    def turn(own, got):
        return (jnp.concatenate([own, got], axis=0)[:, :D].T.reshape(nd, D // nd, -1),)

    cut = row_count // 2
    (left_two,), (active_got,) = stage(
        turn,
        [normed_two, normed_two_got],
        [
            (other(active_dat), swap_core),
        ],
    )
    blocks_proj, (d_hidden_got, left_two_got, got_first) = stage(
        lambda x: grads_by_left(d_ffn_quad, x, active_got, per_c * width, at_ctx, at_own),
        [active_dat],
        [
            (d_hidden_ctx, swap_core),
            (other(left_two), swap_core),
            (d_theirs[:cut], swap_rep),
        ],
    )
    proj = WholeSum(blocks_proj, nc)

    def second_blocks(x, active):
        blocks_fc = grads_by_right(
            left_two, left_two_got, x, d_hidden_got, fc_cols, at_ctx, at_own
        )
        active = after(active, blocks_fc[0])
        return (
            ffn_back(active, units_proj, width, lane_proj, 1, row_count, jnp.bfloat16),
            *blocks_fc,
        )

    (ffn_theirs, *blocks_fc), (got_second, *moved) = stage(
        second_blocks,
        [d_hidden_ctx, active],
        [(d_theirs[cut:], swap_rep), *proj.y_sends(0)],
    )
    proj.take_y(moved, 0)
    fc = WholeSum(blocks_fc, nc)
    d_normed_got = jnp.concatenate([got_first, got_second], axis=0)

    def to_branch(x, got):
        d_resid, d_branch, sums = norm_back(
            x, got, normal_two, inverse_two, gain_two, d_ffn_wide
        )
        d_branch_got = swap_core(d_branch)
        d_attended = ffn_back(
            d_branch[None], weight_out[None, None], D, 0, 0, row_count, jnp.bfloat16
        )
        blocks_out = grads_out(
            left_out,
            left_out_got,
            after(d_branch, d_attended),
            d_branch_got,
            out_cols,
            places,
            at_own,
        )
        return (d_resid, sums, d_attended, blocks_out)

    (d_resid, sums_two, d_attended, blocks_out), moved = stage(
        to_branch,
        [d_normed_own, d_normed_got],
        [*proj.y_sends(1), *proj.z_sends()],
    )
    proj.take_y(moved[: ny - 1], 1)
    proj_next = proj.z_next(moved[ny - 1 :])
    out = MixedSum([blocks_out[:, q] for q in range(ny)])

    middle = PAIRS // 2
    (grads,), moved = stage(
        lambda x: (
            attention_backward(query, kv, x, attended_wide, logs, bias_back, 0, middle),
        ),
        [d_attended],
        [*fc.y_sends(0), *proj_next, *out.x_sends(range(ny))],
    )
    fc.take_y(moved[: ny - 1], 0)
    proj_total = proj.total(moved[ny - 1 : ny])
    out.take_x(moved[ny:], range(ny))
    (grads,), moved = stage(
        lambda x, done: (
            attention_backward(
                query, kv, x, attended_wide, logs, bias_back, middle, PAIRS, [done]
            ),
        ),
        [d_attended, grads],
        [*fc.y_sends(1), *fc.z_sends(), (proj_total, swap_rep), (ffn_theirs[:cut], swap_rep)],
    )
    fc.take_y(moved[: ny - 1], 1)
    *moved, proj_got, ffn_first = moved[ny - 1 :]
    fc_next = fc.z_next(moved)

    (d_normed_own, d_normed_halo), (grads_got, ffn_second, *moved) = stage(
        lambda x: normed_back(x, weights_qkv),
        [grads],
        [(grads, swap_core), (ffn_theirs[cut:], swap_rep), *fc_next, *out.all_y_sends()],
    )
    fc_total = fc.total(moved[:1])
    out.take_all_y(moved[1:])
    returned = d_normed_halo[:row_count]
    for n in range(1, reach_count - 1):
        returned = shift_ctx(returned, -1, reach_count + 1 - n, nc)
        returned = low(sum_of([returned, d_normed_halo[n * row_count : (n + 1) * row_count]]))
    back_one = functools.partial(shift_ctx, steps=-1, first=min(2, reach_count), last=nc)
    back_two = functools.partial(shift_ctx, steps=-1, first=1, last=nc)
    again = reach_count > 1
    others = list(range(1, ny))
    evens = list(range(2, nc, 2))

    def blocks_of(qs):
        return lambda x: [
            grads_mixed(left_one, left_one_got, x, grads_got, qkv_cols, places, at_own, qs)
        ]

    (blocks_others,), (back_first, fc_got, *moved) = stage(
        blocks_of(others),
        [grads],
        [(returned[:cut], back_one), (fc_total, swap_rep), *out.z_sends()],
    )
    out_next = out.z_next(moved)
    parts = [blocks_others[:, n] for n in range(ny - 1)]
    qkv = MixedSum([parts[0], *parts])
    (blocks_first,), moved = stage(
        blocks_of([0]),
        [after(grads, blocks_others)],
        [
            *qkv.x_sends(others),
            *qkv.y_sends(evens),
            (returned[cut:], back_one),
            *out_next,
        ],
    )
    qkv.blocks[0] = blocks_first[:, 0]
    qkv.take_x(moved[: ny - 1], others)
    qkv.take_y(moved[ny - 1 : -2], evens)
    out_total = out.total(moved[-1:])
    back = [back_first, moved[-2]]

    grad_gain_two, grad_shift_two, grad_bias_out = sums_two
    normals = [*normal_halo, normal_own]

    def vectors(halo, own_grad, grads, d_ffn, bias_fc_sum, *back):
        sums_one = column_sums(halo, own_grad, normals, grads)
        bias_proj_sum = jnp.sum(wide(d_ffn), axis=0)
        halves = [jnp.where(rep == n, bias_fc_sum, 0.0) for n in range(2)]
        small_parts = [grad_bias_out, grad_gain_two, grad_shift_two]
        small_parts += [jnp.concatenate(halves, axis=1).reshape(-1), bias_proj_sum]
        small_parts += [sums_one[0, :D], sums_one[1, :D], sums_one[2:4, :D].reshape(-1)]
        if again:
            last_halo = halo[reach_rows - row_count :]
            pairs = zip(back, (last_halo[:cut], last_halo[cut:]))
            back = [low(sum_of(pair)) for pair in pairs]
        return (*SmallSum.prepare(small_parts), *back)

    bias_fc_sum = grad_bias_fc.reshape(blocks, 1, width)
    (small_value, *back), moved = stage(
        vectors,
        [d_normed_halo, d_normed_own, grads, d_ffn, bias_fc_sum, *back],
        [*qkv.x_sends([0]), *qkv.odd_y_sends(), *qkv.z_sends()],
    )
    qkv.take_x(moved[:1], [0])
    qkv.take_odd_y(moved[1:ny])
    qkv_next = qkv.z_next(moved[ny:])
    small = SmallSum(small_value, [D, D, D, ff, D, D, D, 2 * D])

    (ffn_own,), moved = stage(
        lambda x: (ffn_back(x, units_proj, width, lane_proj, 0, row_count, jnp.float32),),
        [active],
        [
            *qkv_next,
            *qkv.y_sends([0]),
            (out_total, swap_rep),
            *small.sends(),
            *[(back[0], back_two)] * again,
        ],
    )
    if again:
        back[0] = moved.pop()
    qkv.take_y(moved[1:ny], [0])
    qkv_total = qkv.total(moved[:1])
    out_got = moved[ny]
    small.take(moved[ny + 1 :])

    def input_part(rows, returned):
        grad = d_normed_own[rows] + wide(returned[:, :D])
        back_grad = norm_backward(grad, gain_one, normal_own[rows], inverse_own[rows])
        return low(d_resid[rows] + back_grad)

    def both_halves(half, got):
        return (jnp.where(rep == 0, half, got), jnp.where(rep == 0, got, half))

    def last(total, got, returned, fc_half, fc_got, proj_half, proj_got, resid, own, top, rest):
        halves = both_halves(fc_half, fc_got)
        if per_b > 1:
            rows = fc_half.shape[0]
            halves = [part.reshape(rows, per_b, 1, width) for part in halves]
            halves = [jnp.concatenate(halves, axis=2).reshape(rows, -1)]
        grad_fc = wide(jnp.concatenate(halves, axis=1))
        halves = both_halves(proj_half.T, proj_got.T)
        if per_c > 1:
            halves = [part.reshape(per_c, 1, width, -1) for part in halves]
            halves = [jnp.concatenate(halves, axis=1).reshape(2 * per_c * width, -1)]
        grad_proj = wide(jnp.concatenate(halves, axis=0))
        result = jnp.concatenate([top, rest], axis=0)
        layer_out = low(resid + own + wide(result[:, :D]) + bias_proj)
        part = input_part(slice(0, cut), returned)
        return (wide(total) + wide(got), part, grad_fc, grad_proj, layer_out)

    (grad_out_weight, input_first, grad_fc, grad_proj, layer_out), (qkv_got, *moved) = stage(
        last,
        [
            out_total,
            out_got,
            back[0],
            fc_total,
            fc_got,
            proj_total,
            proj_got,
            resid,
            ffn_own,
            ffn_first,
            ffn_second,
        ],
        [(qkv_total, swap_rep), *[(back[1], back_two)] * again, *small.sends()],
    )
    if again:
        back[1] = moved[0]
    small.take(moved[-1:])
    input_grad = jnp.concatenate([input_first, input_part(slice(cut, None), back[1])], axis=0)
    grad_qkv = wide(qkv_total) + wide(qkv_got)
    small_out = small.finish()

    grad_bias_out, grad_gain_two, grad_shift_two, grad_bias_fc, grad_bias_proj = small_out[:5]
    grad_gain_one, grad_shift_one, grad_bias_qv = small_out[5:]

    return (
        layer_out[None],
        input_grad[None],
        grad_gain_one,
        grad_shift_one,
        grad_qkv,
        grad_bias_qv,
        grad_out_weight,
        grad_bias_out,
        grad_gain_two,
        grad_shift_two,
        grad_fc,
        grad_bias_fc,
        grad_proj,
        grad_bias_proj,
    )


def solution(mesh):
    in_specs = (
        P(("rep", "dat"), "ctx", None),
        P(("rep", "dat"), None),
        P(("rep", "dat"), "ctx", None),
        P("ctx"),
        P("ctx"),
        P("dat", "ctx"),
        P("ctx"),
        P("dat", "ctx"),
        P("ctx"),
        P("ctx"),
        P("ctx"),
        P("dat", "ctx"),
        P("ctx"),
        P("dat", "ctx"),
        P("ctx"),
    )
    out_specs = (
        P(("rep", "dat"), "ctx", None),
        P(("rep", "dat"), "ctx", None),
        P("ctx"),
        P("ctx"),
        P("dat", "ctx"),
        P("ctx"),
        P("dat", "ctx"),
        P("ctx"),
        P("ctx"),
        P("ctx"),
        P("dat", "ctx"),
        P("ctx"),
        P("dat", "ctx"),
        P("ctx"),
    )
    return jax.shard_map(local, mesh=mesh, in_specs=in_specs, out_specs=out_specs, check_vma=False)
```

```python
import functools

import jax
import jax.numpy as jnp
from jax import lax
from jax.experimental import pallas as pl
from jax.experimental.pallas import tpu as pltpu
from jax.sharding import PartitionSpec as P

D = 1600
HEADS = 25
HEAD_DIM = 64
WINDOW = 1024


EPS = 1e-05
MASKED = -1e30
LANES = 128
PAIRS = -(-HEADS // 2)
WIDE = PAIRS * LANES
SCALE = HEAD_DIM ** (-0.5)
NT = (((1,), (1,)), ((), ()))
TN = (((0,), (0,)), ((), ()))


def permute(value, axes, pairs):
    return lax.ppermute(value, axes, pairs)


def roll_ctx(value, steps):
    count = lax.axis_size("ctx")
    return permute(value, "ctx", [(s, (s + steps) % count) for s in range(count)])


def shift_ctx(value, steps, first, last):
    return permute(value, "ctx", [(s, s + steps) for s in range(first, last)])


def roll_ctx_by_rep(value, steps):
    count = lax.axis_size("ctx")
    pairs = [
        (rep * count + s, rep * count + (s + steps[rep]) % count)
        for rep in range(len(steps))
        for s in range(count)
    ]
    return permute(value, ("rep", "ctx"), pairs)


def roll_y(value, steps):
    count = lax.axis_size("dat")
    return permute(value, "dat", [(s, (s + 2 * steps) % count) for s in range(count)])


def swap_dat(value, bit):
    count = lax.axis_size("dat")
    return permute(value, "dat", [(s, s ^ bit) for s in range(count)])


def swap_rep(value):
    return permute(value, "rep", [(0, 1), (1, 0)])


def norm_forward(values, gain, shift):
    average = jnp.mean(values, axis=-1, keepdims=True)
    centred = values - average
    variance = jnp.mean(centred * centred, axis=-1, keepdims=True)
    inverse = lax.rsqrt(variance + EPS)
    normal = centred * inverse
    return (normal * gain + shift, normal, inverse)


def norm_backward(grad_out, gain, normal, inverse):
    scaled = grad_out * gain
    first = jnp.mean(scaled, axis=-1, keepdims=True)
    second = jnp.mean(scaled * normal, axis=-1, keepdims=True)
    return inverse * (scaled - first - normal * second)


def dot(left, right):
    return jnp.dot(left, right, preferred_element_type=jnp.float32)


def dot_cols(left, right):
    return lax.dot_general(left, right, NT, preferred_element_type=jnp.float32)


def low(value):
    return value.astype(jnp.bfloat16)


def wide(value):
    return value.astype(jnp.float32)


def pick(stacked, index):
    return lax.dynamic_index_in_dim(stacked, index, axis=0, keepdims=False)


def stage(run, ready, sends):
    count = len(ready)
    flat = lax.optimization_barrier((*ready, *[value for value, _ in sends]))
    outs = run(*flat[:count])
    moved = [move(value) for (_, move), value in zip(sends, flat[count:])]
    flat = lax.optimization_barrier((*outs, *moved))
    return (list(flat[: len(outs)]), list(flat[len(outs) :]))


def after(value, *others):
    return lax.optimization_barrier((value, *others))[0]


def head_lanes(half, rows):
    lane = lax.broadcasted_iota(jnp.int32, (rows, LANES), 1)
    return (lane < HEAD_DIM) if half == 0 else (lane >= HEAD_DIM)


def forward_kernel(sub, q_ref, kv_ref, bias_ref, out_ref, out32_ref, log_ref):
    rows = q_ref.shape[0]
    span = WINDOW + sub
    reach = kv_ref.shape[1] - rows
    for n in range(rows // sub):
        r0 = n * sub
        k0 = reach - WINDOW + r0
        keys = kv_ref[0, k0 : k0 + span, :]
        values = kv_ref[1, k0 : k0 + span, :]
        bias = bias_ref[r0 : r0 + sub, k0 : k0 + span]
        parts = []
        for half in range(2):
            query = jnp.where(
                head_lanes(half, sub), q_ref[r0 : r0 + sub, :] * jnp.bfloat16(SCALE), jnp.bfloat16(0)
            )
            scores = lax.dot_general(query, keys, NT, preferred_element_type=jnp.float32) + bias
            top = jnp.max(scores, axis=1, keepdims=True)
            weights = jnp.exp(scores - top)
            total = jnp.sum(weights, axis=1, keepdims=True)
            summed = jnp.dot(
                weights.astype(jnp.bfloat16), values, preferred_element_type=jnp.float32
            )
            parts.append((summed / total, top + jnp.log(total)))
        first = head_lanes(0, sub)
        out = jnp.where(first, parts[0][0], parts[1][0])
        out_ref[r0 : r0 + sub, :] = out.astype(jnp.bfloat16)
        out32_ref[r0 : r0 + sub, :] = out
        log_ref[r0 : r0 + sub, :] = jnp.where(first, parts[0][1], parts[1][1])


def sub_rows(rows):
    return 256 if rows % 256 == 0 else rows


def pair_block(rows):
    return pl.BlockSpec((rows, LANES), lambda h: (0, h))


def kv_block(rows):
    return pl.BlockSpec((2, rows, LANES), lambda h: (0, 0, h))


def attention_forward(query, kv, bias):
    rows, span = (query.shape[0], kv.shape[1])
    sub = sub_rows(rows)
    return pl.pallas_call(
        functools.partial(forward_kernel, sub),
        grid=(PAIRS,),
        in_specs=[
            pair_block(rows),
            kv_block(span),
            pl.BlockSpec((rows, span), lambda h: (0, 0)),
        ],
        out_specs=[pair_block(rows)] * 3,
        out_shape=[
            jax.ShapeDtypeStruct((rows, WIDE), kind)
            for kind in (jnp.bfloat16, jnp.float32, jnp.float32)
        ],
        compiler_params=pltpu.CompilerParams(vmem_limit_bytes=48 << 20),
        cost_estimate=hint(),
    )(query, kv, bias)


def backward_kernel(
    sub,
    q_ref,
    kv_ref,
    da_ref,
    attended_ref,
    log_ref,
    bias_ref,
    *refs,
):
    out_ref, sum_k_ref, sum_v_ref = refs[-3:]
    rows = q_ref.shape[0]
    span = WINDOW + sub
    reach = kv_ref.shape[1] - rows
    sum_k_ref[...] = jnp.zeros_like(sum_k_ref)
    sum_v_ref[...] = jnp.zeros_like(sum_v_ref)
    for n in range(rows // sub):
        r0 = n * sub
        k0 = reach - WINDOW + r0
        all_da = da_ref[r0 : r0 + sub, :]
        product = jnp.transpose(all_da.astype(jnp.float32) * attended_ref[r0 : r0 + sub, :])
        logs = jnp.transpose(log_ref[r0 : r0 + sub, :])
        all_query = q_ref[r0 : r0 + sub, :] * jnp.bfloat16(SCALE)
        keys = kv_ref[0, k0 : k0 + span, :]
        values = kv_ref[1, k0 : k0 + span, :]
        bias = bias_ref[k0 : k0 + span, r0 : r0 + sub]
        d_query = []
        for half in range(2):
            mask = head_lanes(half, sub)
            query = jnp.where(mask, all_query, jnp.bfloat16(0))
            da = jnp.where(mask, all_da, jnp.bfloat16(0))
            h0 = half * HEAD_DIM
            inner = jnp.sum(product[h0 : h0 + HEAD_DIM, :], axis=0, keepdims=True)
            log = logs[h0 : h0 + 1, :]
            scores = lax.dot_general(keys, query, NT, preferred_element_type=jnp.float32) + bias
            probs = jnp.exp(scores - log)
            d_probs = lax.dot_general(values, da, NT, preferred_element_type=jnp.float32)
            d_scores = (probs * (d_probs - inner)).astype(jnp.bfloat16)
            sum_v_ref[k0 : k0 + span, :] += jnp.dot(
                probs.astype(jnp.bfloat16), da, preferred_element_type=jnp.float32
            )
            sum_k_ref[k0 : k0 + span, :] += jnp.dot(
                d_scores, query, preferred_element_type=jnp.float32
            )
            d_query.append(
                lax.dot_general(d_scores, keys, TN, preferred_element_type=jnp.float32)
            )
        merged = jnp.where(head_lanes(0, sub), d_query[0], d_query[1])
        out_ref[out_ref.shape[0] - 1, r0 : r0 + sub, :] = (merged * SCALE).astype(jnp.bfloat16)
    count = out_ref.shape[0] // 2
    out_ref[:count] = sum_k_ref[...].astype(jnp.bfloat16).reshape(count, rows, LANES)
    out_ref[count : 2 * count] = sum_v_ref[...].astype(jnp.bfloat16).reshape(count, rows, LANES)


def attention_backward(query, kv, d_attended, attended, logs, bias, first, last, earlier=()):
    rows, span = (query.shape[0], kv.shape[1])
    count = 2 * (span // rows) + 1
    sub = sub_rows(rows)
    pair = pl.BlockSpec((rows, LANES), lambda h: (0, h + first))
    both = pl.BlockSpec((2, span, LANES), lambda h: (0, 0, h + first))
    return pl.pallas_call(
        functools.partial(backward_kernel, sub),
        grid=(last - first,),
        in_specs=[
            pair,
            both,
            pair,
            pair,
            pair,
            pl.BlockSpec((span, rows), lambda h: (0, 0)),
            *[pl.BlockSpec(memory_space=pl.ANY)] * len(earlier),
        ],
        out_specs=pl.BlockSpec((count, rows, LANES), lambda h: (0, 0, h + first)),
        out_shape=jax.ShapeDtypeStruct((count, rows, WIDE), jnp.bfloat16),
        input_output_aliases={6 + n: n for n in range(len(earlier))},
        scratch_shapes=[pltpu.VMEM((span, LANES), jnp.float32)] * 2,
        compiler_params=pltpu.CompilerParams(vmem_limit_bytes=48 << 20),
        cost_estimate=hint(),
    )(query, kv, d_attended, attended, logs, bias, *earlier)


def row_chunks(rows):
    step = 256 if rows % 256 == 0 else rows
    return [slice(n, n + step) for n in range(0, rows, step)]


def lane_block(cols, full):
    return min(full, full_lanes(cols))


def params(megabytes=56):
    return pltpu.CompilerParams(vmem_limit_bytes=megabytes << 20)


def hint():
    return pl.CostEstimate(flops=1 << 20, bytes_accessed=1 << 20, transcendentals=0)


def full_lanes(cols):
    return -(-cols // LANES) * LANES


def store_wide(ref, at, value):
    cols, full = (value.shape[1], ref.shape[-1])
    ref[(*at, slice(0, cols))] = value.astype(ref.dtype)
    if cols < full:
        ref[(*at, slice(cols, full))] = jnp.zeros((value.shape[0], full - cols), ref.dtype)


def assemble_kernel(cols, blocks_ref, qkv_ref, out_ref):
    count, rows, full = blocks_ref.shape
    fill = jnp.zeros((rows, WIDE - D), qkv_ref.dtype)

    def fill_in(write, start, stop, skip, size):
        for j in range(count):
            first, last = (max(start, j * size), min(stop, (j + 1) * size))
            if first < last:
                cut = slice(skip + first - j * size, skip + last - j * size)
                write(slice(first - start, last - start), blocks_ref[j, :, cut])

    for n in range(3):

        def write(cut, value, n=n):
            qkv_ref[n, :, cut] = value

        fill_in(write, n * D, (n + 1) * D, 0, cols)
        qkv_ref[n, :, D:] = fill

    def write_out(cut, value):
        out_ref[:, cut] = value

    fill_in(write_out, 0, D, cols, full - cols)


def assemble(blocks, cols):
    count, rows, full = blocks.shape
    step = 320 if rows % 320 == 0 else rows
    return pl.pallas_call(
        functools.partial(assemble_kernel, cols),
        grid=(rows // step,),
        in_specs=[pl.BlockSpec((count, step, full), lambda n: (0, n, 0))],
        out_specs=[
            pl.BlockSpec((3, step, WIDE), lambda n: (0, n, 0)),
            pl.BlockSpec((step, D), lambda n: (n, 0)),
        ],
        out_shape=[
            jax.ShapeDtypeStruct((3, rows, WIDE), blocks.dtype),
            jax.ShapeDtypeStruct((rows, D), blocks.dtype),
        ],
        compiler_params=params(),
        cost_estimate=hint(),
    )(blocks)


def project_kernel(x_ref, w_ref, bias_ref, *refs):
    out_ref = refs[-1]
    total = jnp.dot(x_ref[...], w_ref[0], preferred_element_type=jnp.float32)
    out_ref[0] = (total + bias_ref[0]).astype(out_ref.dtype)


def project_own_kernel(x_ref, w_ref, bias_ref, q_ref, kv_ref):
    total = jnp.dot(x_ref[...], w_ref[0], preferred_element_type=jnp.float32)
    total = (total + bias_ref[0]).astype(q_ref.dtype)

    @pl.when(pl.program_id(0) == 0)
    def _():
        q_ref[...] = total

    @pl.when(pl.program_id(0) > 0)
    def _():
        kv_ref[0] = total


def project_own(x, weights, bias, reach):
    rows, depth = x.shape
    full = weights.shape[2]
    return pl.pallas_call(
        project_own_kernel,
        grid=(3,),
        in_specs=[
            pl.BlockSpec((rows, depth), lambda t: (0, 0)),
            pl.BlockSpec((1, depth, full), lambda t: (t, 0, 0)),
            pl.BlockSpec((1, 1, full), lambda t: (t, 0, 0)),
        ],
        out_specs=[
            pl.BlockSpec((rows, full), lambda t: (0, 0)),
            pl.BlockSpec((1, rows, full), lambda t: (jnp.maximum(t - 1, 0), reach, 0)),
        ],
        out_shape=[
            jax.ShapeDtypeStruct((rows, full), jnp.bfloat16),
            jax.ShapeDtypeStruct((2, (reach + 1) * rows, full), jnp.bfloat16),
        ],
        compiler_params=params(),
        cost_estimate=hint(),
    )(x, weights, bias[:, None, :])


def project_earlier(x, weights, bias, kv, at):
    rows, depth = x.shape
    full = weights.shape[2]
    return pl.pallas_call(
        project_kernel,
        grid=(2,),
        in_specs=[
            pl.BlockSpec((rows, depth), lambda p: (0, 0)),
            pl.BlockSpec((1, depth, full), lambda p: (p + 1, 0, 0)),
            pl.BlockSpec((1, 1, full), lambda p: (p + 1, 0, 0)),
            pl.BlockSpec(memory_space=pl.ANY),
        ],
        out_specs=pl.BlockSpec((1, rows, full), lambda p: (p, at, 0)),
        out_shape=jax.ShapeDtypeStruct(kv.shape, kv.dtype),
        input_output_aliases={3: 0},
        compiler_params=params(),
        cost_estimate=hint(),
    )(x, weights, bias[:, None, :], kv)


def norm_back_kernel(own_ref, top_ref, rest_ref, normal_ref, inverse_ref, gain_ref, dy_ref, *outs):
    wide_ref, low_ref, sums_ref = outs
    cols = own_ref.shape[1]
    upper = pl.program_id(0) < pl.num_programs(0) // 2
    got = jnp.where(upper, top_ref[:, :cols], rest_ref[:, :cols])
    grad = own_ref[...] + got.astype(jnp.float32)
    normal = normal_ref[...]
    product = grad * normal
    scaled = grad * gain_ref[...]
    first = jnp.mean(scaled, axis=1, keepdims=True)
    second = jnp.mean(scaled * normal, axis=1, keepdims=True)
    out = dy_ref[:, :cols].astype(jnp.float32) + inverse_ref[...] * (
        scaled - first - normal * second
    )
    rounded = out.astype(jnp.bfloat16)
    wide_ref[...] = out
    store_wide(low_ref, (slice(None),), rounded)
    parts = [product, grad, rounded.astype(jnp.float32)]
    sums = jnp.concatenate([jnp.sum(part, axis=0, keepdims=True) for part in parts], axis=0)

    @pl.when(pl.program_id(0) == 0)
    def _():
        sums_ref[...] = sums

    @pl.when(pl.program_id(0) > 0)
    def _():
        sums_ref[...] += sums


def norm_back(own, top, rest, normal, inverse, gain, dy):
    rows, cols = own.shape
    step = 128 if rows % 256 == 0 else rows // 2
    half = rows // step // 2
    block = lambda size: pl.BlockSpec((step, size), lambda n: (n, 0))
    return pl.pallas_call(
        norm_back_kernel,
        grid=(rows // step,),
        in_specs=[
            block(cols),
            pl.BlockSpec((step, top.shape[1]), lambda n: (jnp.minimum(n, half - 1), 0)),
            pl.BlockSpec((step, rest.shape[1]), lambda n: (jnp.maximum(n - half, 0), 0)),
            block(cols),
            block(1),
            pl.BlockSpec((1, cols), lambda n: (0, 0)),
            block(dy.shape[1]),
        ],
        out_specs=[block(cols), block(WIDE), pl.BlockSpec((3, cols), lambda n: (0, 0))],
        out_shape=[
            jax.ShapeDtypeStruct((rows, cols), jnp.float32),
            jax.ShapeDtypeStruct((rows, WIDE), jnp.bfloat16),
            jax.ShapeDtypeStruct((3, cols), jnp.float32),
        ],
        compiler_params=params(),
        cost_estimate=hint(),
    )(own, top, rest, normal, inverse, gain[None], dy)


def unit_of(w_ref, cols):
    parts, _, rows, lanes = w_ref.shape
    return w_ref[:, 0].reshape(parts * rows, lanes)[:, :cols]


def unit_block(weights, cols, lane):
    parts, _, rows, full = weights.shape
    return pl.BlockSpec((parts, 1, rows, lane_block(cols, full)), lambda b: (0, b, 0, lane))


def ffn_kernel(x_ref, dy_ref, fc_ref, proj_ref, bias_ref, *refs):
    active_ref, d_hidden_ref, sum_ref, out_ref, total_ref = refs[-5:]
    step = pl.program_id(0)
    cols = bias_ref.shape[2]
    first, second = (0.7978845608028654, 0.044715)
    weight = unit_of(fc_ref, cols)
    depth = weight.shape[0]
    u = jnp.dot(x_ref[:, :depth], weight, preferred_element_type=jnp.float32) + bias_ref[0]
    square = u * u
    t = jnp.tanh(first * u * (1.0 + second * square))
    half = 0.5 * (1.0 + t)
    store_wide(active_ref, (0, slice(None)), u * half)
    slope = half + (0.5 * first) * u * (1.0 - t * t) * (1.0 + (3.0 * second) * square)
    d_active = jnp.dot(
        dy_ref[:, :depth], unit_of(proj_ref, cols), preferred_element_type=jnp.float32
    )
    d_hidden = (d_active * slope).astype(jnp.bfloat16)
    store_wide(d_hidden_ref, (0, slice(None)), d_hidden)
    sum_ref[0] = jnp.sum(d_hidden.astype(jnp.float32), axis=0, keepdims=True)
    part = lax.dot_general(d_hidden, weight, NT, preferred_element_type=jnp.float32)

    @pl.when(step == 0)
    def _():
        total_ref[...] = part

    @pl.when(step > 0)
    def _():
        total_ref[...] += part

    @pl.when(step == pl.num_programs(0) - 1)
    def _():
        store_wide(out_ref, (slice(None),), total_ref[...])


def feed_forward(x, dy, fc, proj, lane, bias, part, kind, earlier=()):
    count, cols = bias.shape
    rows = x.shape[0]
    lanes = full_lanes(cols)
    out_cols = WIDE if kind == jnp.bfloat16 else D
    mine = pl.BlockSpec((1, rows, lanes), lambda b: (b, part, 0))
    units = jax.ShapeDtypeStruct((count, 2 * rows, lanes), jnp.bfloat16)
    return pl.pallas_call(
        ffn_kernel,
        grid=(count,),
        in_specs=[
            pl.BlockSpec(x.shape, lambda b: (0, 0)),
            pl.BlockSpec(dy.shape, lambda b: (0, 0)),
            unit_block(fc, cols, 0),
            unit_block(proj, cols, lane),
            pl.BlockSpec((1, 1, cols), lambda b: (b, 0, 0)),
            *[pl.BlockSpec(memory_space=pl.ANY)] * len(earlier),
        ],
        out_specs=[
            mine,
            mine,
            pl.BlockSpec((1, 1, cols), lambda b: (b, 0, 0)),
            pl.BlockSpec((rows, out_cols), lambda b: (0, 0)),
        ],
        out_shape=[
            units,
            units,
            jax.ShapeDtypeStruct((count, 1, cols), jnp.float32),
            jax.ShapeDtypeStruct((rows, out_cols), kind),
        ],
        input_output_aliases={5 + n: n for n in range(len(earlier))},
        scratch_shapes=[pltpu.VMEM((rows, D), jnp.float32)],
        compiler_params=params(),
        cost_estimate=hint(),
    )(x, dy, fc, proj, bias[:, None, :], *earlier)


def back_kernel(cols, x_ref, w_ref, out_ref, sum_ref):
    step = pl.program_id(0)
    part = lax.dot_general(
        x_ref[0][:, :cols], unit_of(w_ref, cols), NT, preferred_element_type=jnp.float32
    )

    @pl.when(step == 0)
    def _():
        sum_ref[...] = part

    @pl.when(step > 0)
    def _():
        sum_ref[...] += part

    @pl.when(step == pl.num_programs(0) - 1)
    def _():
        store_wide(out_ref, (slice(None),), sum_ref[...])


def ffn_back(x, weights, cols, lane, part, rows, kind):
    count = x.shape[0]
    width = weights.shape[0] * weights.shape[2]
    out_cols = WIDE if kind == jnp.bfloat16 else width
    return pl.pallas_call(
        functools.partial(back_kernel, cols),
        grid=(count,),
        in_specs=[
            pl.BlockSpec((1, rows, x.shape[2]), lambda b: (b, part, 0)),
            unit_block(weights, cols, lane),
        ],
        out_specs=pl.BlockSpec((rows, out_cols), lambda b: (0, 0)),
        out_shape=jax.ShapeDtypeStruct((rows, out_cols), kind),
        scratch_shapes=[pltpu.VMEM((rows, width), jnp.float32)],
        compiler_params=params(),
        cost_estimate=hint(),
    )(x, weights)


def index_list(parts):
    return jnp.stack([jnp.asarray(part, jnp.int32) for part in parts])


def split_specs(count, ny, rows, cols):
    half = count // 2
    block = (1, rows, cols)
    specs = [pl.BlockSpec(block, lambda g, a, b: (g, 0, 0))]
    shapes = [jax.ShapeDtypeStruct((count, rows, cols), jnp.bfloat16)]
    for _ in range(1, ny):
        specs.append(pl.BlockSpec(block, lambda g, a, b: (jnp.minimum(g, half - 1), 0, 0)))
        specs.append(pl.BlockSpec(block, lambda g, a, b: (jnp.maximum(g - half, 0), 0, 0)))
        for size in (half, count - half):
            shapes.append(jax.ShapeDtypeStruct((size, rows, cols), jnp.bfloat16))
    return (specs, shapes)


def store_split(outs, q, value):
    value = value.astype(jnp.bfloat16)
    if q == 0:
        outs[0][0] = value
        return
    step = pl.program_id(0)
    half = pl.num_programs(0) // 2

    @pl.when(step < half)
    def _():
        outs[2 * q - 1][0] = value

    @pl.when(step >= half)
    def _():
        outs[2 * q][0] = value


def by_left_kernel(ny, at_r, at_q, left_ref, *refs):
    rights, got_ref, outs = (refs[:ny], refs[ny], refs[ny + 1 :])
    depth = rights[0].shape[1]
    cols = outs[0].shape[2]
    left = left_ref[0]
    for q in range(ny):
        total = jnp.dot(
            left[:, :depth], rights[q][0][:, :cols], preferred_element_type=jnp.float32
        )
        total += jnp.dot(left[:, depth:], got_ref[q][:, :cols], preferred_element_type=jnp.float32)
        store_split(outs, q, total)


def grads_by_left(left, right, got, cols, at_r, at_q):
    count, (_, rows, depth), (_, half, lanes) = (at_r.size, left.shape, right.shape)
    ny = at_q.size
    own = lambda q: pl.BlockSpec((1, half, lanes), lambda r, a, b: (b[q], 0, 0))
    out_specs, out_shape = split_specs(count, ny, rows, cols)
    return pl.pallas_call(
        functools.partial(by_left_kernel, ny),
        grid_spec=pltpu.PrefetchScalarGridSpec(
            num_scalar_prefetch=2,
            grid=(count,),
            in_specs=[
                pl.BlockSpec((1, rows, depth), lambda r, a, b: (a[r], 0, 0)),
                *[own(q) for q in range(ny)],
                pl.BlockSpec((ny, half, lanes), lambda r, a, b: (0, 0, 0)),
            ],
            out_specs=out_specs,
        ),
        out_shape=out_shape,
        compiler_params=params(),
        cost_estimate=hint(),
    )(at_r, at_q, left, *[right] * ny, got)


def by_right_kernel(ny, at_r, at_q, right_ref, right_got_ref, *refs):
    lefts, got_ref, outs = (refs[:ny], refs[ny], refs[ny + 1 :])
    cols = outs[0].shape[2]
    right, right_got = (right_ref[0][:, :cols], right_got_ref[0][:, :cols])
    for q in range(ny):
        total = jnp.dot(lefts[q][0], right, preferred_element_type=jnp.float32)
        total += jnp.dot(got_ref[q], right_got, preferred_element_type=jnp.float32)
        store_split(outs, q, total)


def grads_by_right(left, left_got, right, right_got, cols, at_r, at_q):
    count, (_, rows, depth) = (at_r.size, left.shape)
    ny = at_q.size
    own = lambda q: pl.BlockSpec((1, rows, depth), lambda r, a, b: (b[q], 0, 0))
    moving = pl.BlockSpec((1, depth, right.shape[2]), lambda r, a, b: (a[r], 0, 0))
    out_specs, out_shape = split_specs(count, ny, rows, cols)
    return pl.pallas_call(
        functools.partial(by_right_kernel, ny),
        grid_spec=pltpu.PrefetchScalarGridSpec(
            num_scalar_prefetch=2,
            grid=(count,),
            in_specs=[
                moving,
                moving,
                *[own(q) for q in range(ny)],
                pl.BlockSpec((ny, rows, depth), lambda r, a, b: (0, 0, 0)),
            ],
            out_specs=out_specs,
        ),
        out_shape=out_shape,
        compiler_params=params(),
        cost_estimate=hint(),
    )(at_r, at_q, right, right_got, *[left] * ny, left_got)


def mixed_kernel(cols, count, at_r, at_q, q_ref, q_got_ref, kv_ref, kv_got_ref, *refs):
    lefts, gots, out_ref = (refs[:count], refs[count:-1], refs[-1])
    step = pl.program_id(0)
    nc = out_ref.shape[0]
    _, own, full = q_ref.shape
    for part, at_step in ((2, 0), (1, 1), (0, 2)):

        @pl.when(step == at_step)
        def _(part=part):
            for q, left_ref in enumerate(lefts):
                if part == 0:
                    first, second = (q_ref[0], q_got_ref[0])
                    left, got = (left_ref[0][:, -own:], gots[q][0][:, -own:])
                else:
                    first, second = (kv_ref[...].reshape(-1, full), kv_got_ref[...].reshape(-1, full))
                    left, got = (left_ref[0], gots[q][0])
                total = jnp.dot(left, first, preferred_element_type=jnp.float32)
                total += jnp.dot(got, second, preferred_element_type=jnp.float32)
                total = total.astype(jnp.bfloat16)
                for j in range(nc):
                    start, stop = (max(part * D, j * cols), min((part + 1) * D, (j + 1) * cols))
                    if start < stop:
                        out_ref[at_r[j], q, :, start - j * cols : stop - j * cols] = total[
                            :, start - part * D : stop - part * D
                        ]


def grads_mixed(left, left_got, grads, grads_got, cols, places, at_q, qs):
    nc = places.size
    _, rows, depth = left.shape
    count, own_rows, wide_cols = grads.shape
    reach = count // 2
    own = lambda q: pl.BlockSpec((1, rows, depth), lambda t, a, b: (b[q], 0, 0))
    once = pl.Buffered(1)
    got = lambda q: pl.BlockSpec((1, rows, depth), lambda t, a, b: (q, 0, 0), pipeline_mode=once)
    query_block = pl.BlockSpec(
        (1, own_rows, wide_cols), lambda t, a, b: (count - 1, 0, 0), pipeline_mode=once
    )
    kv_block = pl.BlockSpec(
        (reach, own_rows, wide_cols), lambda t, a, b: (jnp.where(t == 0, 1, 0), 0, 0)
    )
    return pl.pallas_call(
        functools.partial(mixed_kernel, cols, len(qs)),
        grid_spec=pltpu.PrefetchScalarGridSpec(
            num_scalar_prefetch=2,
            grid=(3,),
            in_specs=[
                query_block,
                query_block,
                kv_block,
                kv_block,
                *[own(q) for q in qs],
                *[got(q) for q in qs],
            ],
            out_specs=pl.BlockSpec((nc, len(qs), rows, cols), lambda t, a, b: (0, 0, 0, 0)),
        ),
        out_shape=jax.ShapeDtypeStruct((nc, len(qs), rows, cols), jnp.bfloat16),
        compiler_params=params(60),
        cost_estimate=hint(),
    )(
        places,
        at_q,
        grads,
        grads_got,
        grads,
        grads_got,
        *[left] * len(qs),
        *[left_got] * len(qs),
    )


def sums_kernel(count, halo_refs, own_ref, normal_refs, q_ref, v_ref, out_ref):
    own = own_ref[...]
    parts = [ref[...].astype(jnp.float32) for ref in halo_refs] + [own]
    down = lambda value: jnp.sum(value, axis=0, keepdims=True)
    gain = sum(down(part * ref[...]) for part, ref in zip(parts, normal_refs))
    shift = sum(down(part) for part in parts)
    query = down(q_ref[0].astype(jnp.float32))
    values = sum(down(v_ref[n].astype(jnp.float32)) for n in range(count))
    fill = jnp.zeros((4, own.shape[1]), jnp.float32)
    out_ref[...] = jnp.concatenate([gain, shift, query, values, fill], axis=0)


def column_sums(halo, own, normals, grads):
    rows = own.shape[0]
    reach = len(normals) - 1
    count = reach + 1
    block = lambda n: pl.BlockSpec((rows, LANES), lambda c: (n, c))

    def kernel(*refs):
        halos, refs = (refs[:reach], refs[reach:])
        sums_kernel(count, halos, refs[0], refs[1 : count + 1], *refs[count + 1 :])

    return pl.pallas_call(
        kernel,
        grid=(PAIRS,),
        in_specs=[
            *[block(n) for n in range(reach)],
            block(0),
            *[block(0)] * count,
            pl.BlockSpec((1, rows, LANES), lambda c: (2 * count, 0, c)),
            pl.BlockSpec((count, rows, LANES), lambda c: (1, 0, c)),
        ],
        out_specs=pl.BlockSpec((8, LANES), lambda c: (0, c)),
        out_shape=jax.ShapeDtypeStruct((8, WIDE), jnp.float32),
        compiler_params=params(),
        cost_estimate=hint(),
    )(*[halo] * reach, own, *normals, grads, grads)


def out_kernel(cols, at_r, at_q, right_ref, right_got_ref, *refs):
    *lefts, got_ref, out_ref = refs
    full = out_ref.shape[0] * cols
    right, right_got = (right_ref[:, :full], right_got_ref[:, :full])
    for q, left_ref in enumerate(lefts):
        total = jnp.dot(left_ref[0], right, preferred_element_type=jnp.float32)
        total += jnp.dot(got_ref[q], right_got, preferred_element_type=jnp.float32)
        total = total.astype(jnp.bfloat16)
        for j in range(out_ref.shape[0]):
            out_ref[at_r[j], q] = total[:, j * cols : (j + 1) * cols]


def grads_out(left, left_got, right, right_got, cols, places, at_q):
    nc = places.size
    ny = at_q.size
    _, rows, depth = left.shape
    own = lambda q: pl.BlockSpec((1, rows, depth), lambda t, a, b: (b[q], 0, 0))
    right_block = pl.BlockSpec(right.shape, lambda t, a, b: (0, 0))
    return pl.pallas_call(
        functools.partial(out_kernel, cols),
        grid_spec=pltpu.PrefetchScalarGridSpec(
            num_scalar_prefetch=2,
            grid=(1,),
            in_specs=[
                right_block,
                right_block,
                *[own(q) for q in range(ny)],
                pl.BlockSpec((ny, rows, depth), lambda t, a, b: (0, 0, 0)),
            ],
            out_specs=pl.BlockSpec((nc, ny, rows, cols), lambda t, a, b: (0, 0, 0, 0)),
        ),
        out_shape=jax.ShapeDtypeStruct((nc, ny, rows, cols), jnp.bfloat16),
        compiler_params=params(),
        cost_estimate=hint(),
    )(
        places,
        at_q,
        right,
        right_got,
        *[left] * ny,
        left_got,
    )


def normed_kernel(q_ref, kv_ref, w_ref, own_ref, halo_ref, sum_ref):
    step = pl.program_id(0)
    count, own, _ = kv_ref.shape

    @pl.when(step == 0)
    def _():
        for n in range(count):
            sum_ref[n * own : (n + 1) * own, :] = lax.dot_general(
                kv_ref[n], w_ref[0], NT, preferred_element_type=jnp.float32
            )

    @pl.when(step == 1)
    def _():
        for n in range(count):
            rows = slice(n * own, (n + 1) * own)
            total = sum_ref[rows, :] + lax.dot_general(
                kv_ref[n], w_ref[0], NT, preferred_element_type=jnp.float32
            )
            if n < count - 1:
                store_wide(halo_ref, (rows,), total)
            else:
                sum_ref[rows, :] = total

    @pl.when(step == 2)
    def _():
        own_ref[...] = sum_ref[(count - 1) * own :, :] + lax.dot_general(
            q_ref[0], w_ref[0], NT, preferred_element_type=jnp.float32
        )


def normed_back(grads, weights):
    count, own, wide_cols = grads.shape
    reach = count // 2
    rows = (reach - 1) * own
    return pl.pallas_call(
        normed_kernel,
        grid=(3,),
        in_specs=[
            pl.BlockSpec((1, own, wide_cols), lambda t: (count - 1, 0, 0)),
            pl.BlockSpec((reach, own, wide_cols), lambda t: (jnp.where(t == 0, 1, 0), 0, 0)),
            pl.BlockSpec((1, D, wide_cols), lambda t: (2 - t, 0, 0)),
        ],
        out_specs=[
            pl.BlockSpec((own, D), lambda t: (0, 0)),
            pl.BlockSpec((rows, WIDE), lambda t: (0, 0)),
        ],
        out_shape=[
            jax.ShapeDtypeStruct((own, D), jnp.float32),
            jax.ShapeDtypeStruct((rows, WIDE), jnp.bfloat16),
        ],
        scratch_shapes=[pltpu.VMEM((reach * own, D), jnp.float32)],
        compiler_params=params(),
        cost_estimate=hint(),
    )(grads, grads, weights)


def place():
    nc, nd = (lax.axis_size("ctx"), lax.axis_size("dat"))
    ctx, dat = (lax.axis_index("ctx"), lax.axis_index("dat"))
    return (nc, nd, ctx, dat // 2, dat % 2)


def dat_of(q, other):
    _, nd, _, y, core = place()
    return 2 * ((y + q) % (nd // 2)) + (1 - core if other else core)


def ctx_of(r):
    nc, _, ctx, _, _ = place()
    return (ctx + r) % nc


def swap_core(value):
    return swap_dat(value, 1)


def ny_of():
    return lax.axis_size("dat") // 2


def sum_of(parts):
    total = wide(parts[0])
    for part in parts[1:]:
        total = total + wide(part)
    return total


def steps_of(nc):
    half = nc // 2
    out = [half]
    for n in range(1, half):
        out += [half + n, half - n]
    return [*out, 0]


class WholeSum:
    def __init__(self, blocks, nc):
        self.own, self.others = (blocks[0], blocks[1:])
        self.order = steps_of(nc)
        self.nc = nc
        self.sums = {}

    def y_sends(self, second):
        return [
            (part, functools.partial(roll_y, steps=q + 1))
            for q, part in enumerate(self.others[second::2])
        ]

    def take_y(self, moved, second):
        half = self.nc // 2
        for n, r in enumerate(self.order[half:] if second else self.order[:half]):
            parts = [part[n] for part in moved]
            self.sums[r] = low(sum_of([self.own[half * second + n], *parts]))

    def z_sends(self):
        half = self.nc // 2
        sends = [(self.sums[half], functools.partial(roll_ctx, steps=1))]
        if half + 1 < self.nc:
            sends.append((self.sums[half + 1], functools.partial(roll_ctx, steps=-1)))
        return sends

    def z_next(self, moved):
        half = self.nc // 2
        ahead = moved[0]
        for r in range(half - 1, 0, -1):
            ahead = low(sum_of([self.sums[r], ahead]))
            if r > 1:
                ahead = roll_ctx(ahead, 1)
        back = moved[1] if len(moved) > 1 else None
        for r in range(half + 2, self.nc):
            back = roll_ctx(low(sum_of([self.sums[r], back])), -1)
        self.back = back
        return [(ahead, functools.partial(roll_ctx, steps=1))]

    def total(self, moved):
        parts = [self.sums[0], moved[0]]
        if self.back is not None:
            parts.append(self.back)
        return low(sum_of(parts))


def mixed_places():
    nc, _, ctx, _, _ = place()
    rep = lax.axis_index("rep")
    quarter = nc // 4
    places = []
    for r in range(nc):
        if r == 0:
            places.append(nc - 1)
        elif r % 2 == 0:
            places.append(2 * quarter + r // 2 - 1)
        else:
            places.append(r // 4 + quarter * jnp.where(rep == r % 4 // 2, 1, 0))
    places = index_list(places)
    return index_list([places[(j - ctx) % nc] for j in range(nc)])


class MixedSum:
    def __init__(self, blocks):
        self.blocks = blocks
        self.nc, self.ny = (blocks[0].shape[0], len(blocks))
        self.quarter = self.nc // 4
        self.rep = lax.axis_index("rep")
        self.kept = {}
        self.sums = {}

    def even(self, r):
        return self.nc - 1 if r == 0 else 2 * self.quarter + r // 2 - 1

    def x_sends(self, qs):
        if len(qs) == self.ny:
            return [(jnp.stack([self.blocks[q][: self.quarter] for q in qs], axis=1), swap_rep)]
        return [(self.blocks[q][: self.quarter], swap_rep) for q in qs]

    def take_x(self, moved, qs):
        for n, q in enumerate(qs):
            got = moved[0][:, q] if len(qs) == self.ny else moved[n]
            self.kept[q] = low(sum_of([self.blocks[q][self.quarter : 2 * self.quarter], got]))

    def y_sends(self, steps):
        return [
            (self.blocks[q][self.even(r)], functools.partial(roll_y, steps=q))
            for r in steps
            for q in range(1, self.ny)
        ]

    def take_y(self, moved, steps):
        for n, r in enumerate(steps):
            parts = moved[n * (self.ny - 1) : (n + 1) * (self.ny - 1)]
            self.sums[r] = low(sum_of([self.blocks[0][self.even(r)], *parts]))

    def odd_y_sends(self):
        return [
            (self.kept[q], functools.partial(roll_y, steps=q)) for q in range(1, self.ny)
        ]

    def take_odd_y(self, moved):
        total = low(sum_of([self.kept[0], *moved]))
        for m in range(self.quarter):
            self.sums[4 * m + 1] = total[m]

    def all_y_sends(self):
        return [
            (
                jnp.concatenate([self.blocks[q][2 * self.quarter :], self.kept[q]], axis=0),
                functools.partial(roll_y, steps=q),
            )
            for q in range(1, self.ny)
        ]

    def take_all_y(self, moved):
        evens = self.nc // 2
        own = jnp.concatenate([self.blocks[0][2 * self.quarter :], self.kept[0]], axis=0)
        total = low(sum_of([own, *moved]))
        for n in range(evens):
            self.sums[2 * n + 2 if n < evens - 1 else 0] = total[n]
        for m in range(self.quarter):
            self.sums[4 * m + 1] = total[evens + m]

    def at(self, distance):
        if distance % 2 == 0:
            if 2 * distance == self.nc:
                return self.sums[distance]
            return jnp.where(self.rep == 0, self.sums[distance], self.sums[self.nc - distance])
        if distance % 4 == 1:
            return self.sums[distance]
        return None

    def move(self, value):
        return roll_ctx_by_rep(value, (1, -1))

    def z_sends(self):
        return [(self.at(self.nc - 2), self.move)]

    def z_next(self, moved):
        carried = moved[0]
        for distance in range(self.nc - 3, 0, -1):
            part = self.at(distance)
            carried = carried if part is None else low(sum_of([part, carried]))
            if distance > 1:
                carried = self.move(carried)
        return [(carried, self.move)]

    def total(self, moved):
        return low(sum_of([self.sums[0], moved[0]]))


class SmallSum:
    @staticmethod
    def prepare(parts):
        nc = lax.axis_size("ctx")
        return (jnp.concatenate([part.reshape(nc, -1) for part in parts], axis=1),)

    def __init__(self, value, sizes):
        nc, nd, ctx, _, _ = place()
        self.sizes = [size // nc for size in sizes]
        self.value = value
        self.ctx = ctx
        self.left = []
        bit = nc // 2
        while bit:
            self.left.append(("ctx", bit))
            bit //= 2
        bit = 1
        while bit < nd:
            self.left.append(("dat", bit))
            bit *= 2
        self.left.append(("rep", 1))

    def sends(self):
        axis, bit = self.left[0]
        count = lax.axis_size(axis)
        pairs = [(s, s ^ bit) for s in range(count)]
        if axis != "ctx":
            return [(self.value, lambda value: permute(value, axis, pairs))]
        halves = self.value.reshape(2, bit, -1)
        mine = (self.ctx // bit) % 2
        self.value = pick(halves, mine)
        return [(pick(halves, 1 - mine), lambda value: permute(value, axis, pairs))]

    def take(self, moved):
        self.left.pop(0)
        self.value = self.value + moved[0].reshape(self.value.shape)

    def finish(self):
        while self.left:
            self.take([move(value) for value, move in self.sends()])
        value = self.value.reshape(-1)
        outs, at = ([], 0)
        for size in self.sizes:
            outs.append(value[at : at + size])
            at += size
        return outs


def gather_small(vector):
    nc, _, ctx, _, _ = place()
    out = jnp.zeros((nc,) + vector.shape, vector.dtype)
    for r in range(nc):
        part = roll_ctx(vector, r) if r else vector
        out = lax.dynamic_update_index_in_dim(out, part, (ctx - r) % nc, 0)
    return out


def pad_cols(value):
    return jnp.pad(value, ((0, 0), (0, WIDE - value.shape[1])))


def regroup(units, count):
    have, rows, cols = units.shape
    if have == count:
        return units
    if have > count:
        per = have // count
        return units.reshape(count, per, rows, cols).swapaxes(1, 2).reshape(count, rows, -1)
    per = count // have
    return units.reshape(have, rows, per, cols // per).swapaxes(1, 2).reshape(count, rows, -1)


def regroup_wide(units, cols, count):
    if units.shape[0] == count:
        return units
    value = regroup(units[:, :, :cols], count)
    return jnp.pad(value, ((0, 0), (0, 0), (0, full_lanes(value.shape[2]) - value.shape[2])))


def local(
    tokens,
    segments,
    cotangent,
    ln1_gain,
    ln1_bias,
    w_qkv,
    b_qv,
    w_out,
    b_out,
    ln2_gain,
    ln2_bias,
    w_fc,
    b_fc,
    w_proj,
    b_proj,
):
    nc, nd, ctx, y, core = place()
    rep = lax.axis_index("rep")
    ff = w_fc.shape[1] * nc
    row_count = tokens.shape[1]
    reach_count = -(-WINDOW // row_count)
    reach_rows = reach_count * row_count

    blocks = max(nc, nd)
    width = ff // blocks // 2
    per_b, per_c = (blocks // nc, blocks // nd)
    qkv_cols, out_cols = (w_qkv.shape[1], w_out.shape[1])
    fc_cols = per_b * width

    small_all = gather_small(
        low(jnp.concatenate([ln1_gain, ln1_bias, b_qv, b_out, ln2_gain, ln2_bias, b_fc, b_proj]))
    )
    smalls, at = ([], 0)
    for part in (ln1_gain, ln1_bias, b_qv, b_out, ln2_gain, ln2_bias, b_fc, b_proj):
        size = part.shape[0]
        smalls.append(wide(small_all[:, at : at + size].reshape(-1)))
        at += size
    gain_one, shift_one, bias_qv, bias_out, gain_two, shift_two, bias_fc, bias_proj = smalls
    bias_half = bias_fc.reshape(blocks, 2, width)
    bias_half = lax.dynamic_index_in_dim(bias_half, rep, axis=1, keepdims=False)

    inputs = wide(tokens[0])
    d_ffn = cotangent[0]
    d_ffn_wide = pad_cols(d_ffn)
    d_ffn_got = swap_rep(d_ffn_wide)
    d_ffn_pair = jnp.concatenate([d_ffn_wide, d_ffn_got], axis=0)
    d_ffn_quad = jnp.concatenate([d_ffn_pair, swap_core(d_ffn_pair)], axis=0)[:, :D]
    d_ffn_quad = d_ffn_quad.T.reshape(nc, D // nc, -1)
    order = steps_of(nc)
    at_ctx = index_list([ctx_of(r) for r in order])
    at_own = index_list([dat_of(q, False) for q in range(nd // 2)])
    at_other = [dat_of(q, True) for q in range(nd // 2)]
    places = mixed_places()
    at_ctx, at_own, places, d_ffn_quad = lax.optimization_barrier(
        (at_ctx, at_own, places, d_ffn_quad)
    )

    def from_other_core(stacked):
        return swap_core(jnp.stack([pick(stacked, at) for at in at_other]))

    shard_a = jnp.concatenate([low(w_qkv), low(w_out)], axis=1)
    full_a = lax.all_gather(shard_a, ("ctx", "dat"), axis=0, tiled=True)
    full_a = full_a.reshape(nc, D, qkv_cols + out_cols)
    normed_own, normal_own, inverse_own = norm_forward(inputs, gain_one, shift_one)
    normed_own = low(normed_own)
    full_a = after(full_a, normed_own, d_ffn_quad)

    segment_row = segments[0]
    padded_segment = jnp.concatenate([jnp.full((reach_rows,), -1, jnp.int32), segment_row])
    key_segment = lax.dynamic_slice_in_dim(padded_segment, ctx * row_count, reach_rows + row_count)
    query_segment = lax.dynamic_slice_in_dim(segment_row, ctx * row_count, row_count)
    query_position = reach_rows + jnp.arange(row_count, dtype=jnp.int32)
    key_position = jnp.arange(reach_rows + row_count, dtype=jnp.int32)

    def mask(at_query, at_key):
        visible = (
            (at_query(query_segment) == at_key(key_segment))
            & (at_key(key_position) <= at_query(query_position))
            & (at_key(key_position) > at_query(query_position) - WINDOW)
        )
        return jnp.where(visible, 0.0, MASKED)

    as_column, as_row = (lambda v: v[:, None], lambda v: v[None, :])
    bias_forward, bias_back = (mask(as_column, as_row), mask(as_row, as_column))
    left_own = normed_own.T

    fc_half = lax.dynamic_index_in_dim(
        low(w_fc).reshape(-1, per_b, 2, width), rep, axis=2, keepdims=False
    ).reshape(-1, fc_cols)
    proj_half = lax.dynamic_index_in_dim(
        low(w_proj).reshape(per_c, 2, width, -1), rep, axis=1, keepdims=False
    ).reshape(per_c * width, -1)
    proj_half = proj_half.T
    shard_b = None
    if nc == nd:
        fill = jnp.zeros((fc_half.shape[0], full_lanes(width) - width), jnp.bfloat16)
        shard_b = jnp.concatenate([fc_half, fill, proj_half, fill], axis=1)
        full_a = after(full_a, shard_b)
    tokens_wide, normed_own, full_a, bias_forward, bias_back, left_own = lax.optimization_barrier(
        (pad_cols(tokens[0]), normed_own, full_a, bias_forward, bias_back, left_own)
    )
    bias_qkv = pad_cols(jnp.stack([bias_qv[:D], jnp.zeros((D,), jnp.float32), bias_qv[D:]]))

    def first_weights(weights, x):
        weights_qkv, weight_out = assemble(weights, qkv_cols)
        return (weights_qkv, weight_out, *project_own(x, weights_qkv, bias_qkv, reach_count))

    (weights_qkv, weight_out, query, kv), (halo,) = stage(
        first_weights,
        [full_a, normed_own],
        [(tokens_wide, functools.partial(shift_ctx, steps=1, first=0, last=nc - 1))],
    )
    normed_halo, normal_halo = ([], [])
    for n in range(reach_count):

        def next_block(tokens_of, kv, n=n):
            normed, normal, _ = norm_forward(wide(tokens_of[:, :D]), gain_one, shift_one)
            normed = low(normed)
            at = reach_count - 1 - n
            return (normed, normal, project_earlier(normed, weights_qkv, bias_qkv, kv, at))

        more = n + 1 < reach_count
        (normed, normal, kv), moved = stage(
            next_block,
            [halo, kv],
            [(halo, functools.partial(shift_ctx, steps=1, first=n + 1, last=nc - 1))] * more,
        )
        normed_halo.insert(0, normed)
        normal_halo.insert(0, normal)
        halo = moved[0] if more else halo
    normed_earlier = jnp.concatenate(normed_halo, axis=0)

    if nc == nd:
        shard_b = after(shard_b, small_all, halo)
        gathered = [lax.all_gather(shard_b, ("ctx", "dat"), axis=0, tiled=True)]
    else:
        gathered = [
            lax.all_gather(fc_half, ("ctx", "dat"), axis=0, tiled=True),
            lax.all_gather(proj_half, ("dat", "ctx"), axis=0, tiled=True),
        ]

    attended, attended_wide, logs = attention_forward(query, kv, bias_forward)
    resid = inputs + dot(attended[:, :D], weight_out) + bias_out
    normed_two, normal_two, inverse_two = norm_forward(resid, gain_two, shift_two)
    normed_two = pad_cols(low(normed_two))

    left_one = jnp.concatenate([normed_earlier.T, left_own], axis=1).reshape(nd, D // nd, -1)
    left_out = attended[:, :D].T.reshape(nd, D // nd, -1)
    left_one_got = from_other_core(left_one)
    left_out_got = from_other_core(left_out)
    gathered = [after(part, normed_two, left_one_got, left_out_got) for part in gathered]
    if nc == nd:
        units_proj = gathered[0].reshape(nc, nd, D // nd, -1)
        units_fc = gathered[0].reshape(1, nc, D, -1)
        lane_proj = 1
    else:
        units_fc = regroup(gathered[0].reshape(nc, D, -1), blocks)[None]
        units_proj = regroup(gathered[1].reshape(nd, D, -1), blocks)[None]
        lane_proj = 0

    (active, d_hidden, sums_own, d_normed_own), (normed_two_got,) = stage(
        lambda x: feed_forward(
            x, d_ffn_wide, units_fc, units_proj, lane_proj, bias_half, 0, jnp.float32
        ),
        [normed_two],
        [(normed_two, swap_rep)],
    )
    active, d_hidden, sums_theirs, d_theirs = feed_forward(
        normed_two_got,
        d_ffn_got,
        units_fc,
        units_proj,
        lane_proj,
        bias_half,
        1,
        jnp.bfloat16,
        (active, d_hidden),
    )
    grad_bias_fc = sums_own + sums_theirs
    active_dat = regroup_wide(active, width, nd)
    d_hidden_ctx = regroup_wide(d_hidden, width, nc)
    ny = ny_of()

    def other(stacked):
        return jnp.stack([pick(stacked, at) for at in at_other])

    def turn(own, got):
        return (jnp.concatenate([own, got], axis=0)[:, :D].T.reshape(nd, D // nd, -1),)

    cut = row_count // 2
    (left_two,), (active_got,) = stage(
        turn,
        [normed_two, normed_two_got],
        [
            (other(active_dat), swap_core),
        ],
    )
    blocks_proj, (d_hidden_got, left_two_got, got_first) = stage(
        lambda x: grads_by_left(d_ffn_quad, x, active_got, per_c * width, at_ctx, at_own),
        [active_dat],
        [
            (d_hidden_ctx, swap_core),
            (other(left_two), swap_core),
            (d_theirs[:cut], swap_rep),
        ],
    )
    proj = WholeSum(blocks_proj, nc)

    def second_blocks(x, active):
        blocks_fc = grads_by_right(
            left_two, left_two_got, x, d_hidden_got, fc_cols, at_ctx, at_own
        )
        active = after(active, blocks_fc[0])
        return (
            ffn_back(active, units_proj, width, lane_proj, 1, row_count, jnp.bfloat16),
            *blocks_fc,
        )

    (ffn_theirs, *blocks_fc), (got_second, *moved) = stage(
        second_blocks,
        [d_hidden_ctx, active],
        [(d_theirs[cut:], swap_rep), *proj.y_sends(0)],
    )
    proj.take_y(moved, 0)
    fc = WholeSum(blocks_fc, nc)

    def to_branch(x, top, rest):
        d_resid, d_branch, sums = norm_back(
            x, top, rest, normal_two, inverse_two, gain_two, d_ffn_wide
        )
        d_attended = ffn_back(
            d_branch[None], weight_out[None, None], D, 0, 0, row_count, jnp.bfloat16
        )
        return (d_resid, d_branch, sums, d_attended)

    (d_resid, d_branch, sums_two, d_attended), moved = stage(
        to_branch,
        [d_normed_own, got_first, got_second],
        [*proj.y_sends(1), *proj.z_sends()],
    )
    proj.take_y(moved[: ny - 1], 1)
    proj_next = proj.z_next(moved[ny - 1 :])

    d_branch_got = swap_core(d_branch)
    middle = PAIRS // 2

    def first_heads(x, d_branch, d_branch_got):
        grads = attention_backward(query, kv, x, attended_wide, logs, bias_back, 0, middle)
        d_branch = after(d_branch, grads)
        blocks_out = grads_out(
            left_out, left_out_got, d_branch, d_branch_got, out_cols, places, at_own
        )
        return (grads, blocks_out)

    (grads, blocks_out), (ffn_first, *moved) = stage(
        first_heads,
        [d_attended, d_branch, d_branch_got],
        [(ffn_theirs[:cut], swap_rep), *fc.y_sends(0), *proj_next],
    )
    out = MixedSum([blocks_out[:, q] for q in range(ny)])
    fc.take_y(moved[: ny - 1], 0)
    proj_total = proj.total(moved[ny - 1 :])
    (grads,), moved = stage(
        lambda x, done: (
            attention_backward(
                query, kv, x, attended_wide, logs, bias_back, middle, PAIRS, [done]
            ),
        ),
        [d_attended, grads],
        [*fc.y_sends(1), *fc.z_sends(), *out.x_sends(range(ny))],
    )
    fc.take_y(moved[: ny - 1], 1)
    *moved, out_moved = moved[ny - 1 :]
    fc_next = fc.z_next(moved)
    out.take_x([out_moved], range(ny))

    (d_normed_own, d_normed_halo), (grads_got, *moved) = stage(
        lambda x: normed_back(x, weights_qkv),
        [grads],
        [
            (grads, swap_core),
            *fc_next,
            *out.all_y_sends(),
            (proj_total, swap_rep),
            (ffn_theirs[cut:], swap_rep),
        ],
    )
    fc_total = fc.total(moved[:1])
    *moved, proj_got, ffn_second = moved[1:]
    out.take_all_y(moved)
    returned = d_normed_halo[:row_count]
    for n in range(1, reach_count - 1):
        returned = shift_ctx(returned, -1, reach_count + 1 - n, nc)
        returned = low(sum_of([returned, d_normed_halo[n * row_count : (n + 1) * row_count]]))
    back_one = functools.partial(shift_ctx, steps=-1, first=min(2, reach_count), last=nc)
    back_two = functools.partial(shift_ctx, steps=-1, first=1, last=nc)
    again = reach_count > 1
    others = list(range(1, ny))
    evens = list(range(2, nc, 2))

    def blocks_of(qs):
        return lambda x: [
            grads_mixed(left_one, left_one_got, x, grads_got, qkv_cols, places, at_own, qs)
        ]

    (blocks_others,), (back_first, fc_got, *moved) = stage(
        blocks_of(others),
        [grads],
        [(returned[:cut], back_one), (fc_total, swap_rep), *out.z_sends()],
    )
    out_next = out.z_next(moved)
    parts = [blocks_others[:, n] for n in range(ny - 1)]
    qkv = MixedSum([parts[0], *parts])
    (blocks_first,), moved = stage(
        blocks_of([0]),
        [after(grads, blocks_others)],
        [
            *qkv.x_sends(others),
            *qkv.y_sends(evens),
            (returned[cut:], back_one),
            *out_next,
        ],
    )
    qkv.blocks[0] = blocks_first[:, 0]
    qkv.take_x(moved[: ny - 1], others)
    qkv.take_y(moved[ny - 1 : -2], evens)
    out_total = out.total(moved[-1:])
    back = [back_first, moved[-2]]

    grad_gain_two, grad_shift_two, grad_bias_out = sums_two
    normals = [*normal_halo, normal_own]

    def vectors(halo, own_grad, grads, d_ffn, bias_fc_sum, *back):
        sums_one = column_sums(halo, own_grad, normals, grads)
        bias_proj_sum = jnp.sum(wide(d_ffn), axis=0)
        halves = [jnp.where(rep == n, bias_fc_sum, 0.0) for n in range(2)]
        small_parts = [grad_bias_out, grad_gain_two, grad_shift_two]
        small_parts += [jnp.concatenate(halves, axis=1).reshape(-1), bias_proj_sum]
        small_parts += [sums_one[0, :D], sums_one[1, :D], sums_one[2:4, :D].reshape(-1)]
        if again:
            last_halo = halo[reach_rows - row_count :]
            pairs = zip(back, (last_halo[:cut], last_halo[cut:]))
            back = [low(sum_of(pair)) for pair in pairs]
        return (*SmallSum.prepare(small_parts), *back)

    bias_fc_sum = grad_bias_fc.reshape(blocks, 1, width)
    (small_value, *back), moved = stage(
        vectors,
        [d_normed_halo, d_normed_own, grads, d_ffn, bias_fc_sum, *back],
        [*qkv.x_sends([0]), *qkv.odd_y_sends(), *qkv.z_sends()],
    )
    qkv.take_x(moved[:1], [0])
    qkv.take_odd_y(moved[1:ny])
    qkv_next = qkv.z_next(moved[ny:])
    small = SmallSum(small_value, [D, D, D, ff, D, D, D, 2 * D])

    (ffn_own,), moved = stage(
        lambda x: (ffn_back(x, units_proj, width, lane_proj, 0, row_count, jnp.float32),),
        [active],
        [
            *qkv_next,
            *qkv.y_sends([0]),
            (out_total, swap_rep),
            *small.sends(),
            *[(back[0], back_two)] * again,
        ],
    )
    if again:
        back[0] = moved.pop()
    qkv.take_y(moved[1:ny], [0])
    qkv_total = qkv.total(moved[:1])
    out_got = moved[ny]
    small.take(moved[ny + 1 :])

    def input_part(rows, returned):
        grad = d_normed_own[rows] + wide(returned[:, :D])
        back_grad = norm_backward(grad, gain_one, normal_own[rows], inverse_own[rows])
        return low(d_resid[rows] + back_grad)

    def both_halves(half, got):
        return (jnp.where(rep == 0, half, got), jnp.where(rep == 0, got, half))

    def last(total, got, returned, fc_half, fc_got, proj_half, proj_got, resid, own, top, rest):
        halves = both_halves(fc_half, fc_got)
        if per_b > 1:
            rows = fc_half.shape[0]
            halves = [part.reshape(rows, per_b, 1, width) for part in halves]
            halves = [jnp.concatenate(halves, axis=2).reshape(rows, -1)]
        grad_fc = wide(jnp.concatenate(halves, axis=1))
        halves = both_halves(proj_half.T, proj_got.T)
        if per_c > 1:
            halves = [part.reshape(per_c, 1, width, -1) for part in halves]
            halves = [jnp.concatenate(halves, axis=1).reshape(2 * per_c * width, -1)]
        grad_proj = wide(jnp.concatenate(halves, axis=0))
        result = jnp.concatenate([top, rest], axis=0)
        layer_out = low(resid + own + wide(result[:, :D]) + bias_proj)
        part = input_part(slice(0, cut), returned)
        return (wide(total) + wide(got), part, grad_fc, grad_proj, layer_out)

    (grad_out_weight, input_first, grad_fc, grad_proj, layer_out), (qkv_got, *moved) = stage(
        last,
        [
            out_total,
            out_got,
            back[0],
            fc_total,
            fc_got,
            proj_total,
            proj_got,
            resid,
            ffn_own,
            ffn_first,
            ffn_second,
        ],
        [(qkv_total, swap_rep), *[(back[1], back_two)] * again, *small.sends()],
    )
    if again:
        back[1] = moved[0]
    small.take(moved[-1:])
    input_grad = jnp.concatenate([input_first, input_part(slice(cut, None), back[1])], axis=0)
    grad_qkv = wide(qkv_total) + wide(qkv_got)
    small_out = small.finish()

    grad_bias_out, grad_gain_two, grad_shift_two, grad_bias_fc, grad_bias_proj = small_out[:5]
    grad_gain_one, grad_shift_one, grad_bias_qv = small_out[5:]

    return (
        layer_out[None],
        input_grad[None],
        grad_gain_one,
        grad_shift_one,
        grad_qkv,
        grad_bias_qv,
        grad_out_weight,
        grad_bias_out,
        grad_gain_two,
        grad_shift_two,
        grad_fc,
        grad_bias_fc,
        grad_proj,
        grad_bias_proj,
    )


def solution(mesh):
    in_specs = (
        P(("rep", "dat"), "ctx", None),
        P(("rep", "dat"), None),
        P(("rep", "dat"), "ctx", None),
        P("ctx"),
        P("ctx"),
        P("dat", "ctx"),
        P("ctx"),
        P("dat", "ctx"),
        P("ctx"),
        P("ctx"),
        P("ctx"),
        P("dat", "ctx"),
        P("ctx"),
        P("dat", "ctx"),
        P("ctx"),
    )
    out_specs = (
        P(("rep", "dat"), "ctx", None),
        P(("rep", "dat"), "ctx", None),
        P("ctx"),
        P("ctx"),
        P("dat", "ctx"),
        P("ctx"),
        P("dat", "ctx"),
        P("ctx"),
        P("ctx"),
        P("ctx"),
        P("dat", "ctx"),
        P("ctx"),
        P("dat", "ctx"),
        P("ctx"),
    )
    return jax.shard_map(local, mesh=mesh, in_specs=in_specs, out_specs=out_specs, check_vma=False)
```

```python
import functools

import jax
import jax.numpy as jnp
from jax import lax
from jax.experimental import pallas as pl
from jax.experimental.pallas import tpu as pltpu
from jax.sharding import PartitionSpec as P

D = 1600
HEADS = 25
HEAD_DIM = 64
WINDOW = 1024


EPS = 1e-05
MASKED = -1e30
LANES = 128
PAIRS = -(-HEADS // 2)
WIDE = PAIRS * LANES
SCALE = HEAD_DIM ** (-0.5)
NT = (((1,), (1,)), ((), ()))
TN = (((0,), (0,)), ((), ()))


def permute(value, axes, pairs):
    return lax.ppermute(value, axes, pairs)


def roll_ctx(value, steps):
    count = lax.axis_size("ctx")
    return permute(value, "ctx", [(s, (s + steps) % count) for s in range(count)])


def shift_ctx(value, steps, first, last):
    return permute(value, "ctx", [(s, s + steps) for s in range(first, last)])


def roll_ctx_by_rep(value, steps):
    count = lax.axis_size("ctx")
    pairs = [
        (rep * count + s, rep * count + (s + steps[rep]) % count)
        for rep in range(len(steps))
        for s in range(count)
    ]
    return permute(value, ("rep", "ctx"), pairs)


def roll_y(value, steps):
    count = lax.axis_size("dat")
    return permute(value, "dat", [(s, (s + 2 * steps) % count) for s in range(count)])


def swap_dat(value, bit):
    count = lax.axis_size("dat")
    return permute(value, "dat", [(s, s ^ bit) for s in range(count)])


def swap_rep(value):
    return permute(value, "rep", [(0, 1), (1, 0)])


def norm_forward(values, gain, shift):
    average = jnp.mean(values, axis=-1, keepdims=True)
    centred = values - average
    variance = jnp.mean(centred * centred, axis=-1, keepdims=True)
    inverse = lax.rsqrt(variance + EPS)
    normal = centred * inverse
    return (normal * gain + shift, normal, inverse)


def norm_backward(grad_out, gain, normal, inverse):
    scaled = grad_out * gain
    first = jnp.mean(scaled, axis=-1, keepdims=True)
    second = jnp.mean(scaled * normal, axis=-1, keepdims=True)
    return inverse * (scaled - first - normal * second)


def dot(left, right):
    return jnp.dot(left, right, preferred_element_type=jnp.float32)


def dot_cols(left, right):
    return lax.dot_general(left, right, NT, preferred_element_type=jnp.float32)


def low(value):
    return value.astype(jnp.bfloat16)


def wide(value):
    return value.astype(jnp.float32)


def pick(stacked, index):
    return lax.dynamic_index_in_dim(stacked, index, axis=0, keepdims=False)


def stage(run, ready, sends):
    count = len(ready)
    flat = lax.optimization_barrier((*ready, *[value for value, _ in sends]))
    outs = run(*flat[:count])
    moved = [move(value) for (_, move), value in zip(sends, flat[count:])]
    flat = lax.optimization_barrier((*outs, *moved))
    return (list(flat[: len(outs)]), list(flat[len(outs) :]))


def after(value, *others):
    return lax.optimization_barrier((value, *others))[0]


def head_lanes(half, rows):
    lane = lax.broadcasted_iota(jnp.int32, (rows, LANES), 1)
    return (lane < HEAD_DIM) if half == 0 else (lane >= HEAD_DIM)


def forward_kernel(sub, q_ref, kv_ref, bias_ref, out_ref, out32_ref, log_ref):
    rows = q_ref.shape[0]
    span = WINDOW + sub
    reach = kv_ref.shape[1] - rows
    for n in range(rows // sub):
        r0 = n * sub
        k0 = reach - WINDOW + r0
        keys = kv_ref[0, k0 : k0 + span, :]
        values = kv_ref[1, k0 : k0 + span, :]
        bias = bias_ref[r0 : r0 + sub, k0 : k0 + span]
        parts = []
        for half in range(2):
            query = jnp.where(
                head_lanes(half, sub), q_ref[r0 : r0 + sub, :] * jnp.bfloat16(SCALE), jnp.bfloat16(0)
            )
            scores = lax.dot_general(query, keys, NT, preferred_element_type=jnp.float32) + bias
            top = jnp.max(scores, axis=1, keepdims=True)
            weights = jnp.exp(scores - top)
            total = jnp.sum(weights, axis=1, keepdims=True)
            summed = jnp.dot(
                weights.astype(jnp.bfloat16), values, preferred_element_type=jnp.float32
            )
            parts.append((summed / total, top + jnp.log(total)))
        first = head_lanes(0, sub)
        out = jnp.where(first, parts[0][0], parts[1][0])
        out_ref[r0 : r0 + sub, :] = out.astype(jnp.bfloat16)
        out32_ref[r0 : r0 + sub, :] = out
        log_ref[r0 : r0 + sub, :] = jnp.where(first, parts[0][1], parts[1][1])


def sub_rows(rows):
    return 256 if rows % 256 == 0 else rows


def pair_block(rows):
    return pl.BlockSpec((rows, LANES), lambda h: (0, h))


def kv_block(rows):
    return pl.BlockSpec((2, rows, LANES), lambda h: (0, 0, h))


def attention_forward(query, kv, bias):
    rows, span = (query.shape[0], kv.shape[1])
    sub = sub_rows(rows)
    return pl.pallas_call(
        functools.partial(forward_kernel, sub),
        grid=(PAIRS,),
        in_specs=[
            pair_block(rows),
            kv_block(span),
            pl.BlockSpec((rows, span), lambda h: (0, 0)),
        ],
        out_specs=[pair_block(rows)] * 3,
        out_shape=[
            jax.ShapeDtypeStruct((rows, WIDE), kind)
            for kind in (jnp.bfloat16, jnp.float32, jnp.float32)
        ],
        compiler_params=pltpu.CompilerParams(vmem_limit_bytes=48 << 20),
        cost_estimate=hint(),
    )(query, kv, bias)


def backward_kernel(
    sub,
    q_ref,
    kv_ref,
    da_ref,
    attended_ref,
    log_ref,
    bias_ref,
    *refs,
):
    out_ref, sum_k_ref, sum_v_ref = refs[-3:]
    rows = q_ref.shape[0]
    span = WINDOW + sub
    reach = kv_ref.shape[1] - rows
    sum_k_ref[...] = jnp.zeros_like(sum_k_ref)
    sum_v_ref[...] = jnp.zeros_like(sum_v_ref)
    for n in range(rows // sub):
        r0 = n * sub
        k0 = reach - WINDOW + r0
        all_da = da_ref[r0 : r0 + sub, :]
        product = jnp.transpose(all_da.astype(jnp.float32) * attended_ref[r0 : r0 + sub, :])
        logs = jnp.transpose(log_ref[r0 : r0 + sub, :])
        all_query = q_ref[r0 : r0 + sub, :] * jnp.bfloat16(SCALE)
        keys = kv_ref[0, k0 : k0 + span, :]
        values = kv_ref[1, k0 : k0 + span, :]
        bias = bias_ref[k0 : k0 + span, r0 : r0 + sub]
        d_query = []
        for half in range(2):
            mask = head_lanes(half, sub)
            query = jnp.where(mask, all_query, jnp.bfloat16(0))
            da = jnp.where(mask, all_da, jnp.bfloat16(0))
            h0 = half * HEAD_DIM
            inner = jnp.sum(product[h0 : h0 + HEAD_DIM, :], axis=0, keepdims=True)
            log = logs[h0 : h0 + 1, :]
            scores = lax.dot_general(keys, query, NT, preferred_element_type=jnp.float32) + bias
            probs = jnp.exp(scores - log)
            d_probs = lax.dot_general(values, da, NT, preferred_element_type=jnp.float32)
            d_scores = (probs * (d_probs - inner)).astype(jnp.bfloat16)
            sum_v_ref[k0 : k0 + span, :] += jnp.dot(
                probs.astype(jnp.bfloat16), da, preferred_element_type=jnp.float32
            )
            sum_k_ref[k0 : k0 + span, :] += jnp.dot(
                d_scores, query, preferred_element_type=jnp.float32
            )
            d_query.append(
                lax.dot_general(d_scores, keys, TN, preferred_element_type=jnp.float32)
            )
        merged = jnp.where(head_lanes(0, sub), d_query[0], d_query[1])
        out_ref[out_ref.shape[0] - 1, r0 : r0 + sub, :] = (merged * SCALE).astype(jnp.bfloat16)
    count = out_ref.shape[0] // 2
    out_ref[:count] = sum_k_ref[...].astype(jnp.bfloat16).reshape(count, rows, LANES)
    out_ref[count : 2 * count] = sum_v_ref[...].astype(jnp.bfloat16).reshape(count, rows, LANES)


def attention_backward(query, kv, d_attended, attended, logs, bias, first, last, earlier=()):
    rows, span = (query.shape[0], kv.shape[1])
    count = 2 * (span // rows) + 1
    sub = sub_rows(rows)
    pair = pl.BlockSpec((rows, LANES), lambda h: (0, h + first))
    both = pl.BlockSpec((2, span, LANES), lambda h: (0, 0, h + first))
    return pl.pallas_call(
        functools.partial(backward_kernel, sub),
        grid=(last - first,),
        in_specs=[
            pair,
            both,
            pair,
            pair,
            pair,
            pl.BlockSpec((span, rows), lambda h: (0, 0)),
            *[pl.BlockSpec(memory_space=pl.ANY)] * len(earlier),
        ],
        out_specs=pl.BlockSpec((count, rows, LANES), lambda h: (0, 0, h + first)),
        out_shape=jax.ShapeDtypeStruct((count, rows, WIDE), jnp.bfloat16),
        input_output_aliases={6 + n: n for n in range(len(earlier))},
        scratch_shapes=[pltpu.VMEM((span, LANES), jnp.float32)] * 2,
        compiler_params=pltpu.CompilerParams(vmem_limit_bytes=48 << 20),
        cost_estimate=hint(),
    )(query, kv, d_attended, attended, logs, bias, *earlier)


def row_chunks(rows):
    step = 256 if rows % 256 == 0 else rows
    return [slice(n, n + step) for n in range(0, rows, step)]


def lane_block(cols, full):
    return min(full, full_lanes(cols))


def params(megabytes=56):
    return pltpu.CompilerParams(vmem_limit_bytes=megabytes << 20)


def hint():
    return pl.CostEstimate(flops=1 << 20, bytes_accessed=1 << 20, transcendentals=0)


def full_lanes(cols):
    return -(-cols // LANES) * LANES


def store_wide(ref, at, value):
    cols, full = (value.shape[1], ref.shape[-1])
    ref[(*at, slice(0, cols))] = value.astype(ref.dtype)
    if cols < full:
        ref[(*at, slice(cols, full))] = jnp.zeros((value.shape[0], full - cols), ref.dtype)


def assemble_kernel(cols, blocks_ref, qkv_ref, out_ref):
    count, rows, full = blocks_ref.shape
    fill = jnp.zeros((rows, WIDE - D), qkv_ref.dtype)

    def fill_in(write, start, stop, skip, size):
        for j in range(count):
            first, last = (max(start, j * size), min(stop, (j + 1) * size))
            if first < last:
                cut = slice(skip + first - j * size, skip + last - j * size)
                write(slice(first - start, last - start), blocks_ref[j, :, cut])

    for n in range(3):

        def write(cut, value, n=n):
            qkv_ref[n, :, cut] = value

        fill_in(write, n * D, (n + 1) * D, 0, cols)
        qkv_ref[n, :, D:] = fill

    def write_out(cut, value):
        out_ref[:, cut] = value

    fill_in(write_out, 0, D, cols, full - cols)


def assemble(blocks, cols):
    count, rows, full = blocks.shape
    step = 320 if rows % 320 == 0 else rows
    return pl.pallas_call(
        functools.partial(assemble_kernel, cols),
        grid=(rows // step,),
        in_specs=[pl.BlockSpec((count, step, full), lambda n: (0, n, 0))],
        out_specs=[
            pl.BlockSpec((3, step, WIDE), lambda n: (0, n, 0)),
            pl.BlockSpec((step, D), lambda n: (n, 0)),
        ],
        out_shape=[
            jax.ShapeDtypeStruct((3, rows, WIDE), blocks.dtype),
            jax.ShapeDtypeStruct((rows, D), blocks.dtype),
        ],
        compiler_params=params(),
        cost_estimate=hint(),
    )(blocks)


def project_kernel(x_ref, w_ref, bias_ref, *refs):
    out_ref = refs[-1]
    total = jnp.dot(x_ref[...], w_ref[0], preferred_element_type=jnp.float32)
    out_ref[0] = (total + bias_ref[0]).astype(out_ref.dtype)


def project_own_kernel(x_ref, w_ref, bias_ref, q_ref, kv_ref):
    total = jnp.dot(x_ref[...], w_ref[0], preferred_element_type=jnp.float32)
    total = (total + bias_ref[0]).astype(q_ref.dtype)

    @pl.when(pl.program_id(0) == 0)
    def _():
        q_ref[...] = total

    @pl.when(pl.program_id(0) > 0)
    def _():
        kv_ref[0] = total


def project_own(x, weights, bias, reach):
    rows, depth = x.shape
    full = weights.shape[2]
    return pl.pallas_call(
        project_own_kernel,
        grid=(3,),
        in_specs=[
            pl.BlockSpec((rows, depth), lambda t: (0, 0)),
            pl.BlockSpec((1, depth, full), lambda t: (t, 0, 0)),
            pl.BlockSpec((1, 1, full), lambda t: (t, 0, 0)),
        ],
        out_specs=[
            pl.BlockSpec((rows, full), lambda t: (0, 0)),
            pl.BlockSpec((1, rows, full), lambda t: (jnp.maximum(t - 1, 0), reach, 0)),
        ],
        out_shape=[
            jax.ShapeDtypeStruct((rows, full), jnp.bfloat16),
            jax.ShapeDtypeStruct((2, (reach + 1) * rows, full), jnp.bfloat16),
        ],
        compiler_params=params(),
        cost_estimate=hint(),
    )(x, weights, bias[:, None, :])


def project_earlier(x, weights, bias, kv, at):
    rows, depth = x.shape
    full = weights.shape[2]
    return pl.pallas_call(
        project_kernel,
        grid=(2,),
        in_specs=[
            pl.BlockSpec((rows, depth), lambda p: (0, 0)),
            pl.BlockSpec((1, depth, full), lambda p: (p + 1, 0, 0)),
            pl.BlockSpec((1, 1, full), lambda p: (p + 1, 0, 0)),
            pl.BlockSpec(memory_space=pl.ANY),
        ],
        out_specs=pl.BlockSpec((1, rows, full), lambda p: (p, at, 0)),
        out_shape=jax.ShapeDtypeStruct(kv.shape, kv.dtype),
        input_output_aliases={3: 0},
        compiler_params=params(),
        cost_estimate=hint(),
    )(x, weights, bias[:, None, :], kv)


def norm_back_kernel(own_ref, top_ref, rest_ref, normal_ref, inverse_ref, gain_ref, dy_ref, *outs):
    wide_ref, low_ref, sums_ref = outs
    cols = own_ref.shape[1]
    upper = pl.program_id(0) < pl.num_programs(0) // 2
    got = jnp.where(upper, top_ref[:, :cols], rest_ref[:, :cols])
    grad = own_ref[...] + got.astype(jnp.float32)
    normal = normal_ref[...]
    product = grad * normal
    scaled = grad * gain_ref[...]
    first = jnp.mean(scaled, axis=1, keepdims=True)
    second = jnp.mean(scaled * normal, axis=1, keepdims=True)
    out = dy_ref[:, :cols].astype(jnp.float32) + inverse_ref[...] * (
        scaled - first - normal * second
    )
    rounded = out.astype(jnp.bfloat16)
    wide_ref[...] = out
    store_wide(low_ref, (slice(None),), rounded)
    parts = [product, grad, rounded.astype(jnp.float32)]
    sums = jnp.concatenate([jnp.sum(part, axis=0, keepdims=True) for part in parts], axis=0)

    @pl.when(pl.program_id(0) == 0)
    def _():
        sums_ref[...] = sums

    @pl.when(pl.program_id(0) > 0)
    def _():
        sums_ref[...] += sums


def norm_back(own, top, rest, normal, inverse, gain, dy):
    rows, cols = own.shape
    step = 128 if rows % 256 == 0 else rows // 2
    half = rows // step // 2
    block = lambda size: pl.BlockSpec((step, size), lambda n: (n, 0))
    return pl.pallas_call(
        norm_back_kernel,
        grid=(rows // step,),
        in_specs=[
            block(cols),
            pl.BlockSpec((step, top.shape[1]), lambda n: (jnp.minimum(n, half - 1), 0)),
            pl.BlockSpec((step, rest.shape[1]), lambda n: (jnp.maximum(n - half, 0), 0)),
            block(cols),
            block(1),
            pl.BlockSpec((1, cols), lambda n: (0, 0)),
            block(dy.shape[1]),
        ],
        out_specs=[block(cols), block(WIDE), pl.BlockSpec((3, cols), lambda n: (0, 0))],
        out_shape=[
            jax.ShapeDtypeStruct((rows, cols), jnp.float32),
            jax.ShapeDtypeStruct((rows, WIDE), jnp.bfloat16),
            jax.ShapeDtypeStruct((3, cols), jnp.float32),
        ],
        compiler_params=params(),
        cost_estimate=hint(),
    )(own, top, rest, normal, inverse, gain[None], dy)


def unit_of(w_ref, cols):
    parts, _, rows, lanes = w_ref.shape
    return w_ref[:, 0].reshape(parts * rows, lanes)[:, :cols]


def unit_block(weights, cols, lane):
    parts, _, rows, full = weights.shape
    return pl.BlockSpec((parts, 1, rows, lane_block(cols, full)), lambda b: (0, b, 0, lane))


def ffn_kernel(x_ref, dy_ref, fc_ref, proj_ref, bias_ref, *refs):
    active_ref, d_hidden_ref, sum_ref, out_ref, total_ref = refs[-5:]
    step = pl.program_id(0)
    cols = bias_ref.shape[2]
    first, second = (0.7978845608028654, 0.044715)
    weight = unit_of(fc_ref, cols)
    depth = weight.shape[0]
    u = jnp.dot(x_ref[:, :depth], weight, preferred_element_type=jnp.float32) + bias_ref[0]
    square = u * u
    t = jnp.tanh(first * u * (1.0 + second * square))
    half = 0.5 * (1.0 + t)
    store_wide(active_ref, (0, slice(None)), u * half)
    slope = half + (0.5 * first) * u * (1.0 - t * t) * (1.0 + (3.0 * second) * square)
    d_active = jnp.dot(
        dy_ref[:, :depth], unit_of(proj_ref, cols), preferred_element_type=jnp.float32
    )
    d_hidden = (d_active * slope).astype(jnp.bfloat16)
    store_wide(d_hidden_ref, (0, slice(None)), d_hidden)
    sum_ref[0] = jnp.sum(d_hidden.astype(jnp.float32), axis=0, keepdims=True)
    part = lax.dot_general(d_hidden, weight, NT, preferred_element_type=jnp.float32)

    @pl.when(step == 0)
    def _():
        total_ref[...] = part

    @pl.when(step > 0)
    def _():
        total_ref[...] += part

    @pl.when(step == pl.num_programs(0) - 1)
    def _():
        store_wide(out_ref, (slice(None),), total_ref[...])


def feed_forward(x, dy, fc, proj, lane, bias, part, kind, earlier=()):
    count, cols = bias.shape
    rows = x.shape[0]
    lanes = full_lanes(cols)
    out_cols = WIDE if kind == jnp.bfloat16 else D
    mine = pl.BlockSpec((1, rows, lanes), lambda b: (b, part, 0))
    units = jax.ShapeDtypeStruct((count, 2 * rows, lanes), jnp.bfloat16)
    return pl.pallas_call(
        ffn_kernel,
        grid=(count,),
        in_specs=[
            pl.BlockSpec(x.shape, lambda b: (0, 0)),
            pl.BlockSpec(dy.shape, lambda b: (0, 0)),
            unit_block(fc, cols, 0),
            unit_block(proj, cols, lane),
            pl.BlockSpec((1, 1, cols), lambda b: (b, 0, 0)),
            *[pl.BlockSpec(memory_space=pl.ANY)] * len(earlier),
        ],
        out_specs=[
            mine,
            mine,
            pl.BlockSpec((1, 1, cols), lambda b: (b, 0, 0)),
            pl.BlockSpec((rows, out_cols), lambda b: (0, 0)),
        ],
        out_shape=[
            units,
            units,
            jax.ShapeDtypeStruct((count, 1, cols), jnp.float32),
            jax.ShapeDtypeStruct((rows, out_cols), kind),
        ],
        input_output_aliases={5 + n: n for n in range(len(earlier))},
        scratch_shapes=[pltpu.VMEM((rows, D), jnp.float32)],
        compiler_params=params(),
        cost_estimate=hint(),
    )(x, dy, fc, proj, bias[:, None, :], *earlier)


def back_kernel(cols, x_ref, w_ref, out_ref, sum_ref):
    step = pl.program_id(0)
    part = lax.dot_general(
        x_ref[0][:, :cols], unit_of(w_ref, cols), NT, preferred_element_type=jnp.float32
    )

    @pl.when(step == 0)
    def _():
        sum_ref[...] = part

    @pl.when(step > 0)
    def _():
        sum_ref[...] += part

    @pl.when(step == pl.num_programs(0) - 1)
    def _():
        store_wide(out_ref, (slice(None),), sum_ref[...])


def ffn_back(x, weights, cols, lane, part, rows, kind):
    count = x.shape[0]
    width = weights.shape[0] * weights.shape[2]
    out_cols = WIDE if kind == jnp.bfloat16 else width
    return pl.pallas_call(
        functools.partial(back_kernel, cols),
        grid=(count,),
        in_specs=[
            pl.BlockSpec((1, rows, x.shape[2]), lambda b: (b, part, 0)),
            unit_block(weights, cols, lane),
        ],
        out_specs=pl.BlockSpec((rows, out_cols), lambda b: (0, 0)),
        out_shape=jax.ShapeDtypeStruct((rows, out_cols), kind),
        scratch_shapes=[pltpu.VMEM((rows, width), jnp.float32)],
        compiler_params=params(),
        cost_estimate=hint(),
    )(x, weights)


def index_list(parts):
    return jnp.stack([jnp.asarray(part, jnp.int32) for part in parts])


def split_specs(count, ny, rows, cols):
    half = count // 2
    block = (1, rows, cols)
    specs = [pl.BlockSpec(block, lambda g, a, b: (g, 0, 0))]
    shapes = [jax.ShapeDtypeStruct((count, rows, cols), jnp.bfloat16)]
    for _ in range(1, ny):
        specs.append(pl.BlockSpec(block, lambda g, a, b: (jnp.minimum(g, half - 1), 0, 0)))
        specs.append(pl.BlockSpec(block, lambda g, a, b: (jnp.maximum(g - half, 0), 0, 0)))
        for size in (half, count - half):
            shapes.append(jax.ShapeDtypeStruct((size, rows, cols), jnp.bfloat16))
    return (specs, shapes)


def store_split(outs, q, value):
    value = value.astype(jnp.bfloat16)
    if q == 0:
        outs[0][0] = value
        return
    step = pl.program_id(0)
    half = pl.num_programs(0) // 2

    @pl.when(step < half)
    def _():
        outs[2 * q - 1][0] = value

    @pl.when(step >= half)
    def _():
        outs[2 * q][0] = value


def by_left_kernel(ny, at_r, at_q, left_ref, *refs):
    rights, gots, outs = (refs[:ny], refs[ny : 2 * ny], refs[2 * ny :])
    depth = rights[0].shape[1]
    cols = outs[0].shape[2]
    left = left_ref[0]
    for q in range(ny):
        total = jnp.dot(
            left[:, :depth], rights[q][0][:, :cols], preferred_element_type=jnp.float32
        )
        total += jnp.dot(left[:, depth:], gots[q][0][:, :cols], preferred_element_type=jnp.float32)
        store_split(outs, q, total)


def grads_by_left(left, right, got, cols, at_r, at_q):
    count, (_, rows, depth), (_, half, lanes) = (at_r.size, left.shape, right.shape)
    ny = at_q.size
    own = lambda q: pl.BlockSpec((1, half, lanes), lambda r, a, b: (b[q], 0, 0))
    out_specs, out_shape = split_specs(count, ny, rows, cols)
    return pl.pallas_call(
        functools.partial(by_left_kernel, ny),
        grid_spec=pltpu.PrefetchScalarGridSpec(
            num_scalar_prefetch=2,
            grid=(count,),
            in_specs=[
                pl.BlockSpec((1, rows, depth), lambda r, a, b: (a[r], 0, 0)),
                *[own(q) for q in range(ny)] * 2,
            ],
            out_specs=out_specs,
        ),
        out_shape=out_shape,
        compiler_params=params(),
        cost_estimate=hint(),
    )(at_r, at_q, left, *[right] * ny, *[got] * ny)


def by_right_kernel(ny, at_r, at_q, right_ref, right_got_ref, *refs):
    lefts, gots, outs = (refs[:ny], refs[ny : 2 * ny], refs[2 * ny :])
    cols = outs[0].shape[2]
    right, right_got = (right_ref[0][:, :cols], right_got_ref[0][:, :cols])
    for q in range(ny):
        total = jnp.dot(lefts[q][0], right, preferred_element_type=jnp.float32)
        total += jnp.dot(gots[q][0], right_got, preferred_element_type=jnp.float32)
        store_split(outs, q, total)


def grads_by_right(left, left_got, right, right_got, cols, at_r, at_q):
    count, (_, rows, depth) = (at_r.size, left.shape)
    ny = at_q.size
    own = lambda q: pl.BlockSpec((1, rows, depth), lambda r, a, b: (b[q], 0, 0))
    moving = pl.BlockSpec((1, depth, right.shape[2]), lambda r, a, b: (a[r], 0, 0))
    out_specs, out_shape = split_specs(count, ny, rows, cols)
    return pl.pallas_call(
        functools.partial(by_right_kernel, ny),
        grid_spec=pltpu.PrefetchScalarGridSpec(
            num_scalar_prefetch=2,
            grid=(count,),
            in_specs=[
                moving,
                moving,
                *[own(q) for q in range(ny)] * 2,
            ],
            out_specs=out_specs,
        ),
        out_shape=out_shape,
        compiler_params=params(),
        cost_estimate=hint(),
    )(at_r, at_q, right, right_got, *[left] * ny, *[left_got] * ny)


def mixed_kernel(cols, count, at_r, at_q, q_ref, q_got_ref, kv_ref, kv_got_ref, *refs):
    lefts, gots, out_ref = (refs[:count], refs[count:-1], refs[-1])
    step = pl.program_id(0)
    nc = out_ref.shape[0]
    _, own, full = q_ref.shape
    for part, at_step in ((2, 0), (1, 1), (0, 2)):

        @pl.when(step == at_step)
        def _(part=part):
            for q, left_ref in enumerate(lefts):
                if part == 0:
                    first, second = (q_ref[0], q_got_ref[0])
                    left, got = (left_ref[0][:, -own:], gots[q][0][:, -own:])
                else:
                    first, second = (kv_ref[...].reshape(-1, full), kv_got_ref[...].reshape(-1, full))
                    left, got = (left_ref[0], gots[q][0])
                total = jnp.dot(left, first, preferred_element_type=jnp.float32)
                total += jnp.dot(got, second, preferred_element_type=jnp.float32)
                total = total.astype(jnp.bfloat16)
                for j in range(nc):
                    start, stop = (max(part * D, j * cols), min((part + 1) * D, (j + 1) * cols))
                    if start < stop:
                        out_ref[at_r[j], q, :, start - j * cols : stop - j * cols] = total[
                            :, start - part * D : stop - part * D
                        ]


def grads_mixed(left, left_got, grads, grads_got, cols, places, at_q, qs):
    nc = places.size
    _, rows, depth = left.shape
    count, own_rows, wide_cols = grads.shape
    reach = count // 2
    own = lambda q: pl.BlockSpec((1, rows, depth), lambda t, a, b: (b[q], 0, 0))
    once = pl.Buffered(1)
    got = lambda q: pl.BlockSpec((1, rows, depth), lambda t, a, b: (q, 0, 0), pipeline_mode=once)
    query_block = pl.BlockSpec(
        (1, own_rows, wide_cols), lambda t, a, b: (count - 1, 0, 0), pipeline_mode=once
    )
    kv_block = pl.BlockSpec(
        (reach, own_rows, wide_cols), lambda t, a, b: (jnp.where(t == 0, 1, 0), 0, 0)
    )
    return pl.pallas_call(
        functools.partial(mixed_kernel, cols, len(qs)),
        grid_spec=pltpu.PrefetchScalarGridSpec(
            num_scalar_prefetch=2,
            grid=(3,),
            in_specs=[
                query_block,
                query_block,
                kv_block,
                kv_block,
                *[own(q) for q in qs],
                *[got(q) for q in qs],
            ],
            out_specs=pl.BlockSpec((nc, len(qs), rows, cols), lambda t, a, b: (0, 0, 0, 0)),
        ),
        out_shape=jax.ShapeDtypeStruct((nc, len(qs), rows, cols), jnp.bfloat16),
        compiler_params=params(60),
        cost_estimate=hint(),
    )(
        places,
        at_q,
        grads,
        grads_got,
        grads,
        grads_got,
        *[left] * len(qs),
        *[left_got] * len(qs),
    )


def sums_kernel(count, halo_refs, own_ref, normal_refs, q_ref, v_ref, out_ref):
    own = own_ref[...]
    parts = [ref[...].astype(jnp.float32) for ref in halo_refs] + [own]
    down = lambda value: jnp.sum(value, axis=0, keepdims=True)
    gain = sum(down(part * ref[...]) for part, ref in zip(parts, normal_refs))
    shift = sum(down(part) for part in parts)
    query = down(q_ref[0].astype(jnp.float32))
    values = sum(down(v_ref[n].astype(jnp.float32)) for n in range(count))
    fill = jnp.zeros((4, own.shape[1]), jnp.float32)
    out_ref[...] = jnp.concatenate([gain, shift, query, values, fill], axis=0)


def column_sums(halo, own, normals, grads):
    rows = own.shape[0]
    reach = len(normals) - 1
    count = reach + 1
    block = lambda n: pl.BlockSpec((rows, LANES), lambda c: (n, c))

    def kernel(*refs):
        halos, refs = (refs[:reach], refs[reach:])
        sums_kernel(count, halos, refs[0], refs[1 : count + 1], *refs[count + 1 :])

    return pl.pallas_call(
        kernel,
        grid=(PAIRS,),
        in_specs=[
            *[block(n) for n in range(reach)],
            block(0),
            *[block(0)] * count,
            pl.BlockSpec((1, rows, LANES), lambda c: (2 * count, 0, c)),
            pl.BlockSpec((count, rows, LANES), lambda c: (1, 0, c)),
        ],
        out_specs=pl.BlockSpec((8, LANES), lambda c: (0, c)),
        out_shape=jax.ShapeDtypeStruct((8, WIDE), jnp.float32),
        compiler_params=params(),
        cost_estimate=hint(),
    )(*[halo] * reach, own, *normals, grads, grads)


def out_kernel(cols, at_r, at_q, right_ref, right_got_ref, *refs):
    *lefts, got_ref, out_ref = refs
    full = out_ref.shape[0] * cols
    right, right_got = (right_ref[:, :full], right_got_ref[:, :full])
    for q, left_ref in enumerate(lefts):
        total = jnp.dot(left_ref[0], right, preferred_element_type=jnp.float32)
        total += jnp.dot(got_ref[q], right_got, preferred_element_type=jnp.float32)
        total = total.astype(jnp.bfloat16)
        for j in range(out_ref.shape[0]):
            out_ref[at_r[j], q] = total[:, j * cols : (j + 1) * cols]


def grads_out(left, left_got, right, right_got, cols, places, at_q):
    nc = places.size
    ny = at_q.size
    _, rows, depth = left.shape
    own = lambda q: pl.BlockSpec((1, rows, depth), lambda t, a, b: (b[q], 0, 0))
    right_block = pl.BlockSpec(right.shape, lambda t, a, b: (0, 0))
    return pl.pallas_call(
        functools.partial(out_kernel, cols),
        grid_spec=pltpu.PrefetchScalarGridSpec(
            num_scalar_prefetch=2,
            grid=(1,),
            in_specs=[
                right_block,
                right_block,
                *[own(q) for q in range(ny)],
                pl.BlockSpec((ny, rows, depth), lambda t, a, b: (0, 0, 0)),
            ],
            out_specs=pl.BlockSpec((nc, ny, rows, cols), lambda t, a, b: (0, 0, 0, 0)),
        ),
        out_shape=jax.ShapeDtypeStruct((nc, ny, rows, cols), jnp.bfloat16),
        compiler_params=params(),
        cost_estimate=hint(),
    )(
        places,
        at_q,
        right,
        right_got,
        *[left] * ny,
        left_got,
    )


def normed_kernel(q_ref, kv_ref, w_ref, own_ref, halo_ref, sum_ref):
    step = pl.program_id(0)
    count, own, _ = kv_ref.shape

    @pl.when(step == 0)
    def _():
        for n in range(count):
            sum_ref[n * own : (n + 1) * own, :] = lax.dot_general(
                kv_ref[n], w_ref[0], NT, preferred_element_type=jnp.float32
            )

    @pl.when(step == 1)
    def _():
        for n in range(count):
            rows = slice(n * own, (n + 1) * own)
            total = sum_ref[rows, :] + lax.dot_general(
                kv_ref[n], w_ref[0], NT, preferred_element_type=jnp.float32
            )
            if n < count - 1:
                store_wide(halo_ref, (rows,), total)
            else:
                sum_ref[rows, :] = total

    @pl.when(step == 2)
    def _():
        own_ref[...] = sum_ref[(count - 1) * own :, :] + lax.dot_general(
            q_ref[0], w_ref[0], NT, preferred_element_type=jnp.float32
        )


def normed_back(grads, weights):
    count, own, wide_cols = grads.shape
    reach = count // 2
    rows = (reach - 1) * own
    return pl.pallas_call(
        normed_kernel,
        grid=(3,),
        in_specs=[
            pl.BlockSpec((1, own, wide_cols), lambda t: (count - 1, 0, 0)),
            pl.BlockSpec((reach, own, wide_cols), lambda t: (jnp.where(t == 0, 1, 0), 0, 0)),
            pl.BlockSpec((1, D, wide_cols), lambda t: (2 - t, 0, 0)),
        ],
        out_specs=[
            pl.BlockSpec((own, D), lambda t: (0, 0)),
            pl.BlockSpec((rows, WIDE), lambda t: (0, 0)),
        ],
        out_shape=[
            jax.ShapeDtypeStruct((own, D), jnp.float32),
            jax.ShapeDtypeStruct((rows, WIDE), jnp.bfloat16),
        ],
        scratch_shapes=[pltpu.VMEM((reach * own, D), jnp.float32)],
        compiler_params=params(),
        cost_estimate=hint(),
    )(grads, grads, weights)


def place():
    nc, nd = (lax.axis_size("ctx"), lax.axis_size("dat"))
    ctx, dat = (lax.axis_index("ctx"), lax.axis_index("dat"))
    return (nc, nd, ctx, dat // 2, dat % 2)


def dat_of(q, other):
    _, nd, _, y, core = place()
    return 2 * ((y + q) % (nd // 2)) + (1 - core if other else core)


def ctx_of(r):
    nc, _, ctx, _, _ = place()
    return (ctx + r) % nc


def swap_core(value):
    return swap_dat(value, 1)


def ny_of():
    return lax.axis_size("dat") // 2


def sum_of(parts):
    total = wide(parts[0])
    for part in parts[1:]:
        total = total + wide(part)
    return total


def steps_of(nc):
    half = nc // 2
    out = [half]
    for n in range(1, half):
        out += [half + n, half - n]
    return [*out, 0]


class WholeSum:
    def __init__(self, blocks, nc):
        self.own, self.others = (blocks[0], blocks[1:])
        self.order = steps_of(nc)
        self.nc = nc
        self.sums = {}

    def y_sends(self, second):
        return [
            (part, functools.partial(roll_y, steps=q + 1))
            for q, part in enumerate(self.others[second::2])
        ]

    def take_y(self, moved, second):
        half = self.nc // 2
        for n, r in enumerate(self.order[half:] if second else self.order[:half]):
            parts = [part[n] for part in moved]
            self.sums[r] = low(sum_of([self.own[half * second + n], *parts]))

    def z_sends(self):
        half = self.nc // 2
        sends = [(self.sums[half], functools.partial(roll_ctx, steps=1))]
        if half + 1 < self.nc:
            sends.append((self.sums[half + 1], functools.partial(roll_ctx, steps=-1)))
        return sends

    def z_next(self, moved):
        half = self.nc // 2
        ahead = moved[0]
        for r in range(half - 1, 0, -1):
            ahead = low(sum_of([self.sums[r], ahead]))
            if r > 1:
                ahead = roll_ctx(ahead, 1)
        back = moved[1] if len(moved) > 1 else None
        for r in range(half + 2, self.nc):
            back = roll_ctx(low(sum_of([self.sums[r], back])), -1)
        self.back = back
        return [(ahead, functools.partial(roll_ctx, steps=1))]

    def total(self, moved):
        parts = [self.sums[0], moved[0]]
        if self.back is not None:
            parts.append(self.back)
        return low(sum_of(parts))


def mixed_places():
    nc, _, ctx, _, _ = place()
    rep = lax.axis_index("rep")
    quarter = nc // 4
    places = []
    for r in range(nc):
        if r == 0:
            places.append(nc - 1)
        elif r % 2 == 0:
            places.append(2 * quarter + r // 2 - 1)
        else:
            places.append(r // 4 + quarter * jnp.where(rep == r % 4 // 2, 1, 0))
    places = index_list(places)
    return index_list([places[(j - ctx) % nc] for j in range(nc)])


class MixedSum:
    def __init__(self, blocks):
        self.blocks = blocks
        self.nc, self.ny = (blocks[0].shape[0], len(blocks))
        self.quarter = self.nc // 4
        self.rep = lax.axis_index("rep")
        self.kept = {}
        self.sums = {}

    def even(self, r):
        return self.nc - 1 if r == 0 else 2 * self.quarter + r // 2 - 1

    def x_sends(self, qs):
        if len(qs) == self.ny:
            return [(jnp.stack([self.blocks[q][: self.quarter] for q in qs], axis=1), swap_rep)]
        return [(self.blocks[q][: self.quarter], swap_rep) for q in qs]

    def take_x(self, moved, qs):
        for n, q in enumerate(qs):
            got = moved[0][:, q] if len(qs) == self.ny else moved[n]
            self.kept[q] = low(sum_of([self.blocks[q][self.quarter : 2 * self.quarter], got]))

    def y_sends(self, steps):
        return [
            (self.blocks[q][self.even(r)], functools.partial(roll_y, steps=q))
            for r in steps
            for q in range(1, self.ny)
        ]

    def take_y(self, moved, steps):
        for n, r in enumerate(steps):
            parts = moved[n * (self.ny - 1) : (n + 1) * (self.ny - 1)]
            self.sums[r] = low(sum_of([self.blocks[0][self.even(r)], *parts]))

    def odd_y_sends(self):
        return [
            (self.kept[q], functools.partial(roll_y, steps=q)) for q in range(1, self.ny)
        ]

    def take_odd_y(self, moved):
        total = low(sum_of([self.kept[0], *moved]))
        for m in range(self.quarter):
            self.sums[4 * m + 1] = total[m]

    def all_y_sends(self):
        return [
            (
                jnp.concatenate([self.blocks[q][2 * self.quarter :], self.kept[q]], axis=0),
                functools.partial(roll_y, steps=q),
            )
            for q in range(1, self.ny)
        ]

    def take_all_y(self, moved):
        evens = self.nc // 2
        own = jnp.concatenate([self.blocks[0][2 * self.quarter :], self.kept[0]], axis=0)
        total = low(sum_of([own, *moved]))
        for n in range(evens):
            self.sums[2 * n + 2 if n < evens - 1 else 0] = total[n]
        for m in range(self.quarter):
            self.sums[4 * m + 1] = total[evens + m]

    def at(self, distance):
        if distance % 2 == 0:
            if 2 * distance == self.nc:
                return self.sums[distance]
            return jnp.where(self.rep == 0, self.sums[distance], self.sums[self.nc - distance])
        if distance % 4 == 1:
            return self.sums[distance]
        return None

    def move(self, value):
        return roll_ctx_by_rep(value, (1, -1))

    def z_sends(self):
        return [(self.at(self.nc - 2), self.move)]

    def z_next(self, moved):
        carried = moved[0]
        for distance in range(self.nc - 3, 0, -1):
            part = self.at(distance)
            carried = carried if part is None else low(sum_of([part, carried]))
            if distance > 1:
                carried = self.move(carried)
        return [(carried, self.move)]

    def total(self, moved):
        return low(sum_of([self.sums[0], moved[0]]))


class SmallSum:
    @staticmethod
    def prepare(parts):
        nc = lax.axis_size("ctx")
        return (jnp.concatenate([part.reshape(nc, -1) for part in parts], axis=1),)

    def __init__(self, value, sizes):
        nc, nd, ctx, _, _ = place()
        self.sizes = [size // nc for size in sizes]
        self.value = value
        self.ctx = ctx
        self.left = []
        bit = nc // 2
        while bit:
            self.left.append(("ctx", bit))
            bit //= 2
        bit = 1
        while bit < nd:
            self.left.append(("dat", bit))
            bit *= 2
        self.left.append(("rep", 1))

    def sends(self):
        axis, bit = self.left[0]
        count = lax.axis_size(axis)
        pairs = [(s, s ^ bit) for s in range(count)]
        if axis != "ctx":
            return [(self.value, lambda value: permute(value, axis, pairs))]
        halves = self.value.reshape(2, bit, -1)
        mine = (self.ctx // bit) % 2
        self.value = pick(halves, mine)
        return [(pick(halves, 1 - mine), lambda value: permute(value, axis, pairs))]

    def take(self, moved):
        self.left.pop(0)
        self.value = self.value + moved[0].reshape(self.value.shape)

    def finish(self):
        while self.left:
            self.take([move(value) for value, move in self.sends()])
        value = self.value.reshape(-1)
        outs, at = ([], 0)
        for size in self.sizes:
            outs.append(value[at : at + size])
            at += size
        return outs


def gather_small(vector):
    nc, _, ctx, _, _ = place()
    out = jnp.zeros((nc,) + vector.shape, vector.dtype)
    for r in range(nc):
        part = roll_ctx(vector, r) if r else vector
        out = lax.dynamic_update_index_in_dim(out, part, (ctx - r) % nc, 0)
    return out


def pad_cols(value):
    return jnp.pad(value, ((0, 0), (0, WIDE - value.shape[1])))


def regroup(units, count):
    have, rows, cols = units.shape
    if have == count:
        return units
    if have > count:
        per = have // count
        return units.reshape(count, per, rows, cols).swapaxes(1, 2).reshape(count, rows, -1)
    per = count // have
    return units.reshape(have, rows, per, cols // per).swapaxes(1, 2).reshape(count, rows, -1)


def regroup_wide(units, cols, count):
    if units.shape[0] == count:
        return units
    value = regroup(units[:, :, :cols], count)
    return jnp.pad(value, ((0, 0), (0, 0), (0, full_lanes(value.shape[2]) - value.shape[2])))


def local(
    tokens,
    segments,
    cotangent,
    ln1_gain,
    ln1_bias,
    w_qkv,
    b_qv,
    w_out,
    b_out,
    ln2_gain,
    ln2_bias,
    w_fc,
    b_fc,
    w_proj,
    b_proj,
):
    nc, nd, ctx, y, core = place()
    rep = lax.axis_index("rep")
    ff = w_fc.shape[1] * nc
    row_count = tokens.shape[1]
    reach_count = -(-WINDOW // row_count)
    reach_rows = reach_count * row_count

    blocks = max(nc, nd)
    width = ff // blocks // 2
    per_b, per_c = (blocks // nc, blocks // nd)
    qkv_cols, out_cols = (w_qkv.shape[1], w_out.shape[1])
    fc_cols = per_b * width

    small_all = gather_small(
        low(jnp.concatenate([ln1_gain, ln1_bias, b_qv, b_out, ln2_gain, ln2_bias, b_fc, b_proj]))
    )
    smalls, at = ([], 0)
    for part in (ln1_gain, ln1_bias, b_qv, b_out, ln2_gain, ln2_bias, b_fc, b_proj):
        size = part.shape[0]
        smalls.append(wide(small_all[:, at : at + size].reshape(-1)))
        at += size
    gain_one, shift_one, bias_qv, bias_out, gain_two, shift_two, bias_fc, bias_proj = smalls
    bias_half = bias_fc.reshape(blocks, 2, width)
    bias_half = lax.dynamic_index_in_dim(bias_half, rep, axis=1, keepdims=False)

    inputs = wide(tokens[0])
    d_ffn = cotangent[0]
    d_ffn_wide = pad_cols(d_ffn)
    d_ffn_got = swap_rep(d_ffn_wide)
    d_ffn_pair = jnp.concatenate([d_ffn_wide, d_ffn_got], axis=0)
    d_ffn_quad = jnp.concatenate([d_ffn_pair, swap_core(d_ffn_pair)], axis=0)[:, :D]
    d_ffn_quad = d_ffn_quad.T.reshape(nc, D // nc, -1)
    order = steps_of(nc)
    at_ctx = index_list([ctx_of(r) for r in order])
    at_own = index_list([dat_of(q, False) for q in range(nd // 2)])
    at_other = [dat_of(q, True) for q in range(nd // 2)]
    places = mixed_places()
    at_ctx, at_own, places, d_ffn_quad = lax.optimization_barrier(
        (at_ctx, at_own, places, d_ffn_quad)
    )

    def from_other_core(stacked):
        return swap_core(jnp.stack([pick(stacked, at) for at in at_other]))

    shard_a = jnp.concatenate([low(w_qkv), low(w_out)], axis=1)
    full_a = lax.all_gather(shard_a, ("ctx", "dat"), axis=0, tiled=True)
    full_a = full_a.reshape(nc, D, qkv_cols + out_cols)
    normed_own, normal_own, inverse_own = norm_forward(inputs, gain_one, shift_one)
    normed_own = low(normed_own)
    full_a = after(full_a, normed_own, d_ffn_quad)

    segment_row = segments[0]
    padded_segment = jnp.concatenate([jnp.full((reach_rows,), -1, jnp.int32), segment_row])
    key_segment = lax.dynamic_slice_in_dim(padded_segment, ctx * row_count, reach_rows + row_count)
    query_segment = lax.dynamic_slice_in_dim(segment_row, ctx * row_count, row_count)
    query_position = reach_rows + jnp.arange(row_count, dtype=jnp.int32)
    key_position = jnp.arange(reach_rows + row_count, dtype=jnp.int32)

    def mask(at_query, at_key):
        visible = (
            (at_query(query_segment) == at_key(key_segment))
            & (at_key(key_position) <= at_query(query_position))
            & (at_key(key_position) > at_query(query_position) - WINDOW)
        )
        return jnp.where(visible, 0.0, MASKED)

    as_column, as_row = (lambda v: v[:, None], lambda v: v[None, :])
    bias_forward, bias_back = (mask(as_column, as_row), mask(as_row, as_column))
    left_own = normed_own.T

    fc_half = lax.dynamic_index_in_dim(
        low(w_fc).reshape(-1, per_b, 2, width), rep, axis=2, keepdims=False
    ).reshape(-1, fc_cols)
    proj_half = lax.dynamic_index_in_dim(
        low(w_proj).reshape(per_c, 2, width, -1), rep, axis=1, keepdims=False
    ).reshape(per_c * width, -1)
    proj_half = proj_half.T
    shard_b = None
    if nc == nd:
        fill = jnp.zeros((fc_half.shape[0], full_lanes(width) - width), jnp.bfloat16)
        shard_b = jnp.concatenate([fc_half, fill, proj_half, fill], axis=1)
        full_a = after(full_a, shard_b)
    tokens_wide, normed_own, full_a, bias_forward, bias_back, left_own = lax.optimization_barrier(
        (pad_cols(tokens[0]), normed_own, full_a, bias_forward, bias_back, left_own)
    )
    bias_qkv = pad_cols(jnp.stack([bias_qv[:D], jnp.zeros((D,), jnp.float32), bias_qv[D:]]))

    def first_weights(weights, x):
        weights_qkv, weight_out = assemble(weights, qkv_cols)
        return (weights_qkv, weight_out, *project_own(x, weights_qkv, bias_qkv, reach_count))

    (weights_qkv, weight_out, query, kv), (halo,) = stage(
        first_weights,
        [full_a, normed_own],
        [(tokens_wide, functools.partial(shift_ctx, steps=1, first=0, last=nc - 1))],
    )
    normed_halo, normal_halo = ([], [])
    for n in range(reach_count):

        def next_block(tokens_of, kv, n=n):
            normed, normal, _ = norm_forward(wide(tokens_of[:, :D]), gain_one, shift_one)
            normed = low(normed)
            at = reach_count - 1 - n
            return (normed, normal, project_earlier(normed, weights_qkv, bias_qkv, kv, at))

        more = n + 1 < reach_count
        (normed, normal, kv), moved = stage(
            next_block,
            [halo, kv],
            [(halo, functools.partial(shift_ctx, steps=1, first=n + 1, last=nc - 1))] * more,
        )
        normed_halo.insert(0, normed)
        normal_halo.insert(0, normal)
        halo = moved[0] if more else halo
    normed_earlier = jnp.concatenate(normed_halo, axis=0)

    if nc == nd:
        shard_b = after(shard_b, small_all, halo)
        gathered = [lax.all_gather(shard_b, ("ctx", "dat"), axis=0, tiled=True)]
    else:
        gathered = [
            lax.all_gather(fc_half, ("ctx", "dat"), axis=0, tiled=True),
            lax.all_gather(proj_half, ("dat", "ctx"), axis=0, tiled=True),
        ]

    attended, attended_wide, logs = attention_forward(query, kv, bias_forward)
    resid = inputs + dot(attended[:, :D], weight_out) + bias_out
    normed_two, normal_two, inverse_two = norm_forward(resid, gain_two, shift_two)
    normed_two = pad_cols(low(normed_two))

    left_one = jnp.concatenate([normed_earlier.T, left_own], axis=1).reshape(nd, D // nd, -1)
    left_out = attended[:, :D].T.reshape(nd, D // nd, -1)
    left_one_got = from_other_core(left_one)
    left_out_got = from_other_core(left_out)
    gathered = [after(part, normed_two, left_one_got, left_out_got) for part in gathered]
    if nc == nd:
        units_proj = gathered[0].reshape(nc, nd, D // nd, -1)
        units_fc = gathered[0].reshape(1, nc, D, -1)
        lane_proj = 1
    else:
        units_fc = regroup(gathered[0].reshape(nc, D, -1), blocks)[None]
        units_proj = regroup(gathered[1].reshape(nd, D, -1), blocks)[None]
        lane_proj = 0

    (active, d_hidden, sums_own, d_normed_own), (normed_two_got,) = stage(
        lambda x: feed_forward(
            x, d_ffn_wide, units_fc, units_proj, lane_proj, bias_half, 0, jnp.float32
        ),
        [normed_two],
        [(normed_two, swap_rep)],
    )
    active, d_hidden, sums_theirs, d_theirs = feed_forward(
        normed_two_got,
        d_ffn_got,
        units_fc,
        units_proj,
        lane_proj,
        bias_half,
        1,
        jnp.bfloat16,
        (active, d_hidden),
    )
    grad_bias_fc = sums_own + sums_theirs
    active_dat = regroup_wide(active, width, nd)
    d_hidden_ctx = regroup_wide(d_hidden, width, nc)
    ny = ny_of()

    def turn(own, got):
        return (jnp.concatenate([own, got], axis=0)[:, :D].T.reshape(nd, D // nd, -1),)

    cut = row_count // 2
    (left_two,), (active_got,) = stage(
        turn,
        [normed_two, normed_two_got],
        [
            (active_dat, swap_core),
        ],
    )
    blocks_proj, (d_hidden_got, left_two_got, got_first) = stage(
        lambda x: grads_by_left(d_ffn_quad, x, active_got, per_c * width, at_ctx, at_own),
        [active_dat],
        [
            (d_hidden_ctx, swap_core),
            (left_two, swap_core),
            (d_theirs[:cut], swap_rep),
        ],
    )
    proj = WholeSum(blocks_proj, nc)

    def second_blocks(x, active):
        blocks_fc = grads_by_right(
            left_two, left_two_got, x, d_hidden_got, fc_cols, at_ctx, at_own
        )
        active = after(active, blocks_fc[0])
        return (
            ffn_back(active, units_proj, width, lane_proj, 1, row_count, jnp.bfloat16),
            *blocks_fc,
        )

    (ffn_theirs, *blocks_fc), (got_second, *moved) = stage(
        second_blocks,
        [d_hidden_ctx, active],
        [(d_theirs[cut:], swap_rep), *proj.y_sends(0)],
    )
    proj.take_y(moved, 0)
    fc = WholeSum(blocks_fc, nc)

    def to_branch(x, top, rest):
        d_resid, d_branch, sums = norm_back(
            x, top, rest, normal_two, inverse_two, gain_two, d_ffn_wide
        )
        d_attended = ffn_back(
            d_branch[None], weight_out[None, None], D, 0, 0, row_count, jnp.bfloat16
        )
        return (d_resid, d_branch, sums, d_attended)

    (d_resid, d_branch, sums_two, d_attended), moved = stage(
        to_branch,
        [d_normed_own, got_first, got_second],
        [*proj.y_sends(1), *proj.z_sends()],
    )
    proj.take_y(moved[: ny - 1], 1)
    proj_next = proj.z_next(moved[ny - 1 :])

    d_branch_got = swap_core(d_branch)
    middle = PAIRS // 2

    def first_heads(x, d_branch, d_branch_got):
        grads = attention_backward(query, kv, x, attended_wide, logs, bias_back, 0, middle)
        d_branch = after(d_branch, grads)
        blocks_out = grads_out(
            left_out, left_out_got, d_branch, d_branch_got, out_cols, places, at_own
        )
        return (grads, blocks_out)

    (grads, blocks_out), (ffn_first, *moved) = stage(
        first_heads,
        [d_attended, d_branch, d_branch_got],
        [(ffn_theirs[:cut], swap_rep), *fc.y_sends(0), *proj_next],
    )
    out = MixedSum([blocks_out[:, q] for q in range(ny)])
    fc.take_y(moved[: ny - 1], 0)
    proj_total = proj.total(moved[ny - 1 :])
    (grads,), moved = stage(
        lambda x, done: (
            attention_backward(
                query, kv, x, attended_wide, logs, bias_back, middle, PAIRS, [done]
            ),
        ),
        [d_attended, grads],
        [*fc.y_sends(1), *fc.z_sends(), *out.x_sends(range(ny))],
    )
    fc.take_y(moved[: ny - 1], 1)
    *moved, out_moved = moved[ny - 1 :]
    fc_next = fc.z_next(moved)
    out.take_x([out_moved], range(ny))

    (d_normed_own, d_normed_halo), (grads_got, *moved) = stage(
        lambda x: normed_back(x, weights_qkv),
        [grads],
        [
            (grads, swap_core),
            *fc_next,
            *out.all_y_sends(),
            (proj_total, swap_rep),
            (ffn_theirs[cut:], swap_rep),
        ],
    )
    fc_total = fc.total(moved[:1])
    *moved, proj_got, ffn_second = moved[1:]
    out.take_all_y(moved)
    returned = d_normed_halo[:row_count]
    for n in range(1, reach_count - 1):
        returned = shift_ctx(returned, -1, reach_count + 1 - n, nc)
        returned = low(sum_of([returned, d_normed_halo[n * row_count : (n + 1) * row_count]]))
    back_one = functools.partial(shift_ctx, steps=-1, first=min(2, reach_count), last=nc)
    back_two = functools.partial(shift_ctx, steps=-1, first=1, last=nc)
    again = reach_count > 1
    others = list(range(1, ny))
    evens = list(range(2, nc, 2))

    def blocks_of(qs):
        return lambda x: [
            grads_mixed(left_one, left_one_got, x, grads_got, qkv_cols, places, at_own, qs)
        ]

    (blocks_others,), (back_first, fc_got, *moved) = stage(
        blocks_of(others),
        [grads],
        [(returned[:cut], back_one), (fc_total, swap_rep), *out.z_sends()],
    )
    out_next = out.z_next(moved)
    parts = [blocks_others[:, n] for n in range(ny - 1)]
    qkv = MixedSum([parts[0], *parts])
    (blocks_first,), moved = stage(
        blocks_of([0]),
        [after(grads, blocks_others)],
        [
            *qkv.x_sends(others),
            *qkv.y_sends(evens),
            (returned[cut:], back_one),
            *out_next,
        ],
    )
    qkv.blocks[0] = blocks_first[:, 0]
    qkv.take_x(moved[: ny - 1], others)
    qkv.take_y(moved[ny - 1 : -2], evens)
    out_total = out.total(moved[-1:])
    back = [back_first, moved[-2]]

    grad_gain_two, grad_shift_two, grad_bias_out = sums_two
    normals = [*normal_halo, normal_own]

    def vectors(halo, own_grad, grads, d_ffn, bias_fc_sum, *back):
        sums_one = column_sums(halo, own_grad, normals, grads)
        bias_proj_sum = jnp.sum(wide(d_ffn), axis=0)
        halves = [jnp.where(rep == n, bias_fc_sum, 0.0) for n in range(2)]
        small_parts = [grad_bias_out, grad_gain_two, grad_shift_two]
        small_parts += [jnp.concatenate(halves, axis=1).reshape(-1), bias_proj_sum]
        small_parts += [sums_one[0, :D], sums_one[1, :D], sums_one[2:4, :D].reshape(-1)]
        if again:
            last_halo = halo[reach_rows - row_count :]
            pairs = zip(back, (last_halo[:cut], last_halo[cut:]))
            back = [low(sum_of(pair)) for pair in pairs]
        return (*SmallSum.prepare(small_parts), *back)

    bias_fc_sum = grad_bias_fc.reshape(blocks, 1, width)
    (small_value, *back), moved = stage(
        vectors,
        [d_normed_halo, d_normed_own, grads, d_ffn, bias_fc_sum, *back],
        [*qkv.x_sends([0]), *qkv.odd_y_sends(), *qkv.z_sends()],
    )
    qkv.take_x(moved[:1], [0])
    qkv.take_odd_y(moved[1:ny])
    qkv_next = qkv.z_next(moved[ny:])
    small = SmallSum(small_value, [D, D, D, ff, D, D, D, 2 * D])

    (ffn_own,), moved = stage(
        lambda x: (ffn_back(x, units_proj, width, lane_proj, 0, row_count, jnp.float32),),
        [active],
        [
            *qkv_next,
            *qkv.y_sends([0]),
            (out_total, swap_rep),
            *small.sends(),
            *[(back[0], back_two)] * again,
        ],
    )
    if again:
        back[0] = moved.pop()
    qkv.take_y(moved[1:ny], [0])
    qkv_total = qkv.total(moved[:1])
    out_got = moved[ny]
    small.take(moved[ny + 1 :])

    def input_part(rows, returned):
        grad = d_normed_own[rows] + wide(returned[:, :D])
        back_grad = norm_backward(grad, gain_one, normal_own[rows], inverse_own[rows])
        return low(d_resid[rows] + back_grad)

    def both_halves(half, got):
        return (jnp.where(rep == 0, half, got), jnp.where(rep == 0, got, half))

    def last(total, got, returned, fc_half, fc_got, proj_half, proj_got, resid, own, top, rest):
        halves = both_halves(fc_half, fc_got)
        if per_b > 1:
            rows = fc_half.shape[0]
            halves = [part.reshape(rows, per_b, 1, width) for part in halves]
            halves = [jnp.concatenate(halves, axis=2).reshape(rows, -1)]
        grad_fc = wide(jnp.concatenate(halves, axis=1))
        halves = both_halves(proj_half.T, proj_got.T)
        if per_c > 1:
            halves = [part.reshape(per_c, 1, width, -1) for part in halves]
            halves = [jnp.concatenate(halves, axis=1).reshape(2 * per_c * width, -1)]
        grad_proj = wide(jnp.concatenate(halves, axis=0))
        result = jnp.concatenate([top, rest], axis=0)
        layer_out = low(resid + own + wide(result[:, :D]) + bias_proj)
        part = input_part(slice(0, cut), returned)
        return (wide(total) + wide(got), part, grad_fc, grad_proj, layer_out)

    (grad_out_weight, input_first, grad_fc, grad_proj, layer_out), (qkv_got, *moved) = stage(
        last,
        [
            out_total,
            out_got,
            back[0],
            fc_total,
            fc_got,
            proj_total,
            proj_got,
            resid,
            ffn_own,
            ffn_first,
            ffn_second,
        ],
        [(qkv_total, swap_rep), *[(back[1], back_two)] * again, *small.sends()],
    )
    if again:
        back[1] = moved[0]
    small.take(moved[-1:])
    input_grad = jnp.concatenate([input_first, input_part(slice(cut, None), back[1])], axis=0)
    grad_qkv = wide(qkv_total) + wide(qkv_got)
    small_out = small.finish()

    grad_bias_out, grad_gain_two, grad_shift_two, grad_bias_fc, grad_bias_proj = small_out[:5]
    grad_gain_one, grad_shift_one, grad_bias_qv = small_out[5:]

    return (
        layer_out[None],
        input_grad[None],
        grad_gain_one,
        grad_shift_one,
        grad_qkv,
        grad_bias_qv,
        grad_out_weight,
        grad_bias_out,
        grad_gain_two,
        grad_shift_two,
        grad_fc,
        grad_bias_fc,
        grad_proj,
        grad_bias_proj,
    )


def solution(mesh):
    in_specs = (
        P(("rep", "dat"), "ctx", None),
        P(("rep", "dat"), None),
        P(("rep", "dat"), "ctx", None),
        P("ctx"),
        P("ctx"),
        P("dat", "ctx"),
        P("ctx"),
        P("dat", "ctx"),
        P("ctx"),
        P("ctx"),
        P("ctx"),
        P("dat", "ctx"),
        P("ctx"),
        P("dat", "ctx"),
        P("ctx"),
    )
    out_specs = (
        P(("rep", "dat"), "ctx", None),
        P(("rep", "dat"), "ctx", None),
        P("ctx"),
        P("ctx"),
        P("dat", "ctx"),
        P("ctx"),
        P("dat", "ctx"),
        P("ctx"),
        P("ctx"),
        P("ctx"),
        P("dat", "ctx"),
        P("ctx"),
        P("dat", "ctx"),
        P("ctx"),
    )
    return jax.shard_map(local, mesh=mesh, in_specs=in_specs, out_specs=out_specs, check_vma=False)
```

```python
import functools

import jax
import jax.numpy as jnp
from jax import lax
from jax.experimental import pallas as pl
from jax.experimental.pallas import tpu as pltpu
from jax.sharding import PartitionSpec as P

D = 1600
HEADS = 25
HEAD_DIM = 64
WINDOW = 1024


EPS = 1e-05
MASKED = -1e30
LANES = 128
PAIRS = -(-HEADS // 2)
WIDE = PAIRS * LANES
SCALE = HEAD_DIM ** (-0.5)
NT = (((1,), (1,)), ((), ()))
TN = (((0,), (0,)), ((), ()))


def permute(value, axes, pairs):
    return lax.ppermute(value, axes, pairs)


def roll_ctx(value, steps):
    count = lax.axis_size("ctx")
    return permute(value, "ctx", [(s, (s + steps) % count) for s in range(count)])


def shift_ctx(value, steps, first, last):
    return permute(value, "ctx", [(s, s + steps) for s in range(first, last)])


def roll_ctx_by_rep(value, steps):
    count = lax.axis_size("ctx")
    pairs = [
        (rep * count + s, rep * count + (s + steps[rep]) % count)
        for rep in range(len(steps))
        for s in range(count)
    ]
    return permute(value, ("rep", "ctx"), pairs)


def roll_y(value, steps):
    count = lax.axis_size("dat")
    return permute(value, "dat", [(s, (s + 2 * steps) % count) for s in range(count)])


def swap_dat(value, bit):
    count = lax.axis_size("dat")
    return permute(value, "dat", [(s, s ^ bit) for s in range(count)])


def swap_rep(value):
    return permute(value, "rep", [(0, 1), (1, 0)])


def norm_forward(values, gain, shift):
    average = jnp.mean(values, axis=-1, keepdims=True)
    centred = values - average
    variance = jnp.mean(centred * centred, axis=-1, keepdims=True)
    inverse = lax.rsqrt(variance + EPS)
    normal = centred * inverse
    return (normal * gain + shift, normal, inverse)


def norm_backward(grad_out, gain, normal, inverse):
    scaled = grad_out * gain
    first = jnp.mean(scaled, axis=-1, keepdims=True)
    second = jnp.mean(scaled * normal, axis=-1, keepdims=True)
    return inverse * (scaled - first - normal * second)


def dot(left, right):
    return jnp.dot(left, right, preferred_element_type=jnp.float32)


def dot_cols(left, right):
    return lax.dot_general(left, right, NT, preferred_element_type=jnp.float32)


def low(value):
    return value.astype(jnp.bfloat16)


def wide(value):
    return value.astype(jnp.float32)


def pick(stacked, index):
    return lax.dynamic_index_in_dim(stacked, index, axis=0, keepdims=False)


def stage(run, ready, sends):
    count = len(ready)
    flat = lax.optimization_barrier((*ready, *[value for value, _ in sends]))
    outs = run(*flat[:count])
    moved = [move(value) for (_, move), value in zip(sends, flat[count:])]
    flat = lax.optimization_barrier((*outs, *moved))
    return (list(flat[: len(outs)]), list(flat[len(outs) :]))


def after(value, *others):
    return lax.optimization_barrier((value, *others))[0]


def head_lanes(half, rows):
    lane = lax.broadcasted_iota(jnp.int32, (rows, LANES), 1)
    return (lane < HEAD_DIM) if half == 0 else (lane >= HEAD_DIM)


def forward_kernel(sub, q_ref, kv_ref, bias_ref, out_ref, out32_ref, log_ref):
    rows = q_ref.shape[0]
    span = WINDOW + sub
    reach = kv_ref.shape[1] - rows
    for n in range(rows // sub):
        r0 = n * sub
        k0 = reach - WINDOW + r0
        keys = kv_ref[0, k0 : k0 + span, :]
        values = kv_ref[1, k0 : k0 + span, :]
        bias = bias_ref[r0 : r0 + sub, k0 : k0 + span]
        parts = []
        for half in range(2):
            query = jnp.where(
                head_lanes(half, sub), q_ref[r0 : r0 + sub, :] * jnp.bfloat16(SCALE), jnp.bfloat16(0)
            )
            scores = lax.dot_general(query, keys, NT, preferred_element_type=jnp.float32) + bias
            top = jnp.max(scores, axis=1, keepdims=True)
            weights = jnp.exp(scores - top)
            total = jnp.sum(weights, axis=1, keepdims=True)
            summed = jnp.dot(
                weights.astype(jnp.bfloat16), values, preferred_element_type=jnp.float32
            )
            parts.append((summed / total, top + jnp.log(total)))
        first = head_lanes(0, sub)
        out = jnp.where(first, parts[0][0], parts[1][0])
        out_ref[r0 : r0 + sub, :] = out.astype(jnp.bfloat16)
        out32_ref[r0 : r0 + sub, :] = out
        log_ref[r0 : r0 + sub, :] = jnp.where(first, parts[0][1], parts[1][1])


def sub_rows(rows):
    return 256 if rows % 256 == 0 else rows


def pair_block(rows):
    return pl.BlockSpec((rows, LANES), lambda h: (0, h))


def kv_block(rows):
    return pl.BlockSpec((2, rows, LANES), lambda h: (0, 0, h))


def attention_forward(query, kv, bias):
    rows, span = (query.shape[0], kv.shape[1])
    sub = sub_rows(rows)
    return pl.pallas_call(
        functools.partial(forward_kernel, sub),
        grid=(PAIRS,),
        in_specs=[
            pair_block(rows),
            kv_block(span),
            pl.BlockSpec((rows, span), lambda h: (0, 0)),
        ],
        out_specs=[pair_block(rows)] * 3,
        out_shape=[
            jax.ShapeDtypeStruct((rows, WIDE), kind)
            for kind in (jnp.bfloat16, jnp.float32, jnp.float32)
        ],
        compiler_params=pltpu.CompilerParams(vmem_limit_bytes=48 << 20),
        cost_estimate=hint(),
    )(query, kv, bias)


def backward_kernel(
    sub,
    q_ref,
    kv_ref,
    da_ref,
    attended_ref,
    log_ref,
    bias_ref,
    *refs,
):
    out_ref, sum_k_ref, sum_v_ref = refs[-3:]
    rows = q_ref.shape[0]
    span = WINDOW + sub
    reach = kv_ref.shape[1] - rows
    sum_k_ref[...] = jnp.zeros_like(sum_k_ref)
    sum_v_ref[...] = jnp.zeros_like(sum_v_ref)
    for n in range(rows // sub):
        r0 = n * sub
        k0 = reach - WINDOW + r0
        all_da = da_ref[r0 : r0 + sub, :]
        product = jnp.transpose(all_da.astype(jnp.float32) * attended_ref[r0 : r0 + sub, :])
        logs = jnp.transpose(log_ref[r0 : r0 + sub, :])
        all_query = q_ref[r0 : r0 + sub, :] * jnp.bfloat16(SCALE)
        keys = kv_ref[0, k0 : k0 + span, :]
        values = kv_ref[1, k0 : k0 + span, :]
        bias = bias_ref[k0 : k0 + span, r0 : r0 + sub]
        d_query = []
        for half in range(2):
            mask = head_lanes(half, sub)
            query = jnp.where(mask, all_query, jnp.bfloat16(0))
            da = jnp.where(mask, all_da, jnp.bfloat16(0))
            h0 = half * HEAD_DIM
            inner = jnp.sum(product[h0 : h0 + HEAD_DIM, :], axis=0, keepdims=True)
            log = logs[h0 : h0 + 1, :]
            scores = lax.dot_general(keys, query, NT, preferred_element_type=jnp.float32) + bias
            probs = jnp.exp(scores - log)
            d_probs = lax.dot_general(values, da, NT, preferred_element_type=jnp.float32)
            d_scores = (probs * (d_probs - inner)).astype(jnp.bfloat16)
            sum_v_ref[k0 : k0 + span, :] += jnp.dot(
                probs.astype(jnp.bfloat16), da, preferred_element_type=jnp.float32
            )
            sum_k_ref[k0 : k0 + span, :] += jnp.dot(
                d_scores, query, preferred_element_type=jnp.float32
            )
            d_query.append(
                lax.dot_general(d_scores, keys, TN, preferred_element_type=jnp.float32)
            )
        merged = jnp.where(head_lanes(0, sub), d_query[0], d_query[1])
        out_ref[out_ref.shape[0] - 1, r0 : r0 + sub, :] = (merged * SCALE).astype(jnp.bfloat16)
    count = out_ref.shape[0] // 2
    out_ref[:count] = sum_k_ref[...].astype(jnp.bfloat16).reshape(count, rows, LANES)
    out_ref[count : 2 * count] = sum_v_ref[...].astype(jnp.bfloat16).reshape(count, rows, LANES)


def attention_backward(query, kv, d_attended, attended, logs, bias, first, last, earlier=()):
    rows, span = (query.shape[0], kv.shape[1])
    count = 2 * (span // rows) + 1
    sub = sub_rows(rows)
    pair = pl.BlockSpec((rows, LANES), lambda h: (0, h + first))
    both = pl.BlockSpec((2, span, LANES), lambda h: (0, 0, h + first))
    return pl.pallas_call(
        functools.partial(backward_kernel, sub),
        grid=(last - first,),
        in_specs=[
            pair,
            both,
            pair,
            pair,
            pair,
            pl.BlockSpec((span, rows), lambda h: (0, 0)),
            *[pl.BlockSpec(memory_space=pl.ANY)] * len(earlier),
        ],
        out_specs=pl.BlockSpec((count, rows, LANES), lambda h: (0, 0, h + first)),
        out_shape=jax.ShapeDtypeStruct((count, rows, WIDE), jnp.bfloat16),
        input_output_aliases={6 + n: n for n in range(len(earlier))},
        scratch_shapes=[pltpu.VMEM((span, LANES), jnp.float32)] * 2,
        compiler_params=pltpu.CompilerParams(vmem_limit_bytes=48 << 20),
        cost_estimate=hint(),
    )(query, kv, d_attended, attended, logs, bias, *earlier)


def row_chunks(rows):
    step = 256 if rows % 256 == 0 else rows
    return [slice(n, n + step) for n in range(0, rows, step)]


def lane_block(cols, full):
    return min(full, full_lanes(cols))


def params(megabytes=56):
    return pltpu.CompilerParams(vmem_limit_bytes=megabytes << 20)


def hint():
    return pl.CostEstimate(flops=1 << 20, bytes_accessed=1 << 20, transcendentals=0)


def full_lanes(cols):
    return -(-cols // LANES) * LANES


def store_wide(ref, at, value):
    cols, full = (value.shape[1], ref.shape[-1])
    ref[(*at, slice(0, cols))] = value.astype(ref.dtype)
    if cols < full:
        ref[(*at, slice(cols, full))] = jnp.zeros((value.shape[0], full - cols), ref.dtype)


def assemble_kernel(cols, blocks_ref, qkv_ref, out_ref):
    count, rows, full = blocks_ref.shape
    fill = jnp.zeros((rows, WIDE - D), qkv_ref.dtype)

    def fill_in(write, start, stop, skip, size):
        for j in range(count):
            first, last = (max(start, j * size), min(stop, (j + 1) * size))
            if first < last:
                cut = slice(skip + first - j * size, skip + last - j * size)
                write(slice(first - start, last - start), blocks_ref[j, :, cut])

    for n in range(3):

        def write(cut, value, n=n):
            qkv_ref[n, :, cut] = value

        fill_in(write, n * D, (n + 1) * D, 0, cols)
        qkv_ref[n, :, D:] = fill

    def write_out(cut, value):
        out_ref[:, cut] = value

    fill_in(write_out, 0, D, cols, full - cols)


def assemble(blocks, cols):
    count, rows, full = blocks.shape
    step = 320 if rows % 320 == 0 else rows
    return pl.pallas_call(
        functools.partial(assemble_kernel, cols),
        grid=(rows // step,),
        in_specs=[pl.BlockSpec((count, step, full), lambda n: (0, n, 0))],
        out_specs=[
            pl.BlockSpec((3, step, WIDE), lambda n: (0, n, 0)),
            pl.BlockSpec((step, D), lambda n: (n, 0)),
        ],
        out_shape=[
            jax.ShapeDtypeStruct((3, rows, WIDE), blocks.dtype),
            jax.ShapeDtypeStruct((rows, D), blocks.dtype),
        ],
        compiler_params=params(),
        cost_estimate=hint(),
    )(blocks)


def project_kernel(x_ref, w_ref, bias_ref, *refs):
    out_ref = refs[-1]
    total = jnp.dot(x_ref[...], w_ref[0], preferred_element_type=jnp.float32)
    out_ref[0] = (total + bias_ref[0]).astype(out_ref.dtype)


def project_own_kernel(x_ref, w_ref, bias_ref, q_ref, kv_ref):
    total = jnp.dot(x_ref[...], w_ref[0], preferred_element_type=jnp.float32)
    total = (total + bias_ref[0]).astype(q_ref.dtype)

    @pl.when(pl.program_id(0) == 0)
    def _():
        q_ref[...] = total

    @pl.when(pl.program_id(0) > 0)
    def _():
        kv_ref[0] = total


def project_own(x, weights, bias, reach):
    rows, depth = x.shape
    full = weights.shape[2]
    return pl.pallas_call(
        project_own_kernel,
        grid=(3,),
        in_specs=[
            pl.BlockSpec((rows, depth), lambda t: (0, 0)),
            pl.BlockSpec((1, depth, full), lambda t: (t, 0, 0)),
            pl.BlockSpec((1, 1, full), lambda t: (t, 0, 0)),
        ],
        out_specs=[
            pl.BlockSpec((rows, full), lambda t: (0, 0)),
            pl.BlockSpec((1, rows, full), lambda t: (jnp.maximum(t - 1, 0), reach, 0)),
        ],
        out_shape=[
            jax.ShapeDtypeStruct((rows, full), jnp.bfloat16),
            jax.ShapeDtypeStruct((2, (reach + 1) * rows, full), jnp.bfloat16),
        ],
        compiler_params=params(),
        cost_estimate=hint(),
    )(x, weights, bias[:, None, :])


def project_earlier(x, weights, bias, kv, at):
    rows, depth = x.shape
    full = weights.shape[2]
    return pl.pallas_call(
        project_kernel,
        grid=(2,),
        in_specs=[
            pl.BlockSpec((rows, depth), lambda p: (0, 0)),
            pl.BlockSpec((1, depth, full), lambda p: (p + 1, 0, 0)),
            pl.BlockSpec((1, 1, full), lambda p: (p + 1, 0, 0)),
            pl.BlockSpec(memory_space=pl.ANY),
        ],
        out_specs=pl.BlockSpec((1, rows, full), lambda p: (p, at, 0)),
        out_shape=jax.ShapeDtypeStruct(kv.shape, kv.dtype),
        input_output_aliases={3: 0},
        compiler_params=params(),
        cost_estimate=hint(),
    )(x, weights, bias[:, None, :], kv)


def norm_back_kernel(own_ref, top_ref, rest_ref, normal_ref, inverse_ref, gain_ref, dy_ref, *outs):
    wide_ref, low_ref, sums_ref = outs
    cols = own_ref.shape[1]
    upper = pl.program_id(0) < pl.num_programs(0) // 2
    got = jnp.where(upper, top_ref[:, :cols], rest_ref[:, :cols])
    grad = own_ref[...] + got.astype(jnp.float32)
    normal = normal_ref[...]
    product = grad * normal
    scaled = grad * gain_ref[...]
    first = jnp.mean(scaled, axis=1, keepdims=True)
    second = jnp.mean(scaled * normal, axis=1, keepdims=True)
    out = dy_ref[:, :cols].astype(jnp.float32) + inverse_ref[...] * (
        scaled - first - normal * second
    )
    rounded = out.astype(jnp.bfloat16)
    wide_ref[...] = out
    store_wide(low_ref, (slice(None),), rounded)
    parts = [product, grad, rounded.astype(jnp.float32)]
    sums = jnp.concatenate([jnp.sum(part, axis=0, keepdims=True) for part in parts], axis=0)

    @pl.when(pl.program_id(0) == 0)
    def _():
        sums_ref[...] = sums

    @pl.when(pl.program_id(0) > 0)
    def _():
        sums_ref[...] += sums


def norm_back(own, top, rest, normal, inverse, gain, dy):
    rows, cols = own.shape
    step = 128 if rows % 256 == 0 else rows // 2
    half = rows // step // 2
    block = lambda size: pl.BlockSpec((step, size), lambda n: (n, 0))
    return pl.pallas_call(
        norm_back_kernel,
        grid=(rows // step,),
        in_specs=[
            block(cols),
            pl.BlockSpec((step, top.shape[1]), lambda n: (jnp.minimum(n, half - 1), 0)),
            pl.BlockSpec((step, rest.shape[1]), lambda n: (jnp.maximum(n - half, 0), 0)),
            block(cols),
            block(1),
            pl.BlockSpec((1, cols), lambda n: (0, 0)),
            block(dy.shape[1]),
        ],
        out_specs=[block(cols), block(WIDE), pl.BlockSpec((3, cols), lambda n: (0, 0))],
        out_shape=[
            jax.ShapeDtypeStruct((rows, cols), jnp.float32),
            jax.ShapeDtypeStruct((rows, WIDE), jnp.bfloat16),
            jax.ShapeDtypeStruct((3, cols), jnp.float32),
        ],
        compiler_params=params(),
        cost_estimate=hint(),
    )(own, top, rest, normal, inverse, gain[None], dy)


def unit_of(w_ref, cols):
    parts, _, rows, lanes = w_ref.shape
    return w_ref[:, 0].reshape(parts * rows, lanes)[:, :cols]


def unit_block(weights, cols, lane):
    parts, _, rows, full = weights.shape
    return pl.BlockSpec((parts, 1, rows, lane_block(cols, full)), lambda b: (0, b, 0, lane))


def ffn_kernel(x_ref, dy_ref, fc_ref, proj_ref, bias_ref, *refs):
    active_ref, d_hidden_ref, sum_ref, out_ref, total_ref = refs[-5:]
    step = pl.program_id(0)
    cols = bias_ref.shape[2]
    first, second = (0.7978845608028654, 0.044715)
    weight = unit_of(fc_ref, cols)
    depth = weight.shape[0]
    u = jnp.dot(x_ref[:, :depth], weight, preferred_element_type=jnp.float32) + bias_ref[0]
    square = u * u
    t = jnp.tanh(first * u * (1.0 + second * square))
    half = 0.5 * (1.0 + t)
    store_wide(active_ref, (0, slice(None)), u * half)
    slope = half + (0.5 * first) * u * (1.0 - t * t) * (1.0 + (3.0 * second) * square)
    d_active = jnp.dot(
        dy_ref[:, :depth], unit_of(proj_ref, cols), preferred_element_type=jnp.float32
    )
    d_hidden = (d_active * slope).astype(jnp.bfloat16)
    store_wide(d_hidden_ref, (0, slice(None)), d_hidden)
    sum_ref[0] = jnp.sum(d_hidden.astype(jnp.float32), axis=0, keepdims=True)
    part = lax.dot_general(d_hidden, weight, NT, preferred_element_type=jnp.float32)

    @pl.when(step == 0)
    def _():
        total_ref[...] = part

    @pl.when(step > 0)
    def _():
        total_ref[...] += part

    @pl.when(step == pl.num_programs(0) - 1)
    def _():
        store_wide(out_ref, (slice(None),), total_ref[...])


def feed_forward(x, dy, fc, proj, lane, bias, part, kind, earlier=()):
    count, cols = bias.shape
    rows = x.shape[0]
    lanes = full_lanes(cols)
    out_cols = WIDE if kind == jnp.bfloat16 else D
    mine = pl.BlockSpec((1, rows, lanes), lambda b: (b, part, 0))
    units = jax.ShapeDtypeStruct((count, 2 * rows, lanes), jnp.bfloat16)
    return pl.pallas_call(
        ffn_kernel,
        grid=(count,),
        in_specs=[
            pl.BlockSpec(x.shape, lambda b: (0, 0)),
            pl.BlockSpec(dy.shape, lambda b: (0, 0)),
            unit_block(fc, cols, 0),
            unit_block(proj, cols, lane),
            pl.BlockSpec((1, 1, cols), lambda b: (b, 0, 0)),
            *[pl.BlockSpec(memory_space=pl.ANY)] * len(earlier),
        ],
        out_specs=[
            mine,
            mine,
            pl.BlockSpec((1, 1, cols), lambda b: (b, 0, 0)),
            pl.BlockSpec((rows, out_cols), lambda b: (0, 0)),
        ],
        out_shape=[
            units,
            units,
            jax.ShapeDtypeStruct((count, 1, cols), jnp.float32),
            jax.ShapeDtypeStruct((rows, out_cols), kind),
        ],
        input_output_aliases={5 + n: n for n in range(len(earlier))},
        scratch_shapes=[pltpu.VMEM((rows, D), jnp.float32)],
        compiler_params=params(),
        cost_estimate=hint(),
    )(x, dy, fc, proj, bias[:, None, :], *earlier)


def back_kernel(cols, x_ref, w_ref, out_ref, sum_ref):
    step = pl.program_id(0)
    part = lax.dot_general(
        x_ref[0][:, :cols], unit_of(w_ref, cols), NT, preferred_element_type=jnp.float32
    )

    @pl.when(step == 0)
    def _():
        sum_ref[...] = part

    @pl.when(step > 0)
    def _():
        sum_ref[...] += part

    @pl.when(step == pl.num_programs(0) - 1)
    def _():
        store_wide(out_ref, (slice(None),), sum_ref[...])


def ffn_back(x, weights, cols, lane, part, rows, kind):
    count = x.shape[0]
    width = weights.shape[0] * weights.shape[2]
    out_cols = WIDE if kind == jnp.bfloat16 else width
    return pl.pallas_call(
        functools.partial(back_kernel, cols),
        grid=(count,),
        in_specs=[
            pl.BlockSpec((1, rows, x.shape[2]), lambda b: (b, part, 0)),
            unit_block(weights, cols, lane),
        ],
        out_specs=pl.BlockSpec((rows, out_cols), lambda b: (0, 0)),
        out_shape=jax.ShapeDtypeStruct((rows, out_cols), kind),
        scratch_shapes=[pltpu.VMEM((rows, width), jnp.float32)],
        compiler_params=params(),
        cost_estimate=hint(),
    )(x, weights)


def index_list(parts):
    return jnp.stack([jnp.asarray(part, jnp.int32) for part in parts])


def split_specs(count, ny, rows, cols):
    half = count // 2
    block = (1, rows, cols)
    specs = [pl.BlockSpec(block, lambda g, a, b: (g, 0, 0))]
    shapes = [jax.ShapeDtypeStruct((count, rows, cols), jnp.bfloat16)]
    for _ in range(1, ny):
        specs.append(pl.BlockSpec(block, lambda g, a, b: (jnp.minimum(g, half - 1), 0, 0)))
        specs.append(pl.BlockSpec(block, lambda g, a, b: (jnp.maximum(g - half, 0), 0, 0)))
        for size in (half, count - half):
            shapes.append(jax.ShapeDtypeStruct((size, rows, cols), jnp.bfloat16))
    return (specs, shapes)


def store_split(outs, q, value):
    value = value.astype(jnp.bfloat16)
    if q == 0:
        outs[0][0] = value
        return
    step = pl.program_id(0)
    half = pl.num_programs(0) // 2

    @pl.when(step < half)
    def _():
        outs[2 * q - 1][0] = value

    @pl.when(step >= half)
    def _():
        outs[2 * q][0] = value


def by_left_kernel(ny, at_r, at_q, left_ref, *refs):
    rights, gots, outs = (refs[:ny], refs[ny : 2 * ny], refs[2 * ny :])
    depth = rights[0].shape[1]
    cols = outs[0].shape[2]
    left = left_ref[0]
    for q in range(ny):
        total = jnp.dot(
            left[:, :depth], rights[q][0][:, :cols], preferred_element_type=jnp.float32
        )
        total += jnp.dot(left[:, depth:], gots[q][0][:, :cols], preferred_element_type=jnp.float32)
        store_split(outs, q, total)


def grads_by_left(left, right, got, cols, at_r, at_q):
    count, (_, rows, depth), (_, half, lanes) = (at_r.size, left.shape, right.shape)
    ny = at_q.size
    own = lambda q: pl.BlockSpec((1, half, lanes), lambda r, a, b: (b[q], 0, 0))
    out_specs, out_shape = split_specs(count, ny, rows, cols)
    return pl.pallas_call(
        functools.partial(by_left_kernel, ny),
        grid_spec=pltpu.PrefetchScalarGridSpec(
            num_scalar_prefetch=2,
            grid=(count,),
            in_specs=[
                pl.BlockSpec((1, rows, depth), lambda r, a, b: (a[r], 0, 0)),
                *[own(q) for q in range(ny)] * 2,
            ],
            out_specs=out_specs,
        ),
        out_shape=out_shape,
        compiler_params=params(),
        cost_estimate=hint(),
    )(at_r, at_q, left, *[right] * ny, *[got] * ny)


def by_right_kernel(ny, at_r, at_q, right_ref, right_got_ref, *refs):
    lefts, gots, outs = (refs[:ny], refs[ny : 2 * ny], refs[2 * ny :])
    cols = outs[0].shape[2]
    right, right_got = (right_ref[0][:, :cols], right_got_ref[0][:, :cols])
    for q in range(ny):
        total = jnp.dot(lefts[q][0], right, preferred_element_type=jnp.float32)
        total += jnp.dot(gots[q][0], right_got, preferred_element_type=jnp.float32)
        store_split(outs, q, total)


def grads_by_right(left, left_got, right, right_got, cols, at_r, at_q):
    count, (_, rows, depth) = (at_r.size, left.shape)
    ny = at_q.size
    own = lambda q: pl.BlockSpec((1, rows, depth), lambda r, a, b: (b[q], 0, 0))
    moving = pl.BlockSpec((1, depth, right.shape[2]), lambda r, a, b: (a[r], 0, 0))
    out_specs, out_shape = split_specs(count, ny, rows, cols)
    return pl.pallas_call(
        functools.partial(by_right_kernel, ny),
        grid_spec=pltpu.PrefetchScalarGridSpec(
            num_scalar_prefetch=2,
            grid=(count,),
            in_specs=[
                moving,
                moving,
                *[own(q) for q in range(ny)] * 2,
            ],
            out_specs=out_specs,
        ),
        out_shape=out_shape,
        compiler_params=params(),
        cost_estimate=hint(),
    )(at_r, at_q, right, right_got, *[left] * ny, *[left_got] * ny)


def mixed_kernel(cols, count, at_r, at_q, q_ref, q_got_ref, kv_ref, kv_got_ref, *refs):
    lefts, gots, outs = (refs[:count], refs[count : 2 * count], refs[2 * count :])
    step = pl.program_id(0)
    nc = outs[0].shape[0] if len(outs) == 1 else len(outs)
    _, own, full = q_ref.shape
    for part, at_step in ((2, 0), (1, 1), (0, 2)):

        @pl.when(step == at_step)
        def _(part=part):
            for q, left_ref in enumerate(lefts):
                if part == 0:
                    first, second = (q_ref[0], q_got_ref[0])
                    left, got = (left_ref[0][:, -own:], gots[q][0][:, -own:])
                else:
                    first, second = (kv_ref[...].reshape(-1, full), kv_got_ref[...].reshape(-1, full))
                    left, got = (left_ref[0], gots[q][0])
                total = jnp.dot(left, first, preferred_element_type=jnp.float32)
                total += jnp.dot(got, second, preferred_element_type=jnp.float32)
                total = total.astype(jnp.bfloat16)
                for j in range(nc):
                    start, stop = (max(part * D, j * cols), min((part + 1) * D, (j + 1) * cols))
                    if start < stop:
                        cut = slice(start - j * cols, stop - j * cols)
                        value = total[:, start - part * D : stop - part * D]
                        if len(outs) == 1:
                            outs[0][at_r[j], q, :, cut] = value
                            continue
                        for role, out_ref in enumerate(outs):

                            @pl.when(at_r[j] == role)
                            def _(out_ref=out_ref, cut=cut, value=value, q=q):
                                out_ref[q, :, cut] = value


def grads_mixed(left, left_got, grads, grads_got, cols, places, at_q, qs):
    nc = places.size
    _, rows, depth = left.shape
    count, own_rows, wide_cols = grads.shape
    reach = count // 2
    own = lambda q: pl.BlockSpec((1, rows, depth), lambda t, a, b: (b[q], 0, 0))
    once = pl.Buffered(1)
    got = lambda q: pl.BlockSpec((1, rows, depth), lambda t, a, b: (q, 0, 0), pipeline_mode=once)
    query_block = pl.BlockSpec(
        (1, own_rows, wide_cols), lambda t, a, b: (count - 1, 0, 0), pipeline_mode=once
    )
    kv_block = pl.BlockSpec(
        (reach, own_rows, wide_cols), lambda t, a, b: (jnp.where(t == 0, 1, 0), 0, 0)
    )
    outs, shape = (nc, (len(qs), rows, cols)) if nc == 4 else (1, (nc, len(qs), rows, cols))
    return pl.pallas_call(
        functools.partial(mixed_kernel, cols, len(qs)),
        grid_spec=pltpu.PrefetchScalarGridSpec(
            num_scalar_prefetch=2,
            grid=(3,),
            in_specs=[
                query_block,
                query_block,
                kv_block,
                kv_block,
                *[own(q) for q in qs],
                *[got(q) for q in qs],
            ],
            out_specs=[pl.BlockSpec(shape, lambda t, a, b: (0,) * len(shape))] * outs,
        ),
        out_shape=[jax.ShapeDtypeStruct(shape, jnp.bfloat16)] * outs,
        compiler_params=params(60),
        cost_estimate=hint(),
    )(
        places,
        at_q,
        grads,
        grads_got,
        grads,
        grads_got,
        *[left] * len(qs),
        *[left_got] * len(qs),
    )


def sums_kernel(count, halo_refs, own_ref, normal_refs, q_ref, v_ref, out_ref):
    own = own_ref[...]
    parts = [ref[...].astype(jnp.float32) for ref in halo_refs] + [own]
    down = lambda value: jnp.sum(value, axis=0, keepdims=True)
    gain = sum(down(part * ref[...]) for part, ref in zip(parts, normal_refs))
    shift = sum(down(part) for part in parts)
    query = down(q_ref[0].astype(jnp.float32))
    values = sum(down(v_ref[n].astype(jnp.float32)) for n in range(count))
    fill = jnp.zeros((4, own.shape[1]), jnp.float32)
    out_ref[...] = jnp.concatenate([gain, shift, query, values, fill], axis=0)


def column_sums(halo, own, normals, grads):
    rows = own.shape[0]
    reach = len(normals) - 1
    count = reach + 1
    block = lambda n: pl.BlockSpec((rows, LANES), lambda c: (n, c))

    def kernel(*refs):
        halos, refs = (refs[:reach], refs[reach:])
        sums_kernel(count, halos, refs[0], refs[1 : count + 1], *refs[count + 1 :])

    return pl.pallas_call(
        kernel,
        grid=(PAIRS,),
        in_specs=[
            *[block(n) for n in range(reach)],
            block(0),
            *[block(0)] * count,
            pl.BlockSpec((1, rows, LANES), lambda c: (2 * count, 0, c)),
            pl.BlockSpec((count, rows, LANES), lambda c: (1, 0, c)),
        ],
        out_specs=pl.BlockSpec((8, LANES), lambda c: (0, c)),
        out_shape=jax.ShapeDtypeStruct((8, WIDE), jnp.float32),
        compiler_params=params(),
        cost_estimate=hint(),
    )(*[halo] * reach, own, *normals, grads, grads)


def out_kernel(cols, at_r, at_q, right_ref, right_got_ref, *refs):
    *lefts, got_ref, out_ref = refs
    full = out_ref.shape[0] * cols
    right, right_got = (right_ref[:, :full], right_got_ref[:, :full])
    for q, left_ref in enumerate(lefts):
        total = jnp.dot(left_ref[0], right, preferred_element_type=jnp.float32)
        total += jnp.dot(got_ref[q], right_got, preferred_element_type=jnp.float32)
        total = total.astype(jnp.bfloat16)
        for j in range(out_ref.shape[0]):
            out_ref[at_r[j], q] = total[:, j * cols : (j + 1) * cols]


def grads_out(left, left_got, right, right_got, cols, places, at_q):
    nc = places.size
    ny = at_q.size
    _, rows, depth = left.shape
    own = lambda q: pl.BlockSpec((1, rows, depth), lambda t, a, b: (b[q], 0, 0))
    right_block = pl.BlockSpec(right.shape, lambda t, a, b: (0, 0))
    return pl.pallas_call(
        functools.partial(out_kernel, cols),
        grid_spec=pltpu.PrefetchScalarGridSpec(
            num_scalar_prefetch=2,
            grid=(1,),
            in_specs=[
                right_block,
                right_block,
                *[own(q) for q in range(ny)],
                pl.BlockSpec((ny, rows, depth), lambda t, a, b: (0, 0, 0)),
            ],
            out_specs=pl.BlockSpec((nc, ny, rows, cols), lambda t, a, b: (0, 0, 0, 0)),
        ),
        out_shape=jax.ShapeDtypeStruct((nc, ny, rows, cols), jnp.bfloat16),
        compiler_params=params(),
        cost_estimate=hint(),
    )(
        places,
        at_q,
        right,
        right_got,
        *[left] * ny,
        left_got,
    )


def normed_kernel(q_ref, kv_ref, w_ref, own_ref, halo_ref, sum_ref):
    step = pl.program_id(0)
    count, own, _ = kv_ref.shape

    @pl.when(step == 0)
    def _():
        for n in range(count):
            sum_ref[n * own : (n + 1) * own, :] = lax.dot_general(
                kv_ref[n], w_ref[0], NT, preferred_element_type=jnp.float32
            )

    @pl.when(step == 1)
    def _():
        for n in range(count):
            rows = slice(n * own, (n + 1) * own)
            total = sum_ref[rows, :] + lax.dot_general(
                kv_ref[n], w_ref[0], NT, preferred_element_type=jnp.float32
            )
            if n < count - 1:
                store_wide(halo_ref, (rows,), total)
            else:
                sum_ref[rows, :] = total

    @pl.when(step == 2)
    def _():
        own_ref[...] = sum_ref[(count - 1) * own :, :] + lax.dot_general(
            q_ref[0], w_ref[0], NT, preferred_element_type=jnp.float32
        )


def normed_back(grads, weights):
    count, own, wide_cols = grads.shape
    reach = count // 2
    rows = (reach - 1) * own
    return pl.pallas_call(
        normed_kernel,
        grid=(3,),
        in_specs=[
            pl.BlockSpec((1, own, wide_cols), lambda t: (count - 1, 0, 0)),
            pl.BlockSpec((reach, own, wide_cols), lambda t: (jnp.where(t == 0, 1, 0), 0, 0)),
            pl.BlockSpec((1, D, wide_cols), lambda t: (2 - t, 0, 0)),
        ],
        out_specs=[
            pl.BlockSpec((own, D), lambda t: (0, 0)),
            pl.BlockSpec((rows, WIDE), lambda t: (0, 0)),
        ],
        out_shape=[
            jax.ShapeDtypeStruct((own, D), jnp.float32),
            jax.ShapeDtypeStruct((rows, WIDE), jnp.bfloat16),
        ],
        scratch_shapes=[pltpu.VMEM((reach * own, D), jnp.float32)],
        compiler_params=params(),
        cost_estimate=hint(),
    )(grads, grads, weights)


def place():
    nc, nd = (lax.axis_size("ctx"), lax.axis_size("dat"))
    ctx, dat = (lax.axis_index("ctx"), lax.axis_index("dat"))
    return (nc, nd, ctx, dat // 2, dat % 2)


def dat_of(q, other):
    _, nd, _, y, core = place()
    return 2 * ((y + q) % (nd // 2)) + (1 - core if other else core)


def ctx_of(r):
    nc, _, ctx, _, _ = place()
    return (ctx + r) % nc


def swap_core(value):
    return swap_dat(value, 1)


def ny_of():
    return lax.axis_size("dat") // 2


def sum_of(parts):
    total = wide(parts[0])
    for part in parts[1:]:
        total = total + wide(part)
    return total


def steps_of(nc):
    half = nc // 2
    out = [half]
    for n in range(1, half):
        out += [half + n, half - n]
    return [*out, 0]


class WholeSum:
    def __init__(self, blocks, nc):
        self.own, self.others = (blocks[0], blocks[1:])
        self.order = steps_of(nc)
        self.nc = nc
        self.sums = {}

    def y_sends(self, second):
        return [
            (part, functools.partial(roll_y, steps=q + 1))
            for q, part in enumerate(self.others[second::2])
        ]

    def take_y(self, moved, second):
        half = self.nc // 2
        for n, r in enumerate(self.order[half:] if second else self.order[:half]):
            parts = [part[n] for part in moved]
            self.sums[r] = low(sum_of([self.own[half * second + n], *parts]))

    def z_sends(self):
        half = self.nc // 2
        sends = [(self.sums[half], functools.partial(roll_ctx, steps=1))]
        if half + 1 < self.nc:
            sends.append((self.sums[half + 1], functools.partial(roll_ctx, steps=-1)))
        return sends

    def z_next(self, moved):
        half = self.nc // 2
        ahead = moved[0]
        for r in range(half - 1, 0, -1):
            ahead = low(sum_of([self.sums[r], ahead]))
            if r > 1:
                ahead = roll_ctx(ahead, 1)
        back = moved[1] if len(moved) > 1 else None
        for r in range(half + 2, self.nc):
            back = roll_ctx(low(sum_of([self.sums[r], back])), -1)
        self.back = back
        return [(ahead, functools.partial(roll_ctx, steps=1))]

    def total(self, moved):
        parts = [self.sums[0], moved[0]]
        if self.back is not None:
            parts.append(self.back)
        return low(sum_of(parts))


def mixed_places():
    nc, _, ctx, _, _ = place()
    rep = lax.axis_index("rep")
    quarter = nc // 4
    places = []
    for r in range(nc):
        if r == 0:
            places.append(nc - 1)
        elif r % 2 == 0:
            places.append(2 * quarter + r // 2 - 1)
        else:
            places.append(r // 4 + quarter * jnp.where(rep == r % 4 // 2, 1, 0))
    places = index_list(places)
    return index_list([places[(j - ctx) % nc] for j in range(nc)])


class MixedSum:
    def __init__(self, blocks):
        self.blocks = blocks
        self.nc, self.ny = (len(blocks[0]), len(blocks))
        self.quarter = self.nc // 4
        self.rep = lax.axis_index("rep")
        self.kept = {}
        self.sums = {}

    def even(self, r):
        return self.nc - 1 if r == 0 else 2 * self.quarter + r // 2 - 1

    def x_sends(self, qs):
        if len(qs) == self.ny:
            return [(jnp.stack([self.blocks[q][: self.quarter] for q in qs], axis=1), swap_rep)]
        return [(self.cut(q, 0), swap_rep) for q in qs]

    def cut(self, q, start):
        part = self.blocks[q][start : start + self.quarter]
        return jnp.stack(part) if isinstance(part, list) else part

    def take_x(self, moved, qs):
        for n, q in enumerate(qs):
            got = moved[0][:, q] if len(qs) == self.ny else moved[n]
            self.kept[q] = low(sum_of([self.cut(q, self.quarter), got]))

    def y_sends(self, steps):
        return [
            (self.blocks[q][self.even(r)], functools.partial(roll_y, steps=q))
            for r in steps
            for q in range(1, self.ny)
        ]

    def take_y(self, moved, steps):
        for n, r in enumerate(steps):
            parts = moved[n * (self.ny - 1) : (n + 1) * (self.ny - 1)]
            self.sums[r] = low(sum_of([self.blocks[0][self.even(r)], *parts]))

    def odd_y_sends(self):
        return [
            (self.kept[q], functools.partial(roll_y, steps=q)) for q in range(1, self.ny)
        ]

    def take_odd_y(self, moved):
        total = low(sum_of([self.kept[0], *moved]))
        for m in range(self.quarter):
            self.sums[4 * m + 1] = total[m]

    def all_y_sends(self):
        return [
            (
                jnp.concatenate([self.blocks[q][2 * self.quarter :], self.kept[q]], axis=0),
                functools.partial(roll_y, steps=q),
            )
            for q in range(1, self.ny)
        ]

    def take_all_y(self, moved):
        evens = self.nc // 2
        own = jnp.concatenate([self.blocks[0][2 * self.quarter :], self.kept[0]], axis=0)
        total = low(sum_of([own, *moved]))
        for n in range(evens):
            self.sums[2 * n + 2 if n < evens - 1 else 0] = total[n]
        for m in range(self.quarter):
            self.sums[4 * m + 1] = total[evens + m]

    def at(self, distance):
        if distance % 2 == 0:
            if 2 * distance == self.nc:
                return self.sums[distance]
            return jnp.where(self.rep == 0, self.sums[distance], self.sums[self.nc - distance])
        if distance % 4 == 1:
            return self.sums[distance]
        return None

    def move(self, value):
        return roll_ctx_by_rep(value, (1, -1))

    def z_sends(self):
        return [(self.at(self.nc - 2), self.move)]

    def z_next(self, moved):
        carried = moved[0]
        for distance in range(self.nc - 3, 0, -1):
            part = self.at(distance)
            carried = carried if part is None else low(sum_of([part, carried]))
            if distance > 1:
                carried = self.move(carried)
        return [(carried, self.move)]

    def total(self, moved):
        return low(sum_of([self.sums[0], moved[0]]))


class SmallSum:
    @staticmethod
    def prepare(parts):
        nc = lax.axis_size("ctx")
        return (jnp.concatenate([part.reshape(nc, -1) for part in parts], axis=1),)

    def __init__(self, value, sizes):
        nc, nd, ctx, _, _ = place()
        self.sizes = [size // nc for size in sizes]
        self.value = value
        self.ctx = ctx
        self.left = []
        bit = nc // 2
        while bit:
            self.left.append(("ctx", bit))
            bit //= 2
        bit = 1
        while bit < nd:
            self.left.append(("dat", bit))
            bit *= 2
        self.left.append(("rep", 1))

    def sends(self):
        axis, bit = self.left[0]
        count = lax.axis_size(axis)
        pairs = [(s, s ^ bit) for s in range(count)]
        if axis != "ctx":
            return [(self.value, lambda value: permute(value, axis, pairs))]
        halves = self.value.reshape(2, bit, -1)
        mine = (self.ctx // bit) % 2
        self.value = pick(halves, mine)
        return [(pick(halves, 1 - mine), lambda value: permute(value, axis, pairs))]

    def take(self, moved):
        self.left.pop(0)
        self.value = self.value + moved[0].reshape(self.value.shape)

    def finish(self):
        while self.left:
            self.take([move(value) for value, move in self.sends()])
        value = self.value.reshape(-1)
        outs, at = ([], 0)
        for size in self.sizes:
            outs.append(value[at : at + size])
            at += size
        return outs


def gather_small(vector):
    nc, _, ctx, _, _ = place()
    out = jnp.zeros((nc,) + vector.shape, vector.dtype)
    for r in range(nc):
        part = roll_ctx(vector, r) if r else vector
        out = lax.dynamic_update_index_in_dim(out, part, (ctx - r) % nc, 0)
    return out


def pad_cols(value):
    return jnp.pad(value, ((0, 0), (0, WIDE - value.shape[1])))


def regroup(units, count):
    have, rows, cols = units.shape
    if have == count:
        return units
    if have > count:
        per = have // count
        return units.reshape(count, per, rows, cols).swapaxes(1, 2).reshape(count, rows, -1)
    per = count // have
    return units.reshape(have, rows, per, cols // per).swapaxes(1, 2).reshape(count, rows, -1)


def regroup_wide(units, cols, count):
    if units.shape[0] == count:
        return units
    value = regroup(units[:, :, :cols], count)
    return jnp.pad(value, ((0, 0), (0, 0), (0, full_lanes(value.shape[2]) - value.shape[2])))


def local(
    tokens,
    segments,
    cotangent,
    ln1_gain,
    ln1_bias,
    w_qkv,
    b_qv,
    w_out,
    b_out,
    ln2_gain,
    ln2_bias,
    w_fc,
    b_fc,
    w_proj,
    b_proj,
):
    nc, nd, ctx, y, core = place()
    rep = lax.axis_index("rep")
    ff = w_fc.shape[1] * nc
    row_count = tokens.shape[1]
    reach_count = -(-WINDOW // row_count)
    reach_rows = reach_count * row_count

    blocks = max(nc, nd)
    width = ff // blocks // 2
    per_b, per_c = (blocks // nc, blocks // nd)
    qkv_cols, out_cols = (w_qkv.shape[1], w_out.shape[1])
    fc_cols = per_b * width

    small_all = gather_small(
        low(jnp.concatenate([ln1_gain, ln1_bias, b_qv, b_out, ln2_gain, ln2_bias, b_fc, b_proj]))
    )
    smalls, at = ([], 0)
    for part in (ln1_gain, ln1_bias, b_qv, b_out, ln2_gain, ln2_bias, b_fc, b_proj):
        size = part.shape[0]
        smalls.append(wide(small_all[:, at : at + size].reshape(-1)))
        at += size
    gain_one, shift_one, bias_qv, bias_out, gain_two, shift_two, bias_fc, bias_proj = smalls
    bias_half = bias_fc.reshape(blocks, 2, width)
    bias_half = lax.dynamic_index_in_dim(bias_half, rep, axis=1, keepdims=False)

    inputs = wide(tokens[0])
    d_ffn = cotangent[0]
    d_ffn_wide = pad_cols(d_ffn)
    d_ffn_got = swap_rep(d_ffn_wide)
    d_ffn_pair = jnp.concatenate([d_ffn_wide, d_ffn_got], axis=0)
    d_ffn_quad = jnp.concatenate([d_ffn_pair, swap_core(d_ffn_pair)], axis=0)[:, :D]
    d_ffn_quad = d_ffn_quad.T.reshape(nc, D // nc, -1)
    order = steps_of(nc)
    at_ctx = index_list([ctx_of(r) for r in order])
    at_own = index_list([dat_of(q, False) for q in range(nd // 2)])
    at_other = [dat_of(q, True) for q in range(nd // 2)]
    places = mixed_places()
    at_ctx, at_own, places, d_ffn_quad = lax.optimization_barrier(
        (at_ctx, at_own, places, d_ffn_quad)
    )

    def from_other_core(stacked):
        return swap_core(jnp.stack([pick(stacked, at) for at in at_other]))

    shard_a = jnp.concatenate([low(w_qkv), low(w_out)], axis=1)
    full_a = lax.all_gather(shard_a, ("ctx", "dat"), axis=0, tiled=True)
    full_a = full_a.reshape(nc, D, qkv_cols + out_cols)
    normed_own, normal_own, inverse_own = norm_forward(inputs, gain_one, shift_one)
    normed_own = low(normed_own)
    full_a = after(full_a, normed_own, d_ffn_quad)

    segment_row = segments[0]
    padded_segment = jnp.concatenate([jnp.full((reach_rows,), -1, jnp.int32), segment_row])
    key_segment = lax.dynamic_slice_in_dim(padded_segment, ctx * row_count, reach_rows + row_count)
    query_segment = lax.dynamic_slice_in_dim(segment_row, ctx * row_count, row_count)
    query_position = reach_rows + jnp.arange(row_count, dtype=jnp.int32)
    key_position = jnp.arange(reach_rows + row_count, dtype=jnp.int32)

    def mask(at_query, at_key):
        visible = (
            (at_query(query_segment) == at_key(key_segment))
            & (at_key(key_position) <= at_query(query_position))
            & (at_key(key_position) > at_query(query_position) - WINDOW)
        )
        return jnp.where(visible, 0.0, MASKED)

    as_column, as_row = (lambda v: v[:, None], lambda v: v[None, :])
    bias_forward, bias_back = (mask(as_column, as_row), mask(as_row, as_column))
    left_own = normed_own.T

    fc_half = lax.dynamic_index_in_dim(
        low(w_fc).reshape(-1, per_b, 2, width), rep, axis=2, keepdims=False
    ).reshape(-1, fc_cols)
    proj_half = lax.dynamic_index_in_dim(
        low(w_proj).reshape(per_c, 2, width, -1), rep, axis=1, keepdims=False
    ).reshape(per_c * width, -1)
    proj_half = proj_half.T
    shard_b = None
    if nc == nd:
        fill = jnp.zeros((fc_half.shape[0], full_lanes(width) - width), jnp.bfloat16)
        shard_b = jnp.concatenate([fc_half, fill, proj_half, fill], axis=1)
        full_a = after(full_a, shard_b)
    tokens_wide, normed_own, full_a, bias_forward, bias_back, left_own = lax.optimization_barrier(
        (pad_cols(tokens[0]), normed_own, full_a, bias_forward, bias_back, left_own)
    )
    bias_qkv = pad_cols(jnp.stack([bias_qv[:D], jnp.zeros((D,), jnp.float32), bias_qv[D:]]))

    def first_weights(weights, x):
        weights_qkv, weight_out = assemble(weights, qkv_cols)
        return (weights_qkv, weight_out, *project_own(x, weights_qkv, bias_qkv, reach_count))

    (weights_qkv, weight_out, query, kv), (halo,) = stage(
        first_weights,
        [full_a, normed_own],
        [(tokens_wide, functools.partial(shift_ctx, steps=1, first=0, last=nc - 1))],
    )
    normed_halo, normal_halo = ([], [])
    for n in range(reach_count):

        def next_block(tokens_of, kv, n=n):
            normed, normal, _ = norm_forward(wide(tokens_of[:, :D]), gain_one, shift_one)
            normed = low(normed)
            at = reach_count - 1 - n
            return (normed, normal, project_earlier(normed, weights_qkv, bias_qkv, kv, at))

        more = n + 1 < reach_count
        (normed, normal, kv), moved = stage(
            next_block,
            [halo, kv],
            [(halo, functools.partial(shift_ctx, steps=1, first=n + 1, last=nc - 1))] * more,
        )
        normed_halo.insert(0, normed)
        normal_halo.insert(0, normal)
        halo = moved[0] if more else halo
    normed_earlier = jnp.concatenate(normed_halo, axis=0)

    if nc == nd:
        shard_b = after(shard_b, small_all, halo)
        gathered = [lax.all_gather(shard_b, ("ctx", "dat"), axis=0, tiled=True)]
    else:
        gathered = [
            lax.all_gather(fc_half, ("ctx", "dat"), axis=0, tiled=True),
            lax.all_gather(proj_half, ("dat", "ctx"), axis=0, tiled=True),
        ]

    attended, attended_wide, logs = attention_forward(query, kv, bias_forward)
    resid = inputs + dot(attended[:, :D], weight_out) + bias_out
    normed_two, normal_two, inverse_two = norm_forward(resid, gain_two, shift_two)
    normed_two = pad_cols(low(normed_two))

    left_one = jnp.concatenate([normed_earlier.T, left_own], axis=1).reshape(nd, D // nd, -1)
    left_out = attended[:, :D].T.reshape(nd, D // nd, -1)
    left_one_got = from_other_core(left_one)
    left_out_got = from_other_core(left_out)
    gathered = [after(part, normed_two, left_one_got, left_out_got) for part in gathered]
    if nc == nd:
        units_proj = gathered[0].reshape(nc, nd, D // nd, -1)
        units_fc = gathered[0].reshape(1, nc, D, -1)
        lane_proj = 1
    else:
        units_fc = regroup(gathered[0].reshape(nc, D, -1), blocks)[None]
        units_proj = regroup(gathered[1].reshape(nd, D, -1), blocks)[None]
        lane_proj = 0

    (active, d_hidden, sums_own, d_normed_own), (normed_two_got,) = stage(
        lambda x: feed_forward(
            x, d_ffn_wide, units_fc, units_proj, lane_proj, bias_half, 0, jnp.float32
        ),
        [normed_two],
        [(normed_two, swap_rep)],
    )
    active, d_hidden, sums_theirs, d_theirs = feed_forward(
        normed_two_got,
        d_ffn_got,
        units_fc,
        units_proj,
        lane_proj,
        bias_half,
        1,
        jnp.bfloat16,
        (active, d_hidden),
    )
    grad_bias_fc = sums_own + sums_theirs
    active_dat = regroup_wide(active, width, nd)
    d_hidden_ctx = regroup_wide(d_hidden, width, nc)
    ny = ny_of()

    def turn(own, got):
        return (jnp.concatenate([own, got], axis=0)[:, :D].T.reshape(nd, D // nd, -1),)

    cut = row_count // 2
    (left_two,), (active_got,) = stage(
        turn,
        [normed_two, normed_two_got],
        [
            (active_dat, swap_core),
        ],
    )
    blocks_proj, (d_hidden_got, left_two_got, got_first) = stage(
        lambda x: grads_by_left(d_ffn_quad, x, active_got, per_c * width, at_ctx, at_own),
        [active_dat],
        [
            (d_hidden_ctx, swap_core),
            (left_two, swap_core),
            (d_theirs[:cut], swap_rep),
        ],
    )
    proj = WholeSum(blocks_proj, nc)

    def second_blocks(x, active):
        blocks_fc = grads_by_right(
            left_two, left_two_got, x, d_hidden_got, fc_cols, at_ctx, at_own
        )
        active = after(active, blocks_fc[0])
        return (
            ffn_back(active, units_proj, width, lane_proj, 1, row_count, jnp.bfloat16),
            *blocks_fc,
        )

    (ffn_theirs, *blocks_fc), (got_second, *moved) = stage(
        second_blocks,
        [d_hidden_ctx, active],
        [(d_theirs[cut:], swap_rep), *proj.y_sends(0)],
    )
    proj.take_y(moved, 0)
    fc = WholeSum(blocks_fc, nc)

    def to_branch(x, top, rest):
        d_resid, d_branch, sums = norm_back(
            x, top, rest, normal_two, inverse_two, gain_two, d_ffn_wide
        )
        d_attended = ffn_back(
            d_branch[None], weight_out[None, None], D, 0, 0, row_count, jnp.bfloat16
        )
        return (d_resid, d_branch, sums, d_attended)

    (d_resid, d_branch, sums_two, d_attended), moved = stage(
        to_branch,
        [d_normed_own, got_first, got_second],
        [*proj.y_sends(1), *proj.z_sends()],
    )
    proj.take_y(moved[: ny - 1], 1)
    proj_next = proj.z_next(moved[ny - 1 :])

    d_branch_got = swap_core(d_branch)
    middle = PAIRS // 2

    def first_heads(x, d_branch, d_branch_got):
        grads = attention_backward(query, kv, x, attended_wide, logs, bias_back, 0, middle)
        d_branch = after(d_branch, grads)
        blocks_out = grads_out(
            left_out, left_out_got, d_branch, d_branch_got, out_cols, places, at_own
        )
        return (grads, blocks_out)

    (grads, blocks_out), (ffn_first, *moved) = stage(
        first_heads,
        [d_attended, d_branch, d_branch_got],
        [(ffn_theirs[:cut], swap_rep), *fc.y_sends(0), *proj_next],
    )
    out = MixedSum([blocks_out[:, q] for q in range(ny)])
    fc.take_y(moved[: ny - 1], 0)
    proj_total = proj.total(moved[ny - 1 :])
    (grads,), moved = stage(
        lambda x, done: (
            attention_backward(
                query, kv, x, attended_wide, logs, bias_back, middle, PAIRS, [done]
            ),
        ),
        [d_attended, grads],
        [*fc.y_sends(1), *fc.z_sends(), *out.x_sends(range(ny))],
    )
    fc.take_y(moved[: ny - 1], 1)
    *moved, out_moved = moved[ny - 1 :]
    fc_next = fc.z_next(moved)
    out.take_x([out_moved], range(ny))

    (d_normed_own, d_normed_halo), (grads_got, *moved) = stage(
        lambda x: normed_back(x, weights_qkv),
        [grads],
        [
            (grads, swap_core),
            *fc_next,
            *out.all_y_sends(),
            (proj_total, swap_rep),
            (ffn_theirs[cut:], swap_rep),
        ],
    )
    fc_total = fc.total(moved[:1])
    *moved, proj_got, ffn_second = moved[1:]
    out.take_all_y(moved)
    returned = d_normed_halo[:row_count]
    for n in range(1, reach_count - 1):
        returned = shift_ctx(returned, -1, reach_count + 1 - n, nc)
        returned = low(sum_of([returned, d_normed_halo[n * row_count : (n + 1) * row_count]]))
    back_one = functools.partial(shift_ctx, steps=-1, first=min(2, reach_count), last=nc)
    back_two = functools.partial(shift_ctx, steps=-1, first=1, last=nc)
    again = reach_count > 1
    others = list(range(1, ny))
    evens = list(range(2, nc, 2))

    def blocks_of(qs):
        return lambda x: grads_mixed(
            left_one, left_one_got, x, grads_got, qkv_cols, places, at_own, qs
        )

    def by_q(parts, n):
        return [part[n] for part in parts] if len(parts) > 1 else parts[0][:, n]

    blocks_others, (back_first, fc_got, *moved) = stage(
        blocks_of(others),
        [grads],
        [(returned[:cut], back_one), (fc_total, swap_rep), *out.z_sends()],
    )
    out_next = out.z_next(moved)
    parts = [by_q(blocks_others, n) for n in range(ny - 1)]
    qkv = MixedSum([parts[0], *parts])
    blocks_first, moved = stage(
        blocks_of([0]),
        [after(grads, blocks_others[0])],
        [
            *qkv.x_sends(others),
            *qkv.y_sends(evens),
            (returned[cut:], back_one),
            *out_next,
        ],
    )
    qkv.blocks[0] = by_q(blocks_first, 0)
    qkv.take_x(moved[: ny - 1], others)
    qkv.take_y(moved[ny - 1 : -2], evens)
    out_total = out.total(moved[-1:])
    back = [back_first, moved[-2]]

    grad_gain_two, grad_shift_two, grad_bias_out = sums_two
    normals = [*normal_halo, normal_own]

    def vectors(halo, own_grad, grads, d_ffn, bias_fc_sum, *back):
        sums_one = column_sums(halo, own_grad, normals, grads)
        bias_proj_sum = jnp.sum(wide(d_ffn), axis=0)
        halves = [jnp.where(rep == n, bias_fc_sum, 0.0) for n in range(2)]
        small_parts = [grad_bias_out, grad_gain_two, grad_shift_two]
        small_parts += [jnp.concatenate(halves, axis=1).reshape(-1), bias_proj_sum]
        small_parts += [sums_one[0, :D], sums_one[1, :D], sums_one[2:4, :D].reshape(-1)]
        if again:
            last_halo = halo[reach_rows - row_count :]
            pairs = zip(back, (last_halo[:cut], last_halo[cut:]))
            back = [low(sum_of(pair)) for pair in pairs]
        return (*SmallSum.prepare(small_parts), *back)

    bias_fc_sum = grad_bias_fc.reshape(blocks, 1, width)
    (small_value, *back), moved = stage(
        vectors,
        [d_normed_halo, d_normed_own, grads, d_ffn, bias_fc_sum, *back],
        [*qkv.x_sends([0]), *qkv.odd_y_sends(), *qkv.z_sends()],
    )
    qkv.take_x(moved[:1], [0])
    qkv.take_odd_y(moved[1:ny])
    qkv_next = qkv.z_next(moved[ny:])
    small = SmallSum(small_value, [D, D, D, ff, D, D, D, 2 * D])

    (ffn_own,), moved = stage(
        lambda x: (ffn_back(x, units_proj, width, lane_proj, 0, row_count, jnp.float32),),
        [active],
        [
            *qkv_next,
            *qkv.y_sends([0]),
            (out_total, swap_rep),
            *small.sends(),
            *[(back[0], back_two)] * again,
        ],
    )
    if again:
        back[0] = moved.pop()
    qkv.take_y(moved[1:ny], [0])
    qkv_total = qkv.total(moved[:1])
    out_got = moved[ny]
    small.take(moved[ny + 1 :])

    def input_part(rows, returned):
        grad = d_normed_own[rows] + wide(returned[:, :D])
        back_grad = norm_backward(grad, gain_one, normal_own[rows], inverse_own[rows])
        return low(d_resid[rows] + back_grad)

    def both_halves(half, got):
        return (jnp.where(rep == 0, half, got), jnp.where(rep == 0, got, half))

    def last(total, got, returned, fc_half, fc_got, proj_half, proj_got, resid, own, top, rest):
        halves = both_halves(fc_half, fc_got)
        if per_b > 1:
            rows = fc_half.shape[0]
            halves = [part.reshape(rows, per_b, 1, width) for part in halves]
            halves = [jnp.concatenate(halves, axis=2).reshape(rows, -1)]
        grad_fc = wide(jnp.concatenate(halves, axis=1))
        halves = both_halves(proj_half.T, proj_got.T)
        if per_c > 1:
            halves = [part.reshape(per_c, 1, width, -1) for part in halves]
            halves = [jnp.concatenate(halves, axis=1).reshape(2 * per_c * width, -1)]
        grad_proj = wide(jnp.concatenate(halves, axis=0))
        result = jnp.concatenate([top, rest], axis=0)
        layer_out = low(resid + own + wide(result[:, :D]) + bias_proj)
        part = input_part(slice(0, cut), returned)
        return (wide(total) + wide(got), part, grad_fc, grad_proj, layer_out)

    (grad_out_weight, input_first, grad_fc, grad_proj, layer_out), (qkv_got, *moved) = stage(
        last,
        [
            out_total,
            out_got,
            back[0],
            fc_total,
            fc_got,
            proj_total,
            proj_got,
            resid,
            ffn_own,
            ffn_first,
            ffn_second,
        ],
        [(qkv_total, swap_rep), *[(back[1], back_two)] * again, *small.sends()],
    )
    if again:
        back[1] = moved[0]
    small.take(moved[-1:])
    input_grad = jnp.concatenate([input_first, input_part(slice(cut, None), back[1])], axis=0)
    grad_qkv = wide(qkv_total) + wide(qkv_got)
    small_out = small.finish()

    grad_bias_out, grad_gain_two, grad_shift_two, grad_bias_fc, grad_bias_proj = small_out[:5]
    grad_gain_one, grad_shift_one, grad_bias_qv = small_out[5:]

    return (
        layer_out[None],
        input_grad[None],
        grad_gain_one,
        grad_shift_one,
        grad_qkv,
        grad_bias_qv,
        grad_out_weight,
        grad_bias_out,
        grad_gain_two,
        grad_shift_two,
        grad_fc,
        grad_bias_fc,
        grad_proj,
        grad_bias_proj,
    )


def solution(mesh):
    in_specs = (
        P(("rep", "dat"), "ctx", None),
        P(("rep", "dat"), None),
        P(("rep", "dat"), "ctx", None),
        P("ctx"),
        P("ctx"),
        P("dat", "ctx"),
        P("ctx"),
        P("dat", "ctx"),
        P("ctx"),
        P("ctx"),
        P("ctx"),
        P("dat", "ctx"),
        P("ctx"),
        P("dat", "ctx"),
        P("ctx"),
    )
    out_specs = (
        P(("rep", "dat"), "ctx", None),
        P(("rep", "dat"), "ctx", None),
        P("ctx"),
        P("ctx"),
        P("dat", "ctx"),
        P("ctx"),
        P("dat", "ctx"),
        P("ctx"),
        P("ctx"),
        P("ctx"),
        P("dat", "ctx"),
        P("ctx"),
        P("dat", "ctx"),
        P("ctx"),
    )
    return jax.shard_map(local, mesh=mesh, in_specs=in_specs, out_specs=out_specs, check_vma=False)
```
